128 devices in a mesh: grp: 8 (over x, core), tp: 16 (over z, y).
Axes of the slice: x: 4, y: 4, z: 4, core: 2. Of those that a mesh axis runs over, the one named last changes fastest.
Arguments:
- image: bfloat16 [4096, 2432], P('grp'), may hold values from -6 to 6
- prompt_encoder_rows: bfloat16 [2560, 4096], P(('grp', 'tp')), may hold values from -6 to 6
- prompt_row_request: int32 [2560, 1], P(('grp', 'tp')), may hold values from 0 to 15; in each aligned block of 20 rows (0 to 19, 20 to 39, ...) at most 2 rows name the same one
- request_adapter: int32 [16], P('grp'), may hold values from 0 to 31
- modulation: float32 [16, 2, 6, 2432], P('grp'), may hold values from -3 to 3
- query_key_gain: float32 [2, 2, 64], replicated, may hold values from 0.25 to 1.75
- prompt_embed_weight: bfloat16 [4096, 2432], P('tp'), may hold values from -0.09375 to 0.09375
- image_query_key_value: bfloat16 [2432, 3, 2048], P(None, None, 'tp'), may hold values from -0.125 to 0.125
- prompt_query_key_value: bfloat16 [2432, 3, 2048], P(None, None, 'tp'), may hold values from -0.125 to 0.125
- image_out_weight: bfloat16 [2048, 2432], P('tp'), may hold values from -0.125 to 0.125
- prompt_out_weight: bfloat16 [2048, 2432], P('tp'), may hold values from -0.125 to 0.125
- feed_in_weight: bfloat16 [2, 2432, 9728], P(None, None, 'tp'), may hold values from -0.125 to 0.125
- feed_out_weight: bfloat16 [2, 9728, 2432], P(None, 'tp'), may hold values from -0.0625 to 0.0625
- adapter_down: bfloat16 [32, 2432, 192], P(None, 'tp'), may hold values from -0.125 to 0.125
- adapter_up: bfloat16 [32, 3, 64, 2048], P(None, None, None, 'tp'), may hold values from -0.75 to 0.75
Outputs:
- image_out: bfloat16 [4096, 2432], P(('grp', 'tp'))
- prompt_out: bfloat16 [4096, 2432], P(('grp', 'tp'))
The draws below stay inside these ranges and needn't reach their ends.
Inputs may be any that keep to these rules, and one draw needn't show every extreme that they name: `prompt_row_request`: among the rows of one encoder device (20 aligned rows) no request is named more than 2 times, a bound that some block reaches.
All inputs are finite; a program needn't handle non-finite values.
Results may differ from the reference program's by a relative error of at most 0.024.
Values may be sent and summed in bfloat16 or wider, within the bound.
No kernel may reach another device: no remote copies, remote signals or barrier semaphores. Data moves between devices by JAX's collectives and lax.ppermute only.
A program may use at most 128 MiB of HBM per device.

```python
import math
import jax
import jax.numpy as jnp
import numpy as np
from jax import lax

MODEL_WIDTH = 2432
DT = 4096
FF = 9728
HEAD_DIM = 64
ADAPTER_RANK = 64
ADAPTER_COUNT = 32
REQ_GRP = 2
IMG = 256
CAP = 2
REQ = 16
POOL_DEV = 20
POOL = 2560
SLOTS = 256
KEYS = 512
ATTENTION_WIDTH = 2048
PROMPT_ROWS = 4096
N_GRP = 8
N_TP = 16
DEVICES = 128


def plant(drawn, stream_key, smallest, high):
    dims = drawn.shape
    place = [jax.random.randint(jax.random.fold_in(stream_key, axis), (), 0, dims[axis]) for axis in range(len(dims))]
    drawn = drawn.at[tuple(place)].set(smallest)
    longest = dims.index(max(dims))
    place[longest] = (place[longest] + 1) % dims[longest]
    return drawn.at[tuple(place)].set(high)


def block_scale(own_key, shape, cuts, least, high):
    gain = 1.0
    for axis_at, blocks in cuts:
        heights = jax.random.uniform(jax.random.fold_in(jax.random.fold_in(own_key, 6), axis_at), (blocks,), jnp.float32, least / len(cuts), high / len(cuts))
        gain = gain * jnp.repeat(jnp.exp(heights), shape[axis_at] // blocks).reshape((-1,) + (1,) * (len(shape) - 1 - axis_at))
    return gain


def routed_block(own_key, own, number, rows, amount, top, most, slope):
    ranking = jax.random.permutation(own_key, amount)
    packed, ordinary = shares(amount, rows * top, most, slope, True), shares(amount, rows * top, most, slope, False)
    places = jnp.arange(amount)

    def named(tallies, offset_by):
        used = int((tallies > 0).sum())
        fixed = max(1, used // 4)
        passed = fixed + (places - fixed + offset_by * (used - fixed)) % max(1, amount - fixed)
        return jnp.zeros((amount,), jnp.int32).at[ranking[jnp.where(places < fixed, places, passed)]].set(jnp.asarray(tallies, jnp.int32))

    tallies = jnp.where(number % 4 == 0, named(packed, number // 4), named(ordinary, number - number // 4 - 1))
    mixed = jax.random.permutation(jax.random.fold_in(own, 3), amount)
    giver, sink = mixed[0:amount // 2 * 2:2], mixed[1:amount // 2 * 2:2]
    margin = jnp.minimum(tallies[giver] - 1, most - tallies[sink]) // 2
    margin = jnp.where((giver == ranking[0]) | (sink == ranking[0]) | (tallies[sink] == 0), 0, jnp.maximum(margin, 0))
    passed = jax.random.randint(jax.random.fold_in(own, 4), (amount // 2,), 0, 1 << 20) % (margin + 1)
    tallies = tallies.at[giver].add(-passed).at[sink].add(passed)
    labels = jnp.searchsorted(jnp.cumsum(tallies), jnp.arange(rows * top), side="right").astype(jnp.int32)
    table = labels.reshape(top, rows).T
    table = table[jax.random.permutation(jax.random.fold_in(own, 1), rows)]
    offset_by = jax.random.randint(jax.random.fold_in(own, 2), (rows, 1), 0, top)
    return jnp.take_along_axis(table, (jnp.arange(top)[None, :] + offset_by) % top, axis=1)


def shares(amount, total, bound, skew, full):
    portions = [(1 << 20) // math.isqrt(standing ** skew) + 1 for standing in range(1, amount + 1)]
    largest = bound if full else min(bound, max(-(-total // amount), total * portions[0] // sum(portions)))
    least = 1 if total - largest >= amount - 1 else 0
    counts, spare = [largest] + [least] * (amount - 1), total - largest - least * (amount - 1)
    while spare > 0:
        free = [i for i in range(1, amount) if counts[i] < largest] or [i for i in range(1, amount) if counts[i] < bound]
        whole, left = sum([portions[i] for i in free]), spare
        for i in free:
            addition = min(bound - counts[i], max(1, left * portions[i] // whole), spare)
            counts[i] = counts[i] + addition
            spare = spare - addition
    return np.array(counts)


def noise(rng, shape, scale, reach, pieces=(), dtype=jnp.bfloat16):
    gain = block_scale(rng, shape, pieces, -0.22, 0.18) if pieces else 1.0
    result = jax.random.normal(rng, shape, jnp.float32) * scale * gain
    return jnp.minimum(jnp.maximum(result, -reach), reach).astype(dtype)


def setup_inputs(seed: int = 0) -> dict:
    key_list = jax.random.split(jax.random.key(seed), 16)
    image = noise(key_list[0], (REQ * IMG, MODEL_WIDTH), 1.0, 6.0, ((0, 8),))
    prompt_encoder_rows = noise(key_list[1], (POOL, DT), 1.0, 6.0, ((0, 128),))
    prompt_row_request_keys = jax.random.split(jax.random.fold_in(key_list[2], 1), POOL // POOL_DEV)
    prompt_row_request_turns = jax.random.permutation(jax.random.fold_in(key_list[2], 3), POOL // POOL_DEV)
    prompt_row_request = jax.vmap(lambda own, number: routed_block(jax.random.fold_in(key_list[2], 2), own, number, POOL_DEV, REQ, 1, CAP, 2))(prompt_row_request_keys, prompt_row_request_turns).reshape((POOL, 1))
    request_adapter = plant(jax.random.randint(key_list[3], (REQ,), 0, ADAPTER_COUNT), jax.random.fold_in(key_list[3], 1), 0, ADAPTER_COUNT - 1).astype(jnp.int32)
    modulation = noise(key_list[4], (REQ, 2, 6, MODEL_WIDTH), 0.5, 3.0, ((0, 8),), jnp.float32)
    query_key_gain = jnp.clip(1.0 + 0.15 * jax.random.normal(key_list[5], (2, 2, HEAD_DIM), jnp.float32), 0.25, 1.75)
    prompt_embed_weight = noise(key_list[6], (DT, MODEL_WIDTH), DT ** -0.5, 0.09375, ((0, 16),))
    image_query_key_value = noise(key_list[7], (MODEL_WIDTH, 3, ATTENTION_WIDTH), MODEL_WIDTH ** -0.5, 0.125, ((2, 16),))
    prompt_query_key_value = noise(key_list[8], (MODEL_WIDTH, 3, ATTENTION_WIDTH), MODEL_WIDTH ** -0.5, 0.125, ((2, 16),))
    image_out_weight = noise(key_list[9], (ATTENTION_WIDTH, MODEL_WIDTH), ATTENTION_WIDTH ** -0.5, 0.125, ((0, 16),))
    prompt_out_weight = noise(key_list[10], (ATTENTION_WIDTH, MODEL_WIDTH), ATTENTION_WIDTH ** -0.5, 0.125, ((0, 16),))
    feed_in_weight = noise(key_list[11], (2, MODEL_WIDTH, FF), MODEL_WIDTH ** -0.5, 0.125, ((2, 16),))
    feed_out_weight = noise(key_list[12], (2, FF, MODEL_WIDTH), FF ** -0.5, 0.0625, ((1, 16),))
    adapter_down = noise(key_list[13], (ADAPTER_COUNT, MODEL_WIDTH, 3 * ADAPTER_RANK), MODEL_WIDTH ** -0.5, 0.125, ((1, 16),))
    adapter_up = noise(key_list[14], (ADAPTER_COUNT, 3, ADAPTER_RANK, ATTENTION_WIDTH), ADAPTER_RANK ** -0.5, 0.75, ((3, 16),))
    return {"image": image, "prompt_encoder_rows": prompt_encoder_rows, "prompt_row_request": prompt_row_request, "request_adapter": request_adapter, "modulation": modulation, "query_key_gain": query_key_gain, "prompt_embed_weight": prompt_embed_weight, "image_query_key_value": image_query_key_value, "prompt_query_key_value": prompt_query_key_value, "image_out_weight": image_out_weight, "prompt_out_weight": prompt_out_weight, "feed_in_weight": feed_in_weight, "feed_out_weight": feed_out_weight, "adapter_down": adapter_down, "adapter_up": adapter_up}


EPSILON = 1e-06
ADAPTER_SCALE = 0.5

def layer_norm(values):
    centred = values - lax.optimization_barrier(jnp.mean(values, -1, keepdims=True))
    return centred * lax.rsqrt(lax.optimization_barrier(jnp.mean(centred * centred, -1, keepdims=True)) + EPSILON)

def modulate(values, shift, scale):
    return (layer_norm(values) * (1.0 + scale) + shift).astype(jnp.bfloat16)

def split_heads(projected, gains):
    shaped = projected.reshape(projected.shape[0], projected.shape[1], 3, -1, HEAD_DIM)
    normed = shaped * lax.rsqrt(lax.optimization_barrier(jnp.mean(shaped * shaped, -1, keepdims=True)) + EPSILON)
    queries = (normed[:, :, 0] * gains[0]).astype(jnp.bfloat16)
    keys_out = (normed[:, :, 1] * gains[1]).astype(jnp.bfloat16)
    values = shaped[:, :, 2].astype(jnp.bfloat16)
    return (queries, keys_out, values)

def reference(image, prompt_encoder_rows, prompt_row_request, request_adapter, modulation, query_key_gain, prompt_embed_weight, image_query_key_value, prompt_query_key_value, image_out_weight, prompt_out_weight, feed_in_weight, feed_out_weight, adapter_down, adapter_up):
    request = prompt_row_request[:, 0].reshape(DEVICES, POOL_DEV)
    position = jnp.arange(POOL_DEV)
    earlier = (request[:, :, None] == request[:, None, :]) & (position[None, None, :] < position[None, :, None])
    ranked = lax.optimization_barrier(jnp.sum(earlier.astype(jnp.int32), 2))
    device = jnp.arange(DEVICES)[:, None]
    src_grp = device // N_TP
    src_tp = device % N_TP
    target = (((request // REQ_GRP * N_TP + src_tp) * N_GRP + src_grp) * REQ_GRP + request % REQ_GRP) * CAP + ranked
    target = target.reshape(-1).astype(jnp.int32)
    total_slots = N_GRP * N_TP * N_GRP * REQ_GRP * CAP
    slots = jnp.zeros((total_slots, DT), jnp.bfloat16).at[target].set(prompt_encoder_rows)
    keep = jnp.zeros((total_slots,), jnp.float32).at[target].set(1.0)
    embedded = jnp.dot(slots, prompt_embed_weight, preferred_element_type=jnp.float32).astype(jnp.bfloat16)
    embedded = embedded.reshape(N_GRP, N_TP, N_GRP, REQ_GRP, CAP, MODEL_WIDTH)
    keep = keep.reshape(N_GRP, N_TP, N_GRP, REQ_GRP, CAP)
    images = image.reshape(N_GRP, REQ_GRP, IMG, MODEL_WIDTH)
    mods = modulation.reshape(N_GRP, REQ_GRP, 2, 6, MODEL_WIDTH)
    idents = request_adapter.reshape(N_GRP, REQ_GRP)
    single_float = jnp.float32

    def one_group(parts):
        rows_img, emb, keep_slots, mod, identity_matrix = parts
        image32 = rows_img.astype(single_float)
        img_mod = modulate(image32, mod[:, 0, 0][:, None], mod[:, 0, 1][:, None])
        chosen_down = adapter_down[identity_matrix].astype(single_float)
        chosen_up = adapter_up[identity_matrix].astype(single_float)
        rank_product = jnp.einsum('jnd,jdr->jnr', img_mod.astype(single_float), chosen_down).astype(jnp.bfloat16)
        rank_product = rank_product.reshape(REQ_GRP, IMG, 3, ADAPTER_RANK)
        prompt_rows = emb.transpose(2, 0, 1, 3, 4).reshape(REQ_GRP, SLOTS, MODEL_WIDTH)
        txt_mod = modulate(prompt_rows.astype(single_float), mod[:, 1, 0][:, None], mod[:, 1, 1][:, None])
        image_projected = jnp.einsum('jnd,dch->jnch', img_mod.astype(single_float), image_query_key_value.astype(single_float))
        image_projected = image_projected + ADAPTER_SCALE * jnp.einsum('msky,mkyo->msko', rank_product.astype(single_float), chosen_up)
        projected_txt = jnp.einsum('jnd,dch->jnch', txt_mod.astype(single_float), prompt_query_key_value.astype(single_float))
        query_img, key_img, value_img = split_heads(image_projected, query_key_gain[0])
        query_txt, key_txt, value_txt = split_heads(projected_txt, query_key_gain[1])
        queries = jnp.concatenate([query_img, query_txt], 1).astype(single_float)
        keys_all = jnp.concatenate([key_img, key_txt], 1).astype(single_float)
        values_all = jnp.concatenate([value_img, value_txt], 1).astype(single_float)
        keep_txt = keep_slots.transpose(2, 0, 1, 3).reshape(REQ_GRP, SLOTS)
        keep_all = jnp.concatenate([jnp.ones((REQ_GRP, IMG), single_float), keep_txt], 1)
        scores = jnp.einsum('jqhe,jkhe->jhqk', queries, keys_all) * HEAD_DIM ** (-0.5)
        weights = jnp.exp(scores) * keep_all[:, None, None, :]
        probs = (weights / lax.optimization_barrier(jnp.sum(weights, -1, keepdims=True))).astype(jnp.bfloat16)
        attended = jnp.einsum('jhqk,jkhe->jqhe', probs.astype(single_float), values_all).astype(jnp.bfloat16)
        attended = attended.reshape(REQ_GRP, KEYS, ATTENTION_WIDTH).astype(single_float)
        proj_img = jnp.einsum('jnh,hd->jnd', attended[:, :IMG], image_out_weight.astype(single_float))
        att_txt = attended[:, IMG:].reshape(REQ_GRP, N_TP, N_GRP, CAP, ATTENTION_WIDTH).transpose(1, 2, 0, 3, 4)
        proj_txt = jnp.einsum('bajch,hd->bajcd', att_txt, prompt_out_weight.astype(single_float))
        mixed_img = (image32 + mod[:, 0, 2][:, None] * proj_img).astype(jnp.bfloat16)
        mixed_txt = (emb.astype(single_float) + mod[:, 1, 2][None, None, :, None] * proj_txt).astype(jnp.bfloat16)
        norm_img = modulate(mixed_img.astype(single_float), mod[:, 0, 3][:, None], mod[:, 0, 4][:, None])
        norm_txt = modulate(mixed_txt.astype(single_float), mod[:, 1, 3][None, None, :, None], mod[:, 1, 4][None, None, :, None])
        hidden_img = jax.nn.gelu(jnp.einsum('jnd,df->jnf', norm_img.astype(single_float), feed_in_weight[0].astype(single_float)), approximate=True).astype(jnp.bfloat16)
        hidden_txt = jax.nn.gelu(jnp.einsum('bajcd,df->bajcf', norm_txt.astype(single_float), feed_in_weight[1].astype(single_float)), approximate=True).astype(jnp.bfloat16)
        feed_img = jnp.einsum('jnf,fd->jnd', hidden_img.astype(single_float), feed_out_weight[0].astype(single_float))
        feed_txt = jnp.einsum('bajcf,fd->bajcd', hidden_txt.astype(single_float), feed_out_weight[1].astype(single_float))
        result_img = (mixed_img.astype(single_float) + mod[:, 0, 5][:, None] * feed_img).astype(jnp.bfloat16)
        result_txt = ((mixed_txt.astype(single_float) + mod[:, 1, 5][None, None, :, None] * feed_txt) * keep_slots[..., None]).astype(jnp.bfloat16)
        return (result_img, result_txt)
    result_img, result_txt = lax.map(one_group, (images, embedded, keep, mods, idents))
    return (result_img.reshape(REQ * IMG, MODEL_WIDTH), result_txt.reshape(PROMPT_ROWS, MODEL_WIDTH))
```

```python
import jax
import jax.numpy as jnp
from jax import lax
from jax.sharding import PartitionSpec as P

HEAD_DIM = 64
CAP = 2
EPSILON = 1e-06
ADAPTER_SCALE = 0.5
SIDE = 4
F32 = jnp.float32
BF16 = jnp.bfloat16


def torus_shift(values, stage, step):
    pairs = []
    for grp in range(8):
        for tp in range(16):
            z, y = divmod(tp, SIDE)
            if (grp + stage) % 2 == 0:
                y = (y + step) % SIDE
            else:
                z = (z + step) % SIDE
            pairs.append((grp * 16 + tp, grp * 16 + z * SIDE + y))
    return lax.ppermute(values, ("grp", "tp"), pairs)


def x_shift(values, step):
    pairs = [(grp, ((grp // 2 + step) % SIDE) * 2 + grp % 2) for grp in range(8)]
    return lax.ppermute(values, "grp", pairs)


def core_swap(values):
    return lax.ppermute(values, "grp", [(grp, grp ^ 1) for grp in range(8)])


def gather_stage(rows, stage):
    return jnp.concatenate(
        [
            rows,
            torus_shift(rows, stage, -1),
            torus_shift(rows, stage, 2),
            torus_shift(rows, stage, 1),
        ],
        0,
    )


def gather_rows(rows):
    return gather_stage(gather_stage(rows, 0), 1)


def scatter_stage(rows, stage):
    part = rows.shape[0] // SIDE
    chunk = [rows[step * part : (step + 1) * part] for step in range(SIDE)]
    total = chunk[0].astype(F32)
    total = total + torus_shift(chunk[1], stage, 1).astype(F32)
    total = total + torus_shift(chunk[3], stage, -1).astype(F32)
    total = total + torus_shift(chunk[2], stage, 2).astype(F32)
    return total


def scatter_rows(rows):
    return scatter_stage(scatter_stage(rows, 1).astype(BF16), 0)


def swap_cores(values):
    return jnp.stack([values[0], core_swap(values[1])], 0)


def swap_chips(values):
    return jnp.stack(
        [
            values[0],
            x_shift(values[3], -1),
            x_shift(values[2], 2),
            x_shift(values[1], 1),
        ],
        0,
    )


def layer_norm(values):
    centred = values - jnp.mean(values, -1, keepdims=True)
    return centred * lax.rsqrt(jnp.mean(centred * centred, -1, keepdims=True) + EPSILON)


def modulate(values, shift, scale):
    return (layer_norm(values) * (1.0 + scale) + shift).astype(BF16)


def head_norm(values, gains):
    shaped = values.reshape(values.shape[0], -1, HEAD_DIM)
    normed = shaped * lax.rsqrt(jnp.mean(shaped * shaped, -1, keepdims=True) + EPSILON)
    return (normed * gains).astype(BF16).reshape(values.shape)


def split_parts(projected, gains):
    queries = head_norm(projected[:, :128], gains[0])
    keys = head_norm(projected[:, 128:256], gains[1])
    return queries, keys, projected[:, 256:].astype(BF16)


def feed(rows, weight_in, weight_out):
    hidden = jax.nn.gelu(
        jnp.dot(rows, weight_in, preferred_element_type=F32), approximate=True
    ).astype(BF16)
    return jnp.dot(hidden, weight_out, preferred_element_type=F32).astype(BF16)


def shards(
    image,
    prompt_encoder_rows,
    prompt_row_request,
    request_adapter,
    modulation,
    query_key_gain,
    prompt_embed_weight,
    image_query_key_value,
    prompt_query_key_value,
    image_out_weight,
    prompt_out_weight,
    feed_in_weight,
    feed_out_weight,
    adapter_down,
    adapter_up,
):
    grp = lax.axis_index("grp")
    tp = lax.axis_index("tp")
    chip, core = grp // 2, grp % 2
    z, y = tp // SIDE, tp % SIDE
    width = image.shape[1]
    pool_rows = prompt_encoder_rows.shape[0]
    img_count = image.shape[0] // 2

    steps = jnp.arange(16)
    far, near = steps // SIDE, steps % SIDE
    places = jnp.where(
        core == 0,
        ((z + far) % SIDE) * SIDE + (y + near) % SIDE,
        ((z + near) % SIDE) * SIDE + (y + far) % SIDE,
    )
    all_z, all_y = steps // SIDE, steps % SIDE
    dist_z, dist_y = (all_z - z) % SIDE, (all_y - y) % SIDE
    relative = jnp.where(core == 0, dist_z * SIDE + dist_y, dist_y * SIDE + dist_z)

    request = prompt_row_request[:, 0]
    labels = jnp.zeros((16, 256), BF16).at[:, :pool_rows].set(request.astype(BF16)[None, :])
    outgoing = jnp.concatenate(
        [
            prompt_encoder_rows.reshape(pool_rows, 16, 256).transpose(1, 0, 2),
            labels[:, None, :],
            jnp.zeros((16, 3, 256), BF16),
        ],
        1,
    )
    arrived = lax.all_to_all(outgoing, "tp", 0, 0, tiled=True)
    arrived = jnp.take(arrived, places, axis=0)
    features = arrived[:, :pool_rows].reshape(16 * pool_rows, 256)
    requests = arrived[:, pool_rows, :pool_rows].astype(jnp.int32)

    prompt_mod = modulation[:, 1]
    mod_pair = jnp.stack([prompt_mod, core_swap(prompt_mod)], 0)
    mod_all = jnp.stack(
        [mod_pair, x_shift(mod_pair, -1), x_shift(mod_pair, 2), x_shift(mod_pair, 1)], 0
    ).reshape(16, 6 * width)

    def relative_request(values):
        step = (values // 4 - chip) % SIDE
        other = (values // 2 % 2 + core) % 2
        return (step * 2 + other) * 2 + values % 2

    def slot_hot(values):
        position = jnp.arange(pool_rows)
        earlier = (values[:, :, None] == values[:, None, :]) & (
            position[None, None, :] < position[None, :, None]
        )
        ranked = jnp.sum(earlier.astype(jnp.int32), 2)
        target = relative_request(values) * CAP + ranked
        return (jnp.arange(32)[None, :, None] == target[:, None, :]).astype(BF16)

    hot_all = slot_hot(requests)
    hot_own = slot_hot(request[None])[0]
    row_hot = (jnp.arange(16)[None, :] == relative_request(request)[:, None]).astype(F32)
    row_mod = jnp.dot(
        row_hot, mod_all, precision=lax.Precision.HIGHEST, preferred_element_type=F32
    ).reshape(pool_rows, 6, width)

    embed_part = jnp.dot(features, prompt_embed_weight, preferred_element_type=F32).astype(BF16)
    embedded = scatter_rows(embed_part).astype(BF16)
    embedded32 = embedded.astype(F32)
    txt_mod = gather_rows(modulate(embedded32, row_mod[:, 0], row_mod[:, 1]))
    projected_txt = jnp.dot(
        txt_mod, prompt_query_key_value.reshape(width, -1), preferred_element_type=F32
    )
    query_txt, key_txt, value_txt = split_parts(projected_txt, query_key_gain[1])
    parts_txt = jnp.concatenate([query_txt, key_txt, value_txt], -1).reshape(16, pool_rows, 384)
    slots = jnp.einsum("bsr,brc->sbc", hot_all, parts_txt, preferred_element_type=F32).astype(BF16)
    slots = slots.reshape(SIDE, 2, 64, 384)
    flags = jnp.sum(hot_all.astype(F32), 2).T.astype(BF16).reshape(SIDE, 2, 1, 64)
    flags = jnp.pad(flags, ((0, 0), (0, 0), (0, 15), (0, 320)))
    slots = jnp.concatenate([slots, flags], 2).transpose(1, 0, 2, 3)
    slots = swap_cores(slots).transpose(1, 0, 2, 3)
    slots = swap_chips(slots).reshape(8, 80, 384)
    keep_txt = slots[:, 64, :64].astype(F32).reshape(8, 2, 32).transpose(1, 0, 2).reshape(2, 256)
    txt_parts = slots[:, :64].reshape(8, 2, 32, 384).transpose(1, 0, 2, 3).reshape(2, 256, 384)

    image_rows = image.astype(F32).reshape(2, img_count, width)
    img_mod = modulate(image_rows, modulation[:, 0, 0][:, None], modulation[:, 0, 1][:, None])
    chosen_down = jnp.take(adapter_down, request_adapter, axis=0)
    chosen_up = jnp.take(adapter_up, request_adapter, axis=0)
    down_all = gather_rows(chosen_down[None])
    down_all = jnp.take(down_all, relative, axis=0).transpose(1, 0, 2, 3).reshape(2, width, -1)
    low = jnp.einsum("jnd,jdr->jnr", img_mod, down_all, preferred_element_type=F32).astype(BF16)
    low = low.reshape(2, img_count, 3, -1)
    projected_img = jnp.dot(
        img_mod.reshape(2 * img_count, width),
        image_query_key_value.reshape(width, -1),
        preferred_element_type=F32,
    )
    projected_img = projected_img + ADAPTER_SCALE * jnp.einsum(
        "msky,mkyo->msko", low, chosen_up, preferred_element_type=F32
    ).reshape(2 * img_count, -1)
    query_img, key_img, value_img = split_parts(projected_img, query_key_gain[0])
    img_parts = jnp.concatenate([query_img, key_img, value_img], -1).reshape(2, img_count, 384)

    tokens = jnp.concatenate([img_parts, txt_parts], 1)
    token_count = tokens.shape[1]
    tokens = tokens.reshape(2, token_count, 3, 2, HEAD_DIM)
    keep_all = jnp.concatenate([jnp.ones((2, img_count), F32), keep_txt], 1)
    scores = jnp.einsum(
        "jqhe,jkhe->jhqk", tokens[:, :, 0], tokens[:, :, 1], preferred_element_type=F32
    ) * HEAD_DIM ** (-0.5)
    weights = jnp.exp(scores) * keep_all[:, None, None, :]
    probs = (weights / jnp.sum(weights, -1, keepdims=True)).astype(BF16)
    attended = jnp.einsum(
        "jhqk,jkhe->jqhe", probs, tokens[:, :, 2], preferred_element_type=F32
    ).astype(BF16)
    attended = attended.reshape(2, token_count, 128)

    att_img = jnp.take(attended[:, :img_count].reshape(16, 32, 128), places, axis=0)
    term_img = jnp.dot(
        att_img.reshape(512, 128), image_out_weight, preferred_element_type=F32
    ).astype(BF16)
    proj_img = scatter_rows(term_img)
    own_mod = lax.dynamic_index_in_dim(modulation[:, 0], tp // 8, 0, keepdims=False)
    own_image = lax.dynamic_slice_in_dim(image, tp * 32, 32, 0).astype(F32)

    att_txt = attended[:, img_count:].reshape(2, 8, 32, 128).transpose(1, 0, 2, 3)
    att_txt = swap_chips(att_txt.reshape(SIDE, 2, 64, 128)).transpose(1, 0, 2, 3)
    att_txt = swap_cores(att_txt).transpose(1, 0, 2, 3).reshape(32, 16, 128)
    att_txt = jnp.einsum("bsr,sbc->brc", hot_all, att_txt, preferred_element_type=F32).astype(BF16)
    term_txt = jnp.dot(
        att_txt.reshape(16 * pool_rows, 128), prompt_out_weight, preferred_element_type=F32
    ).astype(BF16)
    proj_txt = scatter_rows(term_txt)

    mixed_img = (own_image + own_mod[2] * proj_img).astype(BF16).astype(F32)
    norm_img = gather_rows(modulate(mixed_img, own_mod[3], own_mod[4]))
    mixed_txt = (embedded32 + row_mod[:, 2] * proj_txt).astype(BF16).astype(F32)
    norm_txt = gather_rows(modulate(mixed_txt, row_mod[:, 3], row_mod[:, 4]))

    feed_img = scatter_rows(feed(norm_img, feed_in_weight[0], feed_out_weight[0]))
    feed_txt = scatter_rows(feed(norm_txt, feed_in_weight[1], feed_out_weight[1]))
    image_out = (mixed_img + own_mod[5] * feed_img).astype(BF16)
    rows_out = (mixed_txt + row_mod[:, 5] * feed_txt).astype(BF16)

    placed = jnp.dot(hot_own, rows_out, preferred_element_type=F32).astype(BF16)
    placed = placed.reshape(SIDE, 2, 4, width).transpose(1, 0, 2, 3)
    placed = swap_cores(placed).transpose(1, 0, 2, 3)
    placed = swap_chips(placed).reshape(8, 4, width)
    source = jnp.arange(8)
    order = ((source // 2 - chip) % SIDE) * 2 + (source % 2 + core) % 2
    prompt_out = jnp.take(placed, order, axis=0).reshape(32, width)
    return (image_out, prompt_out)


def solution(mesh):
    placed = (
        P("grp", None),
        P(("grp", "tp"), None),
        P(("grp", "tp"), None),
        P("grp"),
        P("grp", None, None, None),
        P(),
        P("tp", None),
        P(None, None, "tp"),
        P(None, None, "tp"),
        P("tp", None),
        P("tp", None),
        P(None, None, "tp"),
        P(None, "tp", None),
        P(None, "tp", None),
        P(None, None, None, "tp"),
    )
    return jax.shard_map(
        shards,
        mesh=mesh,
        in_specs=placed,
        out_specs=(P(("grp", "tp"), None), P(("grp", "tp"), None)),
        check_vma=False,
    )
```

```python
import functools

import jax
import jax.numpy as jnp
from jax import lax
from jax.experimental import pallas as pl
from jax.experimental.pallas import tpu as pltpu
from jax.sharding import PartitionSpec as P

HEAD_DIM = 64
CAP = 2
EPSILON = 1e-06
ADAPTER_SCALE = 0.5
SIDE = 4
POOL = 20
F32 = jnp.float32
BF16 = jnp.bfloat16


def torus_shift(values, stage, step):
    pairs = []
    for grp in range(8):
        for tp in range(16):
            z, y = divmod(tp, SIDE)
            if (grp + stage) % 2 == 0:
                y = (y + step) % SIDE
            else:
                z = (z + step) % SIDE
            pairs.append((grp * 16 + tp, grp * 16 + z * SIDE + y))
    return lax.ppermute(values, ("grp", "tp"), pairs)


def x_shift(values, step):
    pairs = [(grp, ((grp // 2 + step) % SIDE) * 2 + grp % 2) for grp in range(8)]
    return lax.ppermute(values, "grp", pairs)


def core_swap(values):
    return lax.ppermute(values, "grp", [(grp, grp ^ 1) for grp in range(8)])


def spread(rows, stage):
    return [
        rows,
        torus_shift(rows, stage, -1),
        torus_shift(rows, stage, 2),
        torus_shift(rows, stage, 1),
    ]


def exchange(parts, stage):
    return [
        parts[0],
        torus_shift(parts[3], stage, -1),
        torus_shift(parts[2], stage, 2),
        torus_shift(parts[1], stage, 1),
    ]


def exchange_chips(parts):
    return [parts[0], x_shift(parts[3], -1), x_shift(parts[2], 2), x_shift(parts[1], 1)]


def run(kernel, outs, args, smem=0, scratch=(), flops=0, limit=32):
    specs = [pl.BlockSpec(memory_space=pltpu.SMEM)] * smem
    specs += [pl.BlockSpec(memory_space=pltpu.VMEM)] * (len(args) - smem)
    single = not isinstance(outs, list)
    shapes = [outs] if single else outs
    moved = sum(a.size * a.dtype.itemsize for a in args)
    moved += sum(s.size * s.dtype.itemsize for s in shapes)
    result = pl.pallas_call(
        kernel,
        out_shape=shapes,
        in_specs=specs,
        out_specs=[pl.BlockSpec(memory_space=pltpu.VMEM)] * len(shapes),
        scratch_shapes=list(scratch),
        compiler_params=pltpu.CompilerParams(vmem_limit_bytes=limit << 20),
        cost_estimate=pl.CostEstimate(flops=flops, bytes_accessed=moved, transcendentals=0),
    )(*args)
    return result[0] if single else result


def like(shape, dtype=BF16):
    return jax.ShapeDtypeStruct(shape, dtype)


def normed(values):
    centred = values - jnp.mean(values, -1, keepdims=True)
    return centred * lax.rsqrt(jnp.mean(centred * centred, -1, keepdims=True) + EPSILON)


def low_half(shape):
    return lax.broadcasted_iota(jnp.int32, shape, len(shape) - 1) < HEAD_DIM


def head_norm(values, gains):
    first = low_half(values.shape)
    squares = values * values
    head0 = jnp.sum(jnp.where(first, squares, 0.0), -1, keepdims=True)
    head1 = jnp.sum(jnp.where(first, 0.0, squares), -1, keepdims=True)
    scale = jnp.where(
        first,
        lax.rsqrt(head0 * (1.0 / HEAD_DIM) + EPSILON),
        lax.rsqrt(head1 * (1.0 / HEAD_DIM) + EPSILON),
    )
    return values * scale * gains


def pack_kernel(rows_ref, column_ref, line_ref, out_ref, held):
    column, line = column_ref[...], line_ref[...]
    first = lax.broadcasted_iota(jnp.int32, (POOL, 256), 0)
    second = lax.broadcasted_iota(jnp.int32, (POOL, 256), 1)
    rank = jnp.sum(jnp.where((column == line) & (first < second), 1, 0), 0, keepdims=True)
    held[...] = jnp.zeros_like(held)
    held[POOL : POOL + 1, :] = (line * CAP + rank).astype(F32)
    for block in range(16):
        held[0:POOL, :] = rows_ref[:, block * 256 : (block + 1) * 256].astype(F32)
        out_ref[block] = held[...].astype(BF16)


def embed_kernel(places_ref, arrived_ref, weight_ref, out0, out1, out2, out3, label_ref, held):
    for far, out in enumerate((out0, out1, out2, out3)):
        for near in range(SIDE):
            place = far * SIDE + near
            block = arrived_ref[places_ref[place]].astype(F32)
            held[near * POOL : (near + 1) * POOL, :] = block[0:POOL]
            label_ref[place : place + 1, :] = block[POOL : POOL + 1]
        out[...] = jnp.dot(
            held[...].astype(BF16), weight_ref[...], preferred_element_type=F32
        ).astype(BF16)


def middle_kernel(in0, in1, in2, in3, out0, out1, out2, out3, held):
    held[...] = (in0[...].astype(F32) + in1[...].astype(F32)) + (
        in2[...].astype(F32) + in3[...].astype(F32)
    )
    part = out0.shape[0]
    for place, out in enumerate((out0, out1, out2, out3)):
        out[...] = held[place * part : (place + 1) * part, :].astype(BF16)


def join_kernel(in0, in1, in2, in3, out, held):
    part = in0.shape[0]
    for place, piece in enumerate((in0, in1, in2, in3)):
        held[place * part : (place + 1) * part, :] = piece[...].astype(F32)
    out[...] = held[...].astype(BF16)


def row_mod_kernel(index_ref, mod_ref, out_ref):
    for row in range(POOL):
        values = mod_ref[index_ref[row]]
        for place in range(6):
            out_ref[place, row : row + 1, :] = values[place : place + 1]


def total_of(parts):
    in0, in1, in2, in3 = parts
    return (in0[...].astype(F32) + in1[...].astype(F32)) + (
        in2[...].astype(F32) + in3[...].astype(F32)
    )


def embed_norm_kernel(in0, in1, in2, in3, mod_ref, embedded_ref, out_ref):
    embedded = total_of((in0, in1, in2, in3)).astype(BF16)
    embedded_ref[...] = embedded
    out_ref[...] = (normed(embedded.astype(F32)) * (1.0 + mod_ref[1]) + mod_ref[0]).astype(BF16)


def residual_norm_kernel(base_ref, in0, in1, in2, in3, mod_ref, mixed_ref, out_ref):
    projected = total_of((in0, in1, in2, in3))
    if len(mod_ref.shape) == 3:
        gate, shift, scale = mod_ref[2], mod_ref[3], mod_ref[4]
    else:
        gate, shift, scale = mod_ref[2:3, :], mod_ref[3:4, :], mod_ref[4:5, :]
    mixed = (base_ref[...].astype(F32) + gate * projected).astype(BF16)
    mixed_ref[...] = mixed
    out_ref[...] = (normed(mixed.astype(F32)) * (1.0 + scale) + shift).astype(BF16)


def one_hot(slot_ref, count):
    line = slot_ref[...]
    shape = (count, line.shape[1])
    return jnp.where(lax.broadcasted_iota(jnp.int32, shape, 0) == line, 1.0, 0.0)


def with_keep(values, keep):
    first = low_half(values.shape)
    return jnp.where(first, values, keep), jnp.where(first, keep, values)


def txt_qkv_kernel(
    in0, in1, in2, in3, weight_ref, gain_ref, slot_ref, out0, out1, out2, out3, held
):
    part = in0.shape[0]
    for place, piece in enumerate((in0, in1, in2, in3)):
        projected = jnp.dot(piece[...], weight_ref[...], preferred_element_type=F32)
        rows = slice(place * part, (place + 1) * part)
        held[rows, 0:128] = (head_norm(projected[:, 0:128], gain_ref[0:1, :])).astype(BF16)
        held[rows, 128:256] = (head_norm(projected[:, 128:256], gain_ref[1:2, :])).astype(BF16)
        held[rows, 256:384] = projected[:, 256:384].astype(BF16)
    hot = one_hot(slot_ref, 512)
    keep = jnp.sum(hot, -1, keepdims=True)
    slots = jnp.dot(hot.astype(BF16), held[...], preferred_element_type=F32)
    val0, val1 = with_keep(slots[:, 256:384], keep)
    for step, out in enumerate((out0, out1, out2, out3)):
        for other in range(2):
            rows = slice((other * SIDE + step) * 64, (other * SIDE + step + 1) * 64)
            out[other, :, 0:256] = slots[rows, 0:256].astype(BF16)
            out[other, :, 256:384] = val0[rows].astype(BF16)
            out[other, :, 384:512] = val1[rows].astype(BF16)


def img_project_kernel(image_ref, mod_ref, weight_ref, out_ref, projected_ref):
    rows = image_ref[...].astype(F32)
    modded = (normed(rows) * (1.0 + mod_ref[0, 0, 1:2, :]) + mod_ref[0, 0, 0:1, :]).astype(BF16)
    out_ref[...] = modded
    projected_ref[...] = jnp.dot(modded, weight_ref[...], preferred_element_type=F32)


def img_adapt_kernel(
    places_ref, mod_ref, projected_ref, in0, in1, in2, in3, up_ref, gain_ref, out_ref, down, lift
):
    own = pl.program_id(0)
    depth = in0.shape[2]
    for far, piece in enumerate((in0, in1, in2, in3)):
        for near in range(SIDE):
            start = pl.multiple_of(places_ref[far * SIDE + near] * depth, 8)
            down[pl.ds(start, depth), :] = piece[near, own].astype(F32)
    lift[...] = jnp.zeros_like(lift)
    for part in range(3):
        lift[part * 64 : (part + 1) * 64, part * 128 : (part + 1) * 128] = up_ref[0, part]
    low = jnp.dot(mod_ref[...], down[...].astype(BF16), preferred_element_type=F32).astype(BF16)
    projected = projected_ref[...] + ADAPTER_SCALE * jnp.dot(
        low, lift[...], preferred_element_type=F32
    )
    out_ref[:, 0:128] = head_norm(projected[:, 0:128], gain_ref[0:1, :]).astype(BF16)
    out_ref[:, 128:256] = head_norm(projected[:, 128:256], gain_ref[1:2, :]).astype(BF16)
    val0, val1 = with_keep(projected[:, 256:384], 1.0)
    out_ref[:, 256:384] = val0.astype(BF16)
    out_ref[:, 384:512] = val1.astype(BF16)


def attend(queries, tokens):
    scaled = queries.astype(F32) * HEAD_DIM ** (-0.5)
    first = low_half(scaled.shape)
    keys = tokens[:, 128:256]
    results = []
    for head in range(2):
        own = jnp.where(first if head == 0 else ~first, scaled, 0.0).astype(BF16)
        scores = lax.dot_general(
            own, keys, (((1,), (1,)), ((), ())), preferred_element_type=F32
        )
        weights = jnp.exp(scores).astype(BF16)
        summed = jnp.dot(
            weights, tokens[:, 256 + head * 128 : 384 + head * 128], preferred_element_type=F32
        )
        results.append(summed / pltpu.roll(summed, HEAD_DIM, 1))
    return jnp.where(first, results[0], results[1]).astype(BF16)


def fill_tokens(tokens, img_ref, pieces, swapped):
    for own in range(2):
        tokens[own, 0:256, :] = img_ref[own * 256 : (own + 1) * 256, :]
        for step in range(SIDE):
            start = 256 + step * 64
            rows = slice(own * 32, (own + 1) * 32)
            tokens[own, start : start + 32, :] = pieces[step][0, rows, :]
            tokens[own, start + 32 : start + 64, :] = swapped[step, rows, :]


def img_attend_kernel(
    places_ref, img_ref, in0, in1, in2, in3, swapped, weight_ref,
    out0, out1, out2, out3, token_ref, tokens, held, ranked,
):
    fill_tokens(tokens, img_ref, (in0, in1, in2, in3), swapped)
    token_ref[...] = tokens[...]
    for own in range(2):
        held[own * 256 : (own + 1) * 256, :] = attend(tokens[own, 0:256, 0:128], tokens[own])
    for far, out in enumerate((out0, out1, out2, out3)):
        for near in range(SIDE):
            start = pl.multiple_of(places_ref[far * SIDE + near] * 32, 32)
            ranked[near * 32 : (near + 1) * 32, :] = held[pl.ds(start, 32), :]
        out[...] = jnp.dot(ranked[...], weight_ref[...], preferred_element_type=F32).astype(BF16)


def txt_attend_kernel(token_ref, out0, out1, out2, out3):
    for own in range(2):
        attended = attend(token_ref[own, 256:512, 0:128], token_ref[own])
        for step, out in enumerate((out0, out1, out2, out3)):
            for other in range(2):
                start = step * 64 + other * 32
                out[other, own * 32 : (own + 1) * 32, :] = attended[start : start + 32]


def txt_project_kernel(
    in0, in1, in2, in3, swapped, slot_ref, weight_ref, out0, out1, out2, out3, held
):
    for step, piece in enumerate((in0, in1, in2, in3)):
        held[step * 64 : (step + 1) * 64, :] = piece[0]
        held[(SIDE + step) * 64 : (SIDE + step + 1) * 64, :] = swapped[step]
    hot = one_hot(slot_ref, 512).astype(BF16)
    rows = lax.dot_general(
        hot, held[...], (((0,), (0,)), ((), ())), preferred_element_type=F32
    ).astype(BF16)
    part = out0.shape[0]
    for place, out in enumerate((out0, out1, out2, out3)):
        out[...] = jnp.dot(
            rows[place * part : (place + 1) * part], weight_ref[...], preferred_element_type=F32
        ).astype(BF16)


def feed_kernel(in0, in1, in2, in3, win_ref, wout_ref, out0, out1, out2, out3):
    for piece, out in zip((in0, in1, in2, in3), (out0, out1, out2, out3), strict=True):
        hidden = jnp.dot(piece[...], win_ref[0], preferred_element_type=F32)
        hidden = jax.nn.gelu(hidden, approximate=True).astype(BF16)
        out[...] = jnp.dot(hidden, wout_ref[0], preferred_element_type=F32).astype(BF16)


def txt_final_kernel(mixed_ref, in0, in1, in2, in3, mod_ref, slot_ref, out0, out1, out2, out3):
    rows = mixed_ref[...].astype(F32) + mod_ref[5] * total_of((in0, in1, in2, in3))
    hot = one_hot(slot_ref, 32).astype(BF16)
    placed = jnp.dot(hot, rows.astype(BF16), preferred_element_type=F32)
    for step, out in enumerate((out0, out1, out2, out3)):
        out[...] = placed[step * 8 : (step + 1) * 8].astype(BF16)


def middle(parts):
    rows, width = parts[0].shape
    return run(
        middle_kernel,
        [like((rows // SIDE, width))] * SIDE,
        parts,
        scratch=[pltpu.VMEM((rows, width), F32)],
    )


def join(parts):
    rows, width = parts[0].shape
    return run(
        join_kernel,
        like((rows * SIDE, width)),
        parts,
        scratch=[pltpu.VMEM((rows * SIDE, width), F32)],
    )


def gather_rows(rows):
    return spread(join(spread(rows, 0)), 1)


def scatter_rows(parts):
    return exchange(middle(exchange(parts, 1)), 0)


def feed(parts, weight_in, weight_out, stream):
    rows, width = parts[0].shape
    hidden = weight_in.shape[2]
    plain = pl.BlockSpec((rows, width), lambda i: (0, 0))
    return pl.pallas_call(
        feed_kernel,
        grid=(1,),
        out_shape=[like((rows, width))] * SIDE,
        in_specs=[plain] * SIDE
        + [
            pl.BlockSpec((1, width, hidden), lambda i: (stream, 0, 0)),
            pl.BlockSpec((1, hidden, width), lambda i: (stream, 0, 0)),
        ],
        out_specs=[plain] * SIDE,
        compiler_params=pltpu.CompilerParams(vmem_limit_bytes=40 << 20),
        cost_estimate=pl.CostEstimate(
            flops=rows * SIDE * width * hidden * 4,
            bytes_accessed=width * hidden * 4 + rows * width * 16,
            transcendentals=rows * SIDE * hidden,
        ),
    )(*parts, weight_in, weight_out)


def shards(
    image,
    prompt_encoder_rows,
    prompt_row_request,
    request_adapter,
    modulation,
    query_key_gain,
    prompt_embed_weight,
    image_query_key_value,
    prompt_query_key_value,
    image_out_weight,
    prompt_out_weight,
    feed_in_weight,
    feed_out_weight,
    adapter_down,
    adapter_up,
):
    grp = lax.axis_index("grp")
    tp = lax.axis_index("tp")
    chip, core = grp // 2, grp % 2
    z, y = tp // SIDE, tp % SIDE
    width = image.shape[1]

    steps = jnp.arange(16)
    far, near = steps // SIDE, steps % SIDE
    places = jnp.where(
        core == 0,
        ((z + far) % SIDE) * SIDE + (y + near) % SIDE,
        ((z + near) % SIDE) * SIDE + (y + far) % SIDE,
    ).astype(jnp.int32)
    gains = jnp.concatenate([query_key_gain, query_key_gain], -1)

    request = prompt_row_request[:, 0]
    line = jnp.pad(request[None, :], ((0, 0), (0, 256 - POOL)), constant_values=-1)
    outgoing = run(
        pack_kernel,
        like((16, 32, 256)),
        (prompt_encoder_rows, prompt_row_request, line),
        scratch=[pltpu.VMEM((32, 256), F32)],
    )
    arrived = lax.all_to_all(outgoing, "tp", 0, 0, tiled=True)
    *embed_parts, labels = run(
        embed_kernel,
        [like((SIDE * POOL, width))] * SIDE + [like((16, 256), F32)],
        (places, arrived, prompt_embed_weight),
        smem=1,
        scratch=[pltpu.VMEM((SIDE * POOL, 256), F32)],
        flops=320 * 256 * width * 2,
    )

    prompt_mod = modulation[:, 1]
    mod_pair = jnp.stack([prompt_mod, core_swap(prompt_mod)], 0)
    mod_all = jnp.stack(
        [mod_pair, x_shift(mod_pair, -1), x_shift(mod_pair, 2), x_shift(mod_pair, 1)], 0
    ).reshape(16, 6, width)
    step_own = (request // 4 - chip) % SIDE
    other_own = (request // 2 % 2 + core) % 2
    row_mod = run(
        row_mod_kernel,
        like((6, POOL, width), F32),
        ((step_own * 2 + other_own) * 2 + request % 2, mod_all),
        smem=1,
    )

    target = labels[:, :POOL].astype(jnp.int32)
    slot_step = (target // 8 - chip) % SIDE
    slot_other = (target // 4 % 2 + core) % 2
    slots_all = (slot_other * SIDE + slot_step) * 64 + target // 2 % 2 * 32 + target % 2
    slots_all = (slots_all + 2 * steps[:, None]).reshape(1, 16 * POOL).astype(jnp.int32)
    earlier = (request[:, None] == request[None, :]) & (
        jnp.arange(POOL)[None, :] < jnp.arange(POOL)[:, None]
    )
    ranked = jnp.sum(earlier.astype(jnp.int32), 1)
    slots_own = ((step_own * 2 + other_own) * 2 + request % 2) * CAP + ranked
    slots_own = slots_own.reshape(1, POOL).astype(jnp.int32)

    embed_sums = scatter_rows(embed_parts)
    embedded, txt_mod = run(
        embed_norm_kernel, [like((POOL, width))] * 2, (*embed_sums, row_mod)
    )
    txt_mods = gather_rows(txt_mod)
    slot_parts = run(
        txt_qkv_kernel,
        [like((2, 64, 512))] * SIDE,
        (*txt_mods, prompt_query_key_value.reshape(width, -1), gains[1], slots_all),
        scratch=[pltpu.VMEM((16 * POOL, 384), BF16)],
        flops=320 * width * 384 * 2,
    )
    slot_parts = exchange_chips(slot_parts)
    slots_swapped = core_swap(jnp.stack([part[1] for part in slot_parts], 0))

    blocks = 4
    block = image.shape[0] // blocks
    img_mod, img_projected = pl.pallas_call(
        img_project_kernel,
        grid=(blocks,),
        out_shape=[like(image.shape), like((image.shape[0], 384), F32)],
        in_specs=[
            pl.BlockSpec((block, width), lambda i: (i, 0)),
            pl.BlockSpec((1, 1, 6, width), lambda i: (i // 2, 0, 0, 0)),
            pl.BlockSpec((width, 384), lambda i: (0, 0)),
        ],
        out_specs=[
            pl.BlockSpec((block, width), lambda i: (i, 0)),
            pl.BlockSpec((block, 384), lambda i: (i, 0)),
        ],
        compiler_params=pltpu.CompilerParams(vmem_limit_bytes=32 << 20),
        cost_estimate=pl.CostEstimate(
            flops=512 * width * 384 * 2, bytes_accessed=7 << 20, transcendentals=0
        ),
    )(image, modulation, image_query_key_value.reshape(width, -1))
    chosen_down = jnp.take(adapter_down, request_adapter, axis=0)
    chosen_up = jnp.take(adapter_up, request_adapter, axis=0)
    down_near = jnp.stack(spread(chosen_down, 0), 0)
    down_parts = spread(down_near, 1)
    half = image.shape[0] // 2
    img_parts = pl.pallas_call(
        img_adapt_kernel,
        grid=(2,),
        out_shape=like((image.shape[0], 512)),
        in_specs=[
            pl.BlockSpec(memory_space=pltpu.SMEM),
            pl.BlockSpec((half, width), lambda i: (i, 0)),
            pl.BlockSpec((half, 384), lambda i: (i, 0)),
        ]
        + [pl.BlockSpec(down_near.shape, lambda i: (0, 0, 0, 0))] * SIDE
        + [
            pl.BlockSpec((1, 3, 64, 128), lambda i: (i, 0, 0, 0)),
            pl.BlockSpec((2, 128), lambda i: (0, 0)),
        ],
        out_specs=pl.BlockSpec((half, 512), lambda i: (i, 0)),
        scratch_shapes=[pltpu.VMEM((width, 192), F32), pltpu.VMEM((192, 384), BF16)],
        compiler_params=pltpu.CompilerParams(vmem_limit_bytes=32 << 20),
        cost_estimate=pl.CostEstimate(
            flops=512 * width * 192 * 2, bytes_accessed=6 << 20, transcendentals=0
        ),
    )(places, img_mod, img_projected, *down_parts, chosen_up, gains[0])

    *img_terms, tokens = run(
        img_attend_kernel,
        [like((128, width))] * SIDE + [like((2, 512, 512))],
        (places, img_parts, *slot_parts, slots_swapped, image_out_weight),
        smem=1,
        scratch=[
            pltpu.VMEM((2, 512, 512), BF16),
            pltpu.VMEM((512, 128), BF16),
            pltpu.VMEM((128, 128), BF16),
        ],
        flops=1 << 30,
    )
    img_sums = scatter_rows(img_terms)
    att_parts = run(txt_attend_kernel, [like((2, 64, 128))] * SIDE, (tokens,), flops=1 << 29)
    att_parts = exchange_chips(att_parts)
    att_swapped = core_swap(jnp.stack([part[1] for part in att_parts], 0))
    txt_terms = run(
        txt_project_kernel,
        [like((SIDE * POOL, width))] * SIDE,
        (*att_parts, att_swapped, slots_all, prompt_out_weight),
        scratch=[pltpu.VMEM((512, 128), BF16)],
        flops=320 * 128 * width * 2,
    )
    txt_sums = scatter_rows(txt_terms)

    own_mod = lax.dynamic_index_in_dim(modulation[:, 0], tp // 8, 0, keepdims=False)
    own_image = lax.dynamic_slice_in_dim(image, tp * 32, 32, 0)
    mixed_img, norm_img = run(
        residual_norm_kernel, [like((32, width))] * 2, (own_image, *img_sums, own_mod)
    )
    img_rows = gather_rows(norm_img)
    mixed_txt, norm_txt = run(
        residual_norm_kernel, [like((POOL, width))] * 2, (embedded, *txt_sums, row_mod)
    )
    txt_rows = gather_rows(norm_txt)
    feed_img = scatter_rows(feed(img_rows, feed_in_weight, feed_out_weight, 0))
    feed_txt = scatter_rows(feed(txt_rows, feed_in_weight, feed_out_weight, 1))

    placed = run(
        txt_final_kernel,
        [like((8, width))] * SIDE,
        (mixed_txt, *feed_txt, row_mod, slots_own),
    )
    placed = exchange_chips(placed)
    placed_other = core_swap(jnp.stack([part[4:] for part in placed], 0))
    both = jnp.stack([jnp.stack([part[:4] for part in placed], 0), placed_other], 1)
    source = jnp.arange(8)
    order = ((source // 2 - chip) % SIDE) * 2 + (source % 2 + core) % 2
    prompt_out = jnp.take(both.reshape(8, 4, width), order, axis=0).reshape(32, width)

    feed_sum = functools.reduce(jnp.add, [part.astype(F32) for part in feed_img])
    image_out = (mixed_img.astype(F32) + own_mod[5] * feed_sum).astype(BF16)
    return (image_out, prompt_out)


def solution(mesh):
    placed = (
        P("grp", None),
        P(("grp", "tp"), None),
        P(("grp", "tp"), None),
        P("grp"),
        P("grp", None, None, None),
        P(),
        P("tp", None),
        P(None, None, "tp"),
        P(None, None, "tp"),
        P("tp", None),
        P("tp", None),
        P(None, None, "tp"),
        P(None, "tp", None),
        P(None, "tp", None),
        P(None, None, None, "tp"),
    )
    return jax.shard_map(
        shards,
        mesh=mesh,
        in_specs=placed,
        out_specs=(P(("grp", "tp"), None), P(("grp", "tp"), None)),
        check_vma=False,
    )
```

```python
import functools

import jax
import jax.numpy as jnp
from jax import lax
from jax.experimental import pallas as pl
from jax.experimental.pallas import tpu as pltpu
from jax.sharding import PartitionSpec as P

HEAD_DIM = 64
CAP = 2
EPSILON = 1e-06
ADAPTER_SCALE = 0.5
SIDE = 4
POOL = 20
F32 = jnp.float32
BF16 = jnp.bfloat16


def torus_shift(values, stage, step):
    pairs = []
    for grp in range(8):
        for tp in range(16):
            z, y = divmod(tp, SIDE)
            if (grp + stage) % 2 == 0:
                y = (y + step) % SIDE
            else:
                z = (z + step) % SIDE
            pairs.append((grp * 16 + tp, grp * 16 + z * SIDE + y))
    return lax.ppermute(values, ("grp", "tp"), pairs)


def x_shift(values, step):
    pairs = [(grp, ((grp // 2 + step) % SIDE) * 2 + grp % 2) for grp in range(8)]
    return lax.ppermute(values, "grp", pairs)


def core_swap(values):
    return lax.ppermute(values, "grp", [(grp, grp ^ 1) for grp in range(8)])


def spread(rows, stage):
    return [
        rows,
        torus_shift(rows, stage, -1),
        torus_shift(rows, stage, 2),
        torus_shift(rows, stage, 1),
    ]


def exchange(parts, stage):
    return [
        parts[0],
        torus_shift(parts[3], stage, -1),
        torus_shift(parts[2], stage, 2),
        torus_shift(parts[1], stage, 1),
    ]


def run(kernel, outs, args, smem=0, scratch=(), flops=0, limit=32, after=()):
    specs = [pl.BlockSpec(memory_space=pltpu.SMEM)] * smem
    specs += [pl.BlockSpec(memory_space=pltpu.VMEM)] * (len(args) - smem)
    specs += [pl.BlockSpec(memory_space=pl.ANY)] * len(after)
    count = len(args)
    single = not isinstance(outs, list)
    shapes = [outs] if single else outs
    moved = sum(a.size * a.dtype.itemsize for a in args)
    moved += sum(s.size * s.dtype.itemsize for s in shapes)

    def body(*refs):
        kernel(*refs[:count], *refs[count + len(after) :])

    result = pl.pallas_call(
        body,
        out_shape=shapes,
        in_specs=specs,
        out_specs=[pl.BlockSpec(memory_space=pltpu.VMEM)] * len(shapes),
        scratch_shapes=list(scratch),
        compiler_params=pltpu.CompilerParams(vmem_limit_bytes=limit << 20),
        cost_estimate=pl.CostEstimate(flops=flops, bytes_accessed=moved, transcendentals=0),
    )(*args, *after)
    return result[0] if single else result


def like(shape, dtype=BF16):
    return jax.ShapeDtypeStruct(shape, dtype)


def normed(values):
    centred = values - jnp.mean(values, -1, keepdims=True)
    return centred * lax.rsqrt(jnp.mean(centred * centred, -1, keepdims=True) + EPSILON)


def low_half(shape):
    return lax.broadcasted_iota(jnp.int32, shape, len(shape) - 1) < HEAD_DIM


def head_norm(values, gains):
    first = low_half(values.shape)
    squares = values * values
    head0 = jnp.sum(jnp.where(first, squares, 0.0), -1, keepdims=True)
    head1 = jnp.sum(jnp.where(first, 0.0, squares), -1, keepdims=True)
    scale = jnp.where(
        first,
        lax.rsqrt(head0 * (1.0 / HEAD_DIM) + EPSILON),
        lax.rsqrt(head1 * (1.0 / HEAD_DIM) + EPSILON),
    )
    return values * scale * gains


def pack_kernel(rows_ref, line_ref, out_ref, held, wide):
    wide[...] = jnp.full(wide.shape, -1, jnp.int32)
    wide[0:1, 0:POOL] = line_ref[...]
    line = wide[0:1, :]
    first = lax.broadcasted_iota(jnp.int32, (POOL, 256), 0)
    second = lax.broadcasted_iota(jnp.int32, (POOL, 256), 1)
    column = jnp.sum(jnp.where(first == second, line, 0), 1, keepdims=True)
    rank = jnp.sum(jnp.where((column == line) & (first < second), 1, 0), 0, keepdims=True)
    held[...] = jnp.zeros_like(held)
    held[POOL : POOL + 1, :] = (line * CAP + rank).astype(F32)
    for block in range(16):
        held[0:POOL, :] = rows_ref[:, block * 256 : (block + 1) * 256].astype(F32)
        out_ref[block] = held[...].astype(BF16)


def embed_kernel(places_ref, arrived_ref, weight_ref, out0, out1, out2, out3, label_ref, held):
    for far, out in enumerate((out0, out1, out2, out3)):
        for near in range(SIDE):
            place = far * SIDE + near
            block = arrived_ref[places_ref[place]].astype(F32)
            held[near * POOL : (near + 1) * POOL, :] = block[0:POOL]
            label_ref[place : place + 1, :] = block[POOL : POOL + 1]
        out[...] = jnp.dot(
            held[...].astype(BF16), weight_ref[...], preferred_element_type=F32
        ).astype(BF16)


def middle_kernel(in0, in1, in2, in3, out0, out1, out2, out3, held):
    held[...] = (in0[...].astype(F32) + in1[...].astype(F32)) + (
        in2[...].astype(F32) + in3[...].astype(F32)
    )
    part = out0.shape[0]
    for place, out in enumerate((out0, out1, out2, out3)):
        out[...] = held[place * part : (place + 1) * part, :].astype(BF16)


def join_kernel(in0, in1, in2, in3, out, held):
    part = in0.shape[0]
    for place, piece in enumerate((in0, in1, in2, in3)):
        held[place * part : (place + 1) * part, :] = piece[...].astype(F32)
    out[...] = held[...].astype(BF16)


def row_mod_kernel(index_ref, mod_ref, out_ref):
    for row in range(POOL):
        values = mod_ref[index_ref[row]]
        for place in range(6):
            out_ref[place, row : row + 1, :] = values[place : place + 1]


def total_of(parts):
    in0, in1, in2, in3 = parts
    return (in0[...].astype(F32) + in1[...].astype(F32)) + (
        in2[...].astype(F32) + in3[...].astype(F32)
    )


def embed_norm_kernel(in0, in1, in2, in3, mod_ref, embedded_ref, out_ref):
    embedded = total_of((in0, in1, in2, in3)).astype(BF16)
    embedded_ref[...] = embedded
    out_ref[...] = (normed(embedded.astype(F32)) * (1.0 + mod_ref[1]) + mod_ref[0]).astype(BF16)


def residual_norm_kernel(base_ref, in0, in1, in2, in3, mod_ref, mixed_ref, out_ref):
    projected = total_of((in0, in1, in2, in3))
    if len(mod_ref.shape) == 3:
        gate, shift, scale = mod_ref[2], mod_ref[3], mod_ref[4]
    else:
        gate, shift, scale = mod_ref[2:3, :], mod_ref[3:4, :], mod_ref[4:5, :]
    mixed = (base_ref[...].astype(F32) + gate * projected).astype(BF16)
    mixed_ref[...] = mixed
    out_ref[...] = (normed(mixed.astype(F32)) * (1.0 + scale) + shift).astype(BF16)


def one_hot(slot_ref, count):
    line = slot_ref[...]
    shape = (count, line.shape[1])
    return jnp.where(lax.broadcasted_iota(jnp.int32, shape, 0) == line, 1.0, 0.0)


def with_keep(values, keep):
    first = low_half(values.shape)
    return jnp.where(first, values, keep), jnp.where(first, keep, values)


def project(rows, weight_ref):
    both = jnp.concatenate([weight_ref[0], weight_ref[1]], -1)
    first = jnp.dot(rows, both, preferred_element_type=F32)
    return first, jnp.dot(rows, weight_ref[2], preferred_element_type=F32)


def txt_qkv_kernel(in0, in1, in2, in3, weight_ref, gain_ref, slot_ref, out_ref, held):
    part = in0.shape[0]
    for place, piece in enumerate((in0, in1, in2, in3)):
        projected, values = project(piece[...], weight_ref)
        rows = slice(place * part, (place + 1) * part)
        held[rows, 0:128] = (head_norm(projected[:, 0:128], gain_ref[0:1, :])).astype(BF16)
        held[rows, 128:256] = (head_norm(projected[:, 128:256], gain_ref[1:2, :])).astype(BF16)
        held[rows, 256:384] = values.astype(BF16)
    hot = one_hot(slot_ref, 512)
    keep = jnp.sum(hot, -1, keepdims=True)
    slots = jnp.dot(hot.astype(BF16), held[...], preferred_element_type=F32)
    val0, val1 = with_keep(slots[:, 256:384], keep)
    out_ref[:, 0:256] = slots[:, 0:256].astype(BF16)
    out_ref[:, 256:384] = val0.astype(BF16)
    out_ref[:, 384:512] = val1.astype(BF16)


def img_project_kernel(image_ref, mod_ref, weight_ref, out_ref, projected_ref):
    rows = image_ref[...].astype(F32)
    modded = (normed(rows) * (1.0 + mod_ref[0, 1, 0:1, :]) + mod_ref[0, 0, 0:1, :]).astype(BF16)
    out_ref[...] = modded
    projected, values = project(modded, weight_ref)
    projected_ref[:, 0:256] = projected
    projected_ref[:, 256:384] = values


def img_adapt_kernel(
    places_ref, mod_ref, projected_ref, in0, in1, in2, in3, up_ref, gain_ref, out_ref, down, lift
):
    own = pl.program_id(0)
    depth = in0.shape[2]
    for far, piece in enumerate((in0, in1, in2, in3)):
        for near in range(SIDE):
            start = pl.multiple_of(places_ref[far * SIDE + near] * depth, 8)
            down[pl.ds(start, depth), :] = piece[near, own].astype(F32)
    lift[...] = jnp.zeros_like(lift)
    for part in range(3):
        lift[part * 64 : (part + 1) * 64, part * 128 : (part + 1) * 128] = up_ref[0, part]
    low = jnp.dot(mod_ref[...], down[...].astype(BF16), preferred_element_type=F32).astype(BF16)
    projected = projected_ref[...] + ADAPTER_SCALE * jnp.dot(
        low, lift[...], preferred_element_type=F32
    )
    out_ref[:, 0:128] = head_norm(projected[:, 0:128], gain_ref[0:1, :]).astype(BF16)
    out_ref[:, 128:256] = head_norm(projected[:, 128:256], gain_ref[1:2, :]).astype(BF16)
    val0, val1 = with_keep(projected[:, 256:384], 1.0)
    out_ref[:, 256:384] = val0.astype(BF16)
    out_ref[:, 384:512] = val1.astype(BF16)


def attend(queries, tokens):
    scaled = queries.astype(F32) * HEAD_DIM ** (-0.5)
    first = low_half(scaled.shape)
    keys = tokens[:, 128:256]
    results = []
    for head in range(2):
        own = jnp.where(first if head == 0 else ~first, scaled, 0.0).astype(BF16)
        scores = lax.dot_general(
            own, keys, (((1,), (1,)), ((), ())), preferred_element_type=F32
        )
        weights = jnp.exp(scores).astype(BF16)
        summed = jnp.dot(
            weights, tokens[:, 256 + head * 128 : 384 + head * 128], preferred_element_type=F32
        )
        results.append(summed / pltpu.roll(summed, HEAD_DIM, 1))
    return jnp.where(first, results[0], results[1]).astype(BF16)


def img_attend_kernel(
    places_ref, img_ref, slot_ref, weight_ref,
    out0, out1, out2, out3, token_ref, tokens, held, ranked,
):
    for own in range(2):
        tokens[own, 0:256, :] = img_ref[own * 256 : (own + 1) * 256, :]
        for source in range(8):
            start = 256 + source * 32
            tokens[own, start : start + 32, :] = slot_ref[source, own * 32 : (own + 1) * 32, :]
    token_ref[...] = tokens[...]
    for own in range(2):
        held[own * 256 : (own + 1) * 256, :] = attend(tokens[own, 0:256, 0:128], tokens[own])
    for far, out in enumerate((out0, out1, out2, out3)):
        for near in range(SIDE):
            start = pl.multiple_of(places_ref[far * SIDE + near] * 32, 32)
            ranked[near * 32 : (near + 1) * 32, :] = held[pl.ds(start, 32), :]
        out[...] = jnp.dot(ranked[...], weight_ref[...], preferred_element_type=F32).astype(BF16)


def txt_attend_kernel(token_ref, out_ref):
    for own in range(2):
        attended = attend(token_ref[own, 256:512, 0:128], token_ref[own])
        for source in range(8):
            start = source * 32
            out_ref[source, own * 32 : (own + 1) * 32, :] = attended[start : start + 32]


def txt_project_kernel(att_ref, slot_ref, weight_ref, out0, out1, out2, out3):
    hot = one_hot(slot_ref, 512).astype(BF16)
    rows = lax.dot_general(
        hot, att_ref[...], (((0,), (0,)), ((), ())), preferred_element_type=F32
    ).astype(BF16)
    part = out0.shape[0]
    for place, out in enumerate((out0, out1, out2, out3)):
        out[...] = jnp.dot(
            rows[place * part : (place + 1) * part], weight_ref[...], preferred_element_type=F32
        ).astype(BF16)


def feed_kernel(in0, in1, in2, in3, win_ref, wout_ref, out0, out1, out2, out3):
    for piece, out in zip((in0, in1, in2, in3), (out0, out1, out2, out3), strict=True):
        hidden = lax.dot_general(
            piece[...], win_ref[0], (((1,), (1,)), ((), ())), preferred_element_type=F32
        )
        hidden = jax.nn.gelu(hidden, approximate=True).astype(BF16)
        out[...] = jnp.dot(hidden, wout_ref[0], preferred_element_type=F32).astype(BF16)


def txt_final_kernel(mixed_ref, in0, in1, in2, in3, mod_ref, slot_ref, out_ref):
    rows = mixed_ref[...].astype(F32) + mod_ref[5] * total_of((in0, in1, in2, in3))
    hot = one_hot(slot_ref, 32).astype(BF16)
    out_ref[...] = jnp.dot(hot, rows.astype(BF16), preferred_element_type=F32).astype(BF16)


def middle(parts, after=()):
    rows, width = parts[0].shape
    return run(
        middle_kernel,
        [like((rows // SIDE, width))] * SIDE,
        parts,
        scratch=[pltpu.VMEM((rows, width), F32)],
        after=after,
    )


def join(parts, after=()):
    rows, width = parts[0].shape
    return run(
        join_kernel,
        like((rows * SIDE, width)),
        parts,
        scratch=[pltpu.VMEM((rows * SIDE, width), F32)],
        after=after,
    )


def feed(parts, weight_in, weight_out, stream):
    rows, width = parts[0].shape
    hidden = weight_in.shape[1]
    plain = pl.BlockSpec((rows, width), lambda i: (0, 0))
    return pl.pallas_call(
        feed_kernel,
        grid=(1,),
        out_shape=[like((rows, width))] * SIDE,
        in_specs=[plain] * SIDE
        + [
            pl.BlockSpec((1, hidden, width), lambda i: (stream, 0, 0)),
            pl.BlockSpec((1, hidden, width), lambda i: (stream, 0, 0)),
        ],
        out_specs=[plain] * SIDE,
        compiler_params=pltpu.CompilerParams(vmem_limit_bytes=40 << 20),
        cost_estimate=pl.CostEstimate(
            flops=rows * SIDE * width * hidden * 4,
            bytes_accessed=width * hidden * 4 + rows * width * 16,
            transcendentals=rows * SIDE * hidden,
        ),
    )(*parts, weight_in, weight_out)


def shards(
    image,
    prompt_encoder_rows,
    prompt_row_request,
    request_adapter,
    modulation,
    query_key_gain,
    prompt_embed_weight,
    image_query_key_value,
    prompt_query_key_value,
    image_out_weight,
    prompt_out_weight,
    feed_in_weight,
    feed_out_weight,
    adapter_down,
    adapter_up,
):
    grp = lax.axis_index("grp")
    tp = lax.axis_index("tp")
    chip, core = grp // 2, grp % 2
    z, y = tp // SIDE, tp % SIDE
    width = image.shape[1]

    steps = jnp.arange(16)
    far, near = steps // SIDE, steps % SIDE
    places = jnp.where(
        core == 0,
        ((z + far) % SIDE) * SIDE + (y + near) % SIDE,
        ((z + near) % SIDE) * SIDE + (y + far) % SIDE,
    ).astype(jnp.int32)
    down_places = places.reshape(SIDE, SIDE).T.reshape(16)
    gains = jnp.concatenate([query_key_gain, query_key_gain], -1)

    chosen_down = jnp.take(adapter_down, request_adapter, axis=0)
    chosen_up = jnp.take(adapter_up, request_adapter, axis=0)
    down_near = jnp.stack(spread(chosen_down, 1), 0)
    down_parts = spread(down_near, 0)

    request = prompt_row_request[:, 0]
    outgoing = run(
        pack_kernel,
        like((16, 32, 256)),
        (prompt_encoder_rows, prompt_row_request.reshape(1, POOL)),
        scratch=[pltpu.VMEM((32, 256), F32), pltpu.VMEM((8, 256), jnp.int32)],
    )
    arrived = lax.all_to_all(outgoing, "tp", 0, 0, tiled=True)
    *embed_parts, labels = run(
        embed_kernel,
        [like((SIDE * POOL, width))] * SIDE + [like((16, 256), F32)],
        (places, arrived, prompt_embed_weight),
        smem=1,
        scratch=[pltpu.VMEM((SIDE * POOL, 256), F32)],
        flops=320 * 256 * width * 2,
        after=(down_near,),
    )

    prompt_mod = modulation[:, 1]
    mod_pair = jnp.stack([prompt_mod, core_swap(prompt_mod)], 0)
    mod_all = jnp.stack(
        [mod_pair, x_shift(mod_pair, -1), x_shift(mod_pair, 2), x_shift(mod_pair, 1)], 0
    ).reshape(16, 6, width)
    step_own = (request // 4 - chip) % SIDE
    other_own = (request // 2 % 2 + core) % 2
    row_mod = run(
        row_mod_kernel,
        like((6, POOL, width), F32),
        ((step_own * 2 + other_own) * 2 + request % 2, mod_all),
        smem=1,
    )

    target = labels[:, :POOL].astype(jnp.int32)
    slots_all = target // 4 * 64 + target // 2 % 2 * 32 + target % 2
    slots_all = (slots_all + 2 * steps[:, None]).reshape(1, 16 * POOL).astype(jnp.int32)
    earlier = (request[:, None] == request[None, :]) & (
        jnp.arange(POOL)[None, :] < jnp.arange(POOL)[:, None]
    )
    ranked = jnp.sum(earlier.astype(jnp.int32), 1)
    slots_own = (request * CAP + ranked).reshape(1, POOL).astype(jnp.int32)

    blocks = 4
    block = image.shape[0] // blocks
    img_mod, img_projected = pl.pallas_call(
        img_project_kernel,
        grid=(blocks,),
        out_shape=[like(image.shape), like((image.shape[0], 384), F32)],
        in_specs=[
            pl.BlockSpec((block, width), lambda i: (i, 0)),
            pl.BlockSpec((1, 6, 2, width), lambda i: (i // 2, 0, 0, 0)),
            pl.BlockSpec((3, width, 128), lambda i: (0, 0, 0)),
        ],
        out_specs=[
            pl.BlockSpec((block, width), lambda i: (i, 0)),
            pl.BlockSpec((block, 384), lambda i: (i, 0)),
        ],
        compiler_params=pltpu.CompilerParams(vmem_limit_bytes=32 << 20),
        cost_estimate=pl.CostEstimate(
            flops=512 * width * 384 * 2, bytes_accessed=7 << 20, transcendentals=0
        ),
    )(image, modulation.transpose(0, 2, 1, 3), image_query_key_value.transpose(1, 0, 2))
    half = image.shape[0] // 2
    img_parts = pl.pallas_call(
        img_adapt_kernel,
        grid=(2,),
        out_shape=like((image.shape[0], 512)),
        in_specs=[
            pl.BlockSpec(memory_space=pltpu.SMEM),
            pl.BlockSpec((half, width), lambda i: (i, 0)),
            pl.BlockSpec((half, 384), lambda i: (i, 0)),
        ]
        + [pl.BlockSpec(down_near.shape, lambda i: (0, 0, 0, 0))] * SIDE
        + [
            pl.BlockSpec((1, 3, 64, 128), lambda i: (i, 0, 0, 0)),
            pl.BlockSpec((2, 128), lambda i: (0, 0)),
        ],
        out_specs=pl.BlockSpec((half, 512), lambda i: (i, 0)),
        scratch_shapes=[pltpu.VMEM((width, 192), F32), pltpu.VMEM((192, 384), BF16)],
        compiler_params=pltpu.CompilerParams(vmem_limit_bytes=32 << 20),
        cost_estimate=pl.CostEstimate(
            flops=512 * width * 192 * 2, bytes_accessed=6 << 20, transcendentals=0
        ),
    )(down_places, img_mod, img_projected, *down_parts, chosen_up, gains[0])

    embed_sums = exchange(middle(exchange(embed_parts, 1), after=(img_projected,)), 0)
    embedded, txt_mod = run(
        embed_norm_kernel,
        [like((POOL, width))] * 2,
        (*embed_sums, row_mod),
        after=tuple(down_parts[1:]),
    )
    txt_mods = spread(join(spread(txt_mod, 0)), 1)
    slot_parts = run(
        txt_qkv_kernel,
        like((512, 512)),
        (*txt_mods, prompt_query_key_value.transpose(1, 0, 2), gains[1], slots_all),
        scratch=[pltpu.VMEM((16 * POOL, 384), BF16)],
        flops=320 * width * 384 * 2,
        after=(img_parts,),
    )
    slot_parts = lax.all_to_all(slot_parts.reshape(8, 64, 512), "grp", 0, 0, tiled=True)

    *img_terms, tokens = run(
        img_attend_kernel,
        [like((128, width))] * SIDE + [like((2, 512, 512))],
        (places, img_parts, slot_parts, image_out_weight),
        smem=1,
        scratch=[
            pltpu.VMEM((2, 512, 512), BF16),
            pltpu.VMEM((512, 128), BF16),
            pltpu.VMEM((128, 128), BF16),
        ],
        flops=1 << 30,
    )
    img_halfway = middle(exchange(img_terms, 1))
    att_parts = run(txt_attend_kernel, like((8, 64, 128)), (tokens,), flops=1 << 29)
    att_parts = lax.all_to_all(att_parts, "grp", 0, 0, tiled=True).reshape(512, 128)
    txt_terms = run(
        txt_project_kernel,
        [like((SIDE * POOL, width))] * SIDE,
        (att_parts, slots_all, prompt_out_weight),
        flops=320 * 128 * width * 2,
        after=(img_halfway[0],),
    )

    own_mod = lax.dynamic_index_in_dim(modulation[:, 0], tp // 8, 0, keepdims=False)
    own_image = lax.dynamic_slice_in_dim(image, tp * 32, 32, 0)
    mixed_img, norm_img = run(
        residual_norm_kernel,
        [like((32, width))] * 2,
        (own_image, *exchange(img_halfway, 0), own_mod),
    )
    txt_halfway = middle(exchange(txt_terms, 1), after=(norm_img,))
    img_near = join(spread(norm_img, 0))
    mixed_txt, norm_txt = run(
        residual_norm_kernel,
        [like((POOL, width))] * 2,
        (embedded, *exchange(txt_halfway, 0), row_mod),
        after=(img_near,),
    )
    img_rows = spread(img_near, 1)
    txt_near = join(spread(norm_txt, 0), after=(img_rows[1], img_rows[3]))
    txt_rows = spread(txt_near, 1)
    weight_in = feed_in_weight.transpose(0, 2, 1)
    img_terms = feed(img_rows, weight_in, feed_out_weight, 0)
    txt_terms = feed(txt_rows, weight_in, feed_out_weight, 1)
    img_halfway = middle(exchange(img_terms, 1), after=(txt_terms[0],))
    feed_img = exchange(img_halfway, 0)
    txt_halfway = middle(exchange(txt_terms, 1), after=(feed_img[1],))
    feed_txt = exchange(txt_halfway, 0)

    placed = run(
        txt_final_kernel,
        like((32, width)),
        (mixed_txt, *feed_txt, row_mod, slots_own),
    )
    placed = lax.all_to_all(placed.reshape(8, 4, width), "grp", 0, 0, tiled=True)
    prompt_out = placed.reshape(32, width)

    feed_sum = functools.reduce(jnp.add, [part.astype(F32) for part in feed_img])
    image_out = (mixed_img.astype(F32) + own_mod[5] * feed_sum).astype(BF16)
    return (image_out, prompt_out)


def solution(mesh):
    placed = (
        P("grp", None),
        P(("grp", "tp"), None),
        P(("grp", "tp"), None),
        P("grp"),
        P("grp", None, None, None),
        P(),
        P("tp", None),
        P(None, None, "tp"),
        P(None, None, "tp"),
        P("tp", None),
        P("tp", None),
        P(None, None, "tp"),
        P(None, "tp", None),
        P(None, "tp", None),
        P(None, None, None, "tp"),
    )
    return jax.shard_map(
        shards,
        mesh=mesh,
        in_specs=placed,
        out_specs=(P(("grp", "tp"), None), P(("grp", "tp"), None)),
        check_vma=False,
    )
```

```python
import functools

import jax
import jax.numpy as jnp
from jax import lax
from jax.experimental import pallas as pl
from jax.experimental.pallas import tpu as pltpu
from jax.sharding import PartitionSpec as P

HEAD_DIM = 64
CAP = 2
EPSILON = 1e-06
ADAPTER_SCALE = 0.5
SIDE = 4
POOL = 20
F32 = jnp.float32
BF16 = jnp.bfloat16


def torus_shift(values, stage, step):
    pairs = []
    for grp in range(8):
        for tp in range(16):
            z, y = divmod(tp, SIDE)
            if (grp + stage) % 2 == 0:
                y = (y + step) % SIDE
            else:
                z = (z + step) % SIDE
            pairs.append((grp * 16 + tp, grp * 16 + z * SIDE + y))
    return lax.ppermute(values, ("grp", "tp"), pairs)


def ring_swap(values, stage, far):
    pairs = []
    for grp in range(8):
        for tp in range(16):
            z, y = divmod(tp, SIDE)
            if (grp + stage) % 2 == 0:
                y = 3 - y if far else y ^ 1
            else:
                z = 3 - z if far else z ^ 1
            pairs.append((grp * 16 + tp, grp * 16 + z * SIDE + y))
    return lax.ppermute(values, ("grp", "tp"), pairs)


def chip_swap(values, far):
    pairs = []
    for grp in range(8):
        chip = 3 - grp // 2 if far else (grp // 2) ^ 1
        pairs.append((grp, chip * 2 + grp % 2))
    return lax.ppermute(values, "grp", pairs)


def core_swap(values):
    return lax.ppermute(values, "grp", [(grp, grp ^ 1) for grp in range(8)])


def spread(rows, stage):
    return [
        rows,
        torus_shift(rows, stage, -1),
        torus_shift(rows, stage, 2),
        torus_shift(rows, stage, 1),
    ]


def exchange(parts, stage):
    return [
        parts[0],
        torus_shift(parts[3], stage, -1),
        torus_shift(parts[2], stage, 2),
        torus_shift(parts[1], stage, 1),
    ]


def run(kernel, outs, args, smem=0, scratch=(), flops=0, limit=32, after=()):
    specs = [pl.BlockSpec(memory_space=pltpu.SMEM)] * smem
    specs += [pl.BlockSpec(memory_space=pltpu.VMEM)] * (len(args) - smem)
    specs += [pl.BlockSpec(memory_space=pl.ANY)] * len(after)
    count = len(args)
    single = not isinstance(outs, list)
    shapes = [outs] if single else outs
    moved = sum(a.size * a.dtype.itemsize for a in args)
    moved += sum(s.size * s.dtype.itemsize for s in shapes)

    def body(*refs):
        kernel(*refs[:count], *refs[count + len(after) :])

    result = pl.pallas_call(
        body,
        out_shape=shapes,
        in_specs=specs,
        out_specs=[pl.BlockSpec(memory_space=pltpu.VMEM)] * len(shapes),
        scratch_shapes=list(scratch),
        compiler_params=pltpu.CompilerParams(vmem_limit_bytes=limit << 20),
        cost_estimate=pl.CostEstimate(flops=flops, bytes_accessed=moved, transcendentals=0),
    )(*args, *after)
    return result[0] if single else result


def like(shape, dtype=BF16):
    return jax.ShapeDtypeStruct(shape, dtype)


def normed(values):
    centred = values - jnp.mean(values, -1, keepdims=True)
    return centred * lax.rsqrt(jnp.mean(centred * centred, -1, keepdims=True) + EPSILON)


def low_half(shape):
    return lax.broadcasted_iota(jnp.int32, shape, len(shape) - 1) < HEAD_DIM


def head_norm(values, gains):
    first = low_half(values.shape)
    squares = values * values
    head0 = jnp.sum(jnp.where(first, squares, 0.0), -1, keepdims=True)
    head1 = jnp.sum(jnp.where(first, 0.0, squares), -1, keepdims=True)
    scale = jnp.where(
        first,
        lax.rsqrt(head0 * (1.0 / HEAD_DIM) + EPSILON),
        lax.rsqrt(head1 * (1.0 / HEAD_DIM) + EPSILON),
    )
    return values * scale * gains


def pack_kernel(rows_ref, line_ref, out_ref, held, wide):
    wide[...] = jnp.full(wide.shape, -1, jnp.int32)
    wide[0:1, 0:POOL] = line_ref[...]
    line = wide[0:1, :]
    first = lax.broadcasted_iota(jnp.int32, (POOL, 256), 0)
    second = lax.broadcasted_iota(jnp.int32, (POOL, 256), 1)
    column = jnp.sum(jnp.where(first == second, line, 0), 1, keepdims=True)
    rank = jnp.sum(jnp.where((column == line) & (first < second), 1, 0), 0, keepdims=True)
    held[...] = jnp.zeros_like(held)
    held[POOL : POOL + 1, :] = (line * CAP + rank).astype(F32)
    for block in range(16):
        held[0:POOL, :] = rows_ref[:, block * 256 : (block + 1) * 256].astype(F32)
        out_ref[block] = held[...].astype(BF16)


def embed_kernel(places_ref, arrived_ref, weight_ref, out0, out1, out2, out3, label_ref, held):
    for far, out in enumerate((out0, out1, out2, out3)):
        for near in range(SIDE):
            place = far * SIDE + near
            block = arrived_ref[places_ref[place]].astype(F32)
            held[near * POOL : (near + 1) * POOL, :] = block[0:POOL]
            label_ref[place : place + 1, :] = block[POOL : POOL + 1]
        out[...] = jnp.dot(
            held[...].astype(BF16), weight_ref[...], preferred_element_type=F32
        ).astype(BF16)


def halve_kernel(odd_ref, in0, in1, in2, in3, keep_ref, send_ref, held):
    held[...] = total_of((in0, in1, in2, in3))
    part = send_ref.shape[0] // 2
    parts = [held[place * part : (place + 1) * part, :] for place in range(SIDE)]
    odd = odd_ref[0] == 1
    keep_ref[0] = parts[0]
    keep_ref[1] = jnp.where(odd, parts[3], parts[1])
    held[0:part, :] = jnp.where(odd, parts[1], parts[3])
    held[part : 2 * part, :] = parts[2]
    send_ref[...] = held[0 : 2 * part, :].astype(BF16)


def quarter_kernel(keep_ref, got_ref, own_ref, send_ref, held):
    part = send_ref.shape[0]
    held[...] = got_ref[...].astype(F32)
    own_ref[...] = keep_ref[0] + held[0:part, :]
    send_ref[...] = (keep_ref[1] + held[part : 2 * part, :]).astype(BF16)


def pair_kernel(first_ref, second_ref, out_ref, held):
    part = first_ref.shape[0]
    held[0:part, :] = first_ref[...].astype(F32)
    held[part : 2 * part, :] = second_ref[...].astype(F32)
    out_ref[...] = held[...].astype(BF16)


def join_kernel(odd_ref, pair_ref, far_ref, out_ref, held_pair, held_far, held):
    part = pair_ref.shape[0] // 2
    odd = odd_ref[0] == 1
    held_pair[...] = pair_ref[...].astype(F32)
    held_far[...] = far_ref[...].astype(F32)
    near, ahead = held_pair[part : 2 * part, :], held_far[0:part, :]
    held[0:part, :] = held_pair[0:part, :]
    held[part : 2 * part, :] = jnp.where(odd, ahead, near)
    held[2 * part : 3 * part, :] = held_far[part : 2 * part, :]
    held[3 * part : 4 * part, :] = jnp.where(odd, near, ahead)
    out_ref[...] = held[...].astype(BF16)


def down_kernel(in0, in1, in2, in3, out_ref):
    for place, piece in enumerate((in0, in1, in2, in3)):
        out_ref[place] = piece[...]


def pick_kernel(index_ref, table_ref, out_ref):
    out_ref[...] = table_ref[...]


def prompt_mod_kernel(mod_ref, out_ref):
    for own in range(2):
        for place in range(6):
            out_ref[own, place : place + 1, :] = mod_ref[own, place, 1:2, :]


def mod_pair_kernel(first_ref, second_ref, out_ref):
    count = first_ref.shape[0]
    out_ref[0:count] = first_ref[...]
    out_ref[count : 2 * count] = second_ref[...]


def row_mod_kernel(index_ref, near_ref, far_ref, out_ref):
    for row in range(POOL):
        index = index_ref[row]
        within = lax.rem(index, 8)
        values = jnp.where(index < 8, near_ref[within], far_ref[within])
        for place in range(6):
            out_ref[place, row : row + 1, :] = values[place : place + 1]


def total_of(parts):
    return functools.reduce(jnp.add, [part[...].astype(F32) for part in parts])


def embed_norm_kernel(in0, in1, mod_ref, embedded_ref, out_ref):
    embedded = total_of((in0, in1)).astype(BF16)
    embedded_ref[...] = embedded
    out_ref[...] = (normed(embedded.astype(F32)) * (1.0 + mod_ref[1]) + mod_ref[0]).astype(BF16)


def residual_norm_kernel(base_ref, in0, in1, mod_ref, mixed_ref, out_ref):
    projected = total_of((in0, in1))
    if len(mod_ref.shape) == 3:
        gate, shift, scale = mod_ref[2], mod_ref[3], mod_ref[4]
    else:
        gate, shift, scale = mod_ref[2:3, :], mod_ref[3:4, :], mod_ref[4:5, :]
    mixed = (base_ref[...].astype(F32) + gate * projected).astype(BF16)
    mixed_ref[...] = mixed
    out_ref[...] = (normed(mixed.astype(F32)) * (1.0 + scale) + shift).astype(BF16)


def one_hot(slot_ref, count):
    line = slot_ref[...]
    shape = (count, line.shape[1])
    return jnp.where(lax.broadcasted_iota(jnp.int32, shape, 0) == line, 1.0, 0.0)


def with_keep(values, keep):
    first = low_half(values.shape)
    return jnp.where(first, values, keep), jnp.where(first, keep, values)


def project(rows, weight_ref):
    both = jnp.concatenate([weight_ref[0], weight_ref[1]], -1)
    first = jnp.dot(rows, both, preferred_element_type=F32)
    return first, jnp.dot(rows, weight_ref[2], preferred_element_type=F32)


def txt_qkv_kernel(in0, in1, in2, in3, weight_ref, gain_ref, slot_ref, out_ref, held, rows_ref):
    part = in0.shape[0]
    for place, piece in enumerate((in0, in1, in2, in3)):
        rows_ref[place * part : (place + 1) * part, :] = piece[...]
    projected, values = project(rows_ref[...], weight_ref)
    held[:, 0:128] = head_norm(projected[:, 0:128], gain_ref[0:1, :]).astype(BF16)
    held[:, 128:256] = head_norm(projected[:, 128:256], gain_ref[1:2, :]).astype(BF16)
    held[:, 256:384] = values.astype(BF16)
    hot = one_hot(slot_ref, 512)
    keep = jnp.sum(hot, -1, keepdims=True)
    slots = jnp.dot(hot.astype(BF16), held[...], preferred_element_type=F32)
    val0, val1 = with_keep(slots[:, 256:384], keep)
    out_ref[:, 0:256] = slots[:, 0:256].astype(BF16)
    out_ref[:, 256:384] = val0.astype(BF16)
    out_ref[:, 384:512] = val1.astype(BF16)


def img_project_kernel(image_ref, mod_ref, weight_ref, out_ref, projected_ref):
    rows = image_ref[...].astype(F32)
    modded = (normed(rows) * (1.0 + mod_ref[0, 1, 0:1, :]) + mod_ref[0, 0, 0:1, :]).astype(BF16)
    out_ref[...] = modded
    projected, values = project(modded, weight_ref)
    projected_ref[:, 0:256] = projected
    projected_ref[:, 256:384] = values


def img_adapt_kernel(
    adapter_ref, places_ref, mod_ref, projected_ref, in0, in1, in2, in3, up_ref, gain_ref,
    out_ref, down, lift,
):
    own = pl.program_id(0)
    depth = in0.shape[2]
    for far, piece in enumerate((in0, in1, in2, in3)):
        for near in range(SIDE):
            start = pl.multiple_of(places_ref[far * SIDE + near] * depth, 8)
            down[pl.ds(start, depth), :] = piece[near, own].astype(F32)
    lift[...] = jnp.zeros_like(lift)
    for part in range(3):
        lift[part * 64 : (part + 1) * 64, part * 128 : (part + 1) * 128] = up_ref[0, part]
    low = jnp.dot(mod_ref[...], down[...].astype(BF16), preferred_element_type=F32).astype(BF16)
    projected = projected_ref[...] + ADAPTER_SCALE * jnp.dot(
        low, lift[...], preferred_element_type=F32
    )
    out_ref[:, 0:128] = head_norm(projected[:, 0:128], gain_ref[0:1, :]).astype(BF16)
    out_ref[:, 128:256] = head_norm(projected[:, 128:256], gain_ref[1:2, :]).astype(BF16)
    val0, val1 = with_keep(projected[:, 256:384], 1.0)
    out_ref[:, 256:384] = val0.astype(BF16)
    out_ref[:, 384:512] = val1.astype(BF16)


def attend(queries, tokens):
    scaled = queries.astype(F32) * HEAD_DIM ** (-0.5)
    first = low_half(scaled.shape)
    keys = tokens[:, 128:256]
    results = []
    for head in range(2):
        own = jnp.where(first if head == 0 else ~first, scaled, 0.0).astype(BF16)
        scores = lax.dot_general(
            own, keys, (((1,), (1,)), ((), ())), preferred_element_type=F32
        )
        weights = jnp.exp(scores).astype(BF16)
        summed = jnp.dot(
            weights, tokens[:, 256 + head * 128 : 384 + head * 128], preferred_element_type=F32
        )
        results.append(summed / pltpu.roll(summed, HEAD_DIM, 1))
    return jnp.where(first, results[0], results[1]).astype(BF16)


def img_attend_kernel(
    places_ref, img_ref, slot_ref, weight_ref,
    out0, out1, out2, out3, token_ref, tokens, held, ranked,
):
    for own in range(2):
        tokens[own, 0:256, :] = img_ref[own * 256 : (own + 1) * 256, :]
        for source in range(8):
            start = 256 + source * 32
            tokens[own, start : start + 32, :] = slot_ref[source, own * 32 : (own + 1) * 32, :]
    token_ref[...] = tokens[...]
    for own in range(2):
        held[own * 256 : (own + 1) * 256, :] = attend(tokens[own, 0:256, 0:128], tokens[own])
    for place in range(16):
        start = pl.multiple_of(places_ref[place] * 32, 32)
        ranked[place * 32 : (place + 1) * 32, :] = held[pl.ds(start, 32), :]
    result = jnp.dot(ranked[...], weight_ref[...], preferred_element_type=F32)
    for place, out in enumerate((out0, out1, out2, out3)):
        out[...] = result[place * 128 : (place + 1) * 128].astype(BF16)


def txt_attend_kernel(token_ref, out_ref):
    for own in range(2):
        attended = attend(token_ref[own, 256:512, 0:128], token_ref[own])
        for source in range(8):
            start = source * 32
            out_ref[source, own * 32 : (own + 1) * 32, :] = attended[start : start + 32]


def txt_project_kernel(att_ref, slot_ref, weight_ref, out0, out1, out2, out3):
    hot = one_hot(slot_ref, 512).astype(BF16)
    rows = lax.dot_general(
        hot, att_ref[...], (((0,), (0,)), ((), ())), preferred_element_type=F32
    ).astype(BF16)
    part = out0.shape[0]
    result = jnp.dot(rows, weight_ref[...], preferred_element_type=F32)
    for place, out in enumerate((out0, out1, out2, out3)):
        out[...] = result[place * part : (place + 1) * part].astype(BF16)


def feed_kernel(in0, in1, in2, in3, win_ref, wout_ref, out0, out1, out2, out3, rows_ref):
    part = in0.shape[0]
    for place, piece in enumerate((in0, in1, in2, in3)):
        rows_ref[place * part : (place + 1) * part, :] = piece[...]
    hidden = lax.dot_general(
        rows_ref[...], win_ref[0], (((1,), (1,)), ((), ())), preferred_element_type=F32
    )
    hidden = jax.nn.gelu(hidden, approximate=True).astype(BF16)
    result = jnp.dot(hidden, wout_ref[0], preferred_element_type=F32)
    for place, out in enumerate((out0, out1, out2, out3)):
        out[...] = result[place * part : (place + 1) * part].astype(BF16)


def img_final_kernel(mixed_ref, in0, in1, mod_ref, out_ref):
    rows = mixed_ref[...].astype(F32) + mod_ref[5:6, :] * total_of((in0, in1))
    out_ref[...] = rows.astype(BF16)


def txt_final_kernel(mixed_ref, in0, in1, mod_ref, slot_ref, out_ref):
    rows = mixed_ref[...].astype(F32) + mod_ref[5] * total_of((in0, in1))
    hot = one_hot(slot_ref, 32).astype(BF16)
    out_ref[...] = jnp.dot(hot, rows.astype(BF16), preferred_element_type=F32).astype(BF16)


def halve(parts, odd, after=()):
    rows, width = parts[0].shape
    part = rows // SIDE
    return run(
        halve_kernel,
        [like((2, part, width), F32), like((2 * part, width))],
        (odd, *parts),
        smem=1,
        scratch=[pltpu.VMEM((rows, width), F32)],
        after=after,
    )


def finish(halves):
    keep, send = halves
    rows, width = send.shape
    own, send = run(
        quarter_kernel,
        [like((rows // 2, width), F32), like((rows // 2, width))],
        (keep, ring_swap(send, 0, True)),
        scratch=[pltpu.VMEM((rows, width), F32)],
    )
    return own, ring_swap(send, 0, False)


def near_rows(rows, odd, after=()):
    count, width = rows.shape
    pair = run(
        pair_kernel,
        like((2 * count, width)),
        (rows, ring_swap(rows, 0, False)),
        scratch=[pltpu.VMEM((2 * count, width), F32)],
    )
    return run(
        join_kernel,
        like((4 * count, width)),
        (odd, pair, ring_swap(pair, 0, True)),
        smem=1,
        scratch=[
            pltpu.VMEM((2 * count, width), F32),
            pltpu.VMEM((2 * count, width), F32),
            pltpu.VMEM((4 * count, width), F32),
        ],
        after=after,
    )


def feed(parts, weight_in, weight_out, stream):
    rows, width = parts[0].shape
    hidden = weight_in.shape[1]
    plain = pl.BlockSpec((rows, width), lambda i: (0, 0))
    return pl.pallas_call(
        feed_kernel,
        grid=(1,),
        out_shape=[like((rows, width))] * SIDE,
        in_specs=[plain] * SIDE
        + [
            pl.BlockSpec((1, hidden, width), lambda i: (stream, 0, 0)),
            pl.BlockSpec((1, hidden, width), lambda i: (stream, 0, 0)),
        ],
        out_specs=[plain] * SIDE,
        scratch_shapes=[pltpu.VMEM((rows * SIDE, width), BF16)],
        compiler_params=pltpu.CompilerParams(vmem_limit_bytes=40 << 20),
        cost_estimate=pl.CostEstimate(
            flops=rows * SIDE * width * hidden * 4,
            bytes_accessed=width * hidden * 4 + rows * width * 16,
            transcendentals=rows * SIDE * hidden,
        ),
    )(*parts, weight_in, weight_out)


def shards(
    image,
    prompt_encoder_rows,
    prompt_row_request,
    request_adapter,
    modulation,
    query_key_gain,
    prompt_embed_weight,
    image_query_key_value,
    prompt_query_key_value,
    image_out_weight,
    prompt_out_weight,
    feed_in_weight,
    feed_out_weight,
    adapter_down,
    adapter_up,
):
    grp = lax.axis_index("grp")
    tp = lax.axis_index("tp")
    chip, core = grp // 2, grp % 2
    z, y = tp // SIDE, tp % SIDE
    width = image.shape[1]

    steps = jnp.arange(16)
    far, near = steps // SIDE, steps % SIDE
    places = jnp.where(
        core == 0,
        ((z + far) % SIDE) * SIDE + (y + near) % SIDE,
        ((z + near) % SIDE) * SIDE + (y + far) % SIDE,
    ).astype(jnp.int32)
    down_places = places.reshape(SIDE, SIDE).T.reshape(16)
    gains = jnp.concatenate([query_key_gain, query_key_gain], -1)

    request = prompt_row_request[:, 0]
    outgoing = run(
        pack_kernel,
        like((16, 32, 256)),
        (prompt_encoder_rows, prompt_row_request.reshape(1, POOL)),
        scratch=[pltpu.VMEM((32, 256), F32), pltpu.VMEM((8, 256), jnp.int32)],
    )
    arrived = lax.all_to_all(outgoing, "tp", 0, 0, tiled=True)
    chosen_down = pl.pallas_call(
        pick_kernel,
        grid_spec=pltpu.PrefetchScalarGridSpec(
            num_scalar_prefetch=1,
            grid=(2,),
            in_specs=[pl.BlockSpec((1, *adapter_down.shape[1:]), lambda i, ids: (ids[i], 0, 0))],
            out_specs=pl.BlockSpec((1, *adapter_down.shape[1:]), lambda i, ids: (i, 0, 0)),
        ),
        out_shape=like((2, *adapter_down.shape[1:])),
    )(request_adapter, adapter_down)
    down_pieces = spread(chosen_down, 1)

    prompt_mod = run(
        prompt_mod_kernel, like((2, 6, width), F32), (modulation.transpose(0, 2, 1, 3),)
    )
    mod_own = run(
        mod_pair_kernel, like((4, 6, width), F32), (prompt_mod, core_swap(prompt_mod))
    )
    mod_near = run(
        mod_pair_kernel, like((8, 6, width), F32), (mod_own, chip_swap(mod_own, False))
    )
    home = request // 4
    row_index = jnp.where(
        home == chip, 0, jnp.where(home == (chip ^ 1), 1, jnp.where(home == 3 - chip, 2, 3))
    )
    row_index = row_index * 4 + (request // 2 % 2 + core) % 2 * 2 + request % 2
    row_mod = run(
        row_mod_kernel,
        like((6, POOL, width), F32),
        (row_index, mod_near, chip_swap(mod_near, True)),
        smem=1,
    )

    *embed_parts, labels = run(
        embed_kernel,
        [like((SIDE * POOL, width))] * SIDE + [like((16, 256), F32)],
        (places, arrived, prompt_embed_weight),
        smem=1,
        scratch=[pltpu.VMEM((SIDE * POOL, 256), F32)],
        flops=320 * 256 * width * 2,
        after=(*down_pieces[1:], mod_own),
    )

    target = labels[:, :POOL].astype(jnp.int32)
    slots_all = target // 4 * 64 + target // 2 % 2 * 32 + target % 2
    slots_all = (slots_all + 2 * steps[:, None]).reshape(1, 16 * POOL).astype(jnp.int32)
    earlier = (request[:, None] == request[None, :]) & (
        jnp.arange(POOL)[None, :] < jnp.arange(POOL)[:, None]
    )
    ranked = jnp.sum(earlier.astype(jnp.int32), 1)
    slots_own = (request * CAP + ranked).reshape(1, POOL).astype(jnp.int32)

    blocks = 4
    block = image.shape[0] // blocks
    img_mod, img_projected = pl.pallas_call(
        img_project_kernel,
        grid=(blocks,),
        out_shape=[like(image.shape), like((image.shape[0], 384), F32)],
        in_specs=[
            pl.BlockSpec((block, width), lambda i: (i, 0)),
            pl.BlockSpec((1, 6, 2, width), lambda i: (i // 2, 0, 0, 0)),
            pl.BlockSpec((3, width, 128), lambda i: (0, 0, 0)),
        ],
        out_specs=[
            pl.BlockSpec((block, width), lambda i: (i, 0)),
            pl.BlockSpec((block, 384), lambda i: (i, 0)),
        ],
        compiler_params=pltpu.CompilerParams(vmem_limit_bytes=32 << 20),
        cost_estimate=pl.CostEstimate(
            flops=512 * width * 384 * 2, bytes_accessed=7 << 20, transcendentals=0
        ),
    )(image, modulation.transpose(0, 2, 1, 3), image_query_key_value.transpose(1, 0, 2))
    odd = (jnp.where(core == 0, y, z) % 2).reshape(1).astype(jnp.int32)
    embed_halves = halve(exchange(embed_parts, 1), odd, after=(img_projected, mod_near))
    down_near = run(
        down_kernel,
        like((SIDE, *chosen_down.shape)),
        down_pieces,
        after=(embed_halves[1],),
    )
    down_parts = spread(down_near, 0)
    embedded, txt_mod = run(
        embed_norm_kernel, [like((POOL, width))] * 2, (*finish(embed_halves), row_mod)
    )
    txt_near = near_rows(txt_mod, odd, after=tuple(down_parts[1:]))
    half = image.shape[0] // 2
    img_parts = pl.pallas_call(
        img_adapt_kernel,
        grid_spec=pltpu.PrefetchScalarGridSpec(
            num_scalar_prefetch=2,
            grid=(2,),
            in_specs=[
                pl.BlockSpec((half, width), lambda i, *_: (i, 0)),
                pl.BlockSpec((half, 384), lambda i, *_: (i, 0)),
            ]
            + [pl.BlockSpec(down_near.shape, lambda i, *_: (0, 0, 0, 0))] * SIDE
            + [
                pl.BlockSpec((1, 3, 64, 128), lambda i, ids, _: (ids[i], 0, 0, 0)),
                pl.BlockSpec((2, 128), lambda i, *_: (0, 0)),
            ],
            out_specs=pl.BlockSpec((half, 512), lambda i, *_: (i, 0)),
            scratch_shapes=[pltpu.VMEM((width, 192), F32), pltpu.VMEM((192, 384), BF16)],
        ),
        out_shape=like((image.shape[0], 512)),
        compiler_params=pltpu.CompilerParams(vmem_limit_bytes=32 << 20),
        cost_estimate=pl.CostEstimate(
            flops=512 * width * 192 * 2, bytes_accessed=6 << 20, transcendentals=0
        ),
    )(
        request_adapter, down_places, img_mod, img_projected, *down_parts, adapter_up, gains[0]
    )

    txt_mods = spread(txt_near, 1)
    slot_parts = run(
        txt_qkv_kernel,
        like((512, 512)),
        (*txt_mods, prompt_query_key_value.transpose(1, 0, 2), gains[1], slots_all),
        scratch=[pltpu.VMEM((16 * POOL, 384), BF16), pltpu.VMEM((16 * POOL, width), BF16)],
        flops=320 * width * 384 * 2,
        after=(img_parts,),
    )
    slot_parts = lax.all_to_all(slot_parts.reshape(8, 64, 512), "grp", 0, 0, tiled=True)

    *img_terms, tokens = run(
        img_attend_kernel,
        [like((128, width))] * SIDE + [like((2, 512, 512))],
        (places, img_parts, slot_parts, image_out_weight),
        smem=1,
        scratch=[
            pltpu.VMEM((2, 512, 512), BF16),
            pltpu.VMEM((512, 128), BF16),
            pltpu.VMEM((512, 128), BF16),
        ],
        flops=1 << 30,
    )
    img_halves = halve(exchange(img_terms, 1), odd)
    att_parts = run(txt_attend_kernel, like((8, 64, 128)), (tokens,), flops=1 << 29)
    att_parts = lax.all_to_all(att_parts, "grp", 0, 0, tiled=True).reshape(512, 128)
    txt_terms = run(
        txt_project_kernel,
        [like((SIDE * POOL, width))] * SIDE,
        (att_parts, slots_all, prompt_out_weight),
        flops=320 * 128 * width * 2,
        after=(img_halves[1],),
    )

    own_mod = lax.dynamic_index_in_dim(modulation[:, 0], tp // 8, 0, keepdims=False)
    own_image = lax.dynamic_slice_in_dim(image, tp * 32, 32, 0)
    mixed_img, norm_img = run(
        residual_norm_kernel,
        [like((32, width))] * 2,
        (own_image, *finish(img_halves), own_mod),
    )
    txt_halves = halve(exchange(txt_terms, 1), odd, after=(norm_img,))
    img_near = near_rows(norm_img, odd)
    mixed_txt, norm_txt = run(
        residual_norm_kernel,
        [like((POOL, width))] * 2,
        (embedded, *finish(txt_halves), row_mod),
        after=(img_near,),
    )
    img_rows = spread(img_near, 1)
    txt_near = near_rows(norm_txt, odd, after=(img_rows[1], img_rows[3]))
    txt_rows = spread(txt_near, 1)
    weight_in = feed_in_weight.transpose(0, 2, 1)
    img_terms = feed(img_rows, weight_in, feed_out_weight, 0)
    txt_terms = feed(txt_rows, weight_in, feed_out_weight, 1)
    img_halves = halve(exchange(img_terms, 1), odd, after=(txt_terms[0],))
    image_out = run(
        img_final_kernel, like((32, width)), (mixed_img, *finish(img_halves), own_mod)
    )
    txt_halves = halve(exchange(txt_terms, 1), odd, after=(image_out,))

    placed = run(
        txt_final_kernel,
        like((32, width)),
        (mixed_txt, *finish(txt_halves), row_mod, slots_own),
    )
    placed = lax.all_to_all(placed.reshape(8, 4, width), "grp", 0, 0, tiled=True)
    prompt_out = placed.reshape(32, width)

    return (image_out, prompt_out)


def solution(mesh):
    placed = (
        P("grp", None),
        P(("grp", "tp"), None),
        P(("grp", "tp"), None),
        P("grp"),
        P("grp", None, None, None),
        P(),
        P("tp", None),
        P(None, None, "tp"),
        P(None, None, "tp"),
        P("tp", None),
        P("tp", None),
        P(None, None, "tp"),
        P(None, "tp", None),
        P(None, "tp", None),
        P(None, None, None, "tp"),
    )
    return jax.shard_map(
        shards,
        mesh=mesh,
        in_specs=placed,
        out_specs=(P(("grp", "tp"), None), P(("grp", "tp"), None)),
        check_vma=False,
    )
```

```python
import functools

import jax
import jax.numpy as jnp
from jax import lax
from jax.experimental import pallas as pl
from jax.experimental.pallas import tpu as pltpu
from jax.sharding import PartitionSpec as P

HEAD_DIM = 64
CAP = 2
EPSILON = 1e-06
ADAPTER_SCALE = 0.5
SIDE = 4
POOL = 20
F32 = jnp.float32
BF16 = jnp.bfloat16


def torus_shift(values, stage, step):
    pairs = []
    for grp in range(8):
        for tp in range(16):
            z, y = divmod(tp, SIDE)
            if (grp + stage) % 2 == 0:
                y = (y + step) % SIDE
            else:
                z = (z + step) % SIDE
            pairs.append((grp * 16 + tp, grp * 16 + z * SIDE + y))
    return lax.ppermute(values, ("grp", "tp"), pairs)


def spread(rows, stage):
    return [
        rows,
        torus_shift(rows, stage, -1),
        torus_shift(rows, stage, 2),
        torus_shift(rows, stage, 1),
    ]


def exchange(parts, stage):
    return [
        parts[0],
        torus_shift(parts[3], stage, -1),
        torus_shift(parts[2], stage, 2),
        torus_shift(parts[1], stage, 1),
    ]


def run(kernel, outs, args, smem=0, scratch=(), flops=0, limit=32, after=()):
    specs = [pl.BlockSpec(memory_space=pltpu.SMEM)] * smem
    specs += [pl.BlockSpec(memory_space=pltpu.VMEM)] * (len(args) - smem)
    specs += [pl.BlockSpec(memory_space=pl.ANY)] * len(after)
    count = len(args)
    single = not isinstance(outs, list)
    shapes = [outs] if single else outs
    moved = sum(a.size * a.dtype.itemsize for a in args)
    moved += sum(s.size * s.dtype.itemsize for s in shapes)

    def body(*refs):
        kernel(*refs[:count], *refs[count + len(after) :])

    result = pl.pallas_call(
        body,
        out_shape=shapes,
        in_specs=specs,
        out_specs=[pl.BlockSpec(memory_space=pltpu.VMEM)] * len(shapes),
        scratch_shapes=list(scratch),
        compiler_params=pltpu.CompilerParams(vmem_limit_bytes=limit << 20),
        cost_estimate=pl.CostEstimate(flops=flops, bytes_accessed=moved, transcendentals=0),
    )(*args, *after)
    return result[0] if single else result


def like(shape, dtype=BF16):
    return jax.ShapeDtypeStruct(shape, dtype)


def normed(values):
    centred = values - jnp.mean(values, -1, keepdims=True)
    return centred * lax.rsqrt(jnp.mean(centred * centred, -1, keepdims=True) + EPSILON)


def low_half(shape):
    return lax.broadcasted_iota(jnp.int32, shape, len(shape) - 1) < HEAD_DIM


def head_norm(values, gains):
    first = low_half(values.shape)
    squares = values * values
    head0 = jnp.sum(jnp.where(first, squares, 0.0), -1, keepdims=True)
    head1 = jnp.sum(jnp.where(first, 0.0, squares), -1, keepdims=True)
    scale = jnp.where(
        first,
        lax.rsqrt(head0 * (1.0 / HEAD_DIM) + EPSILON),
        lax.rsqrt(head1 * (1.0 / HEAD_DIM) + EPSILON),
    )
    return values * scale * gains


def pack_kernel(rows_ref, line_ref, out_ref, held, wide):
    wide[...] = jnp.full(wide.shape, -1, jnp.int32)
    wide[0:1, 0:POOL] = line_ref[...]
    line = wide[0:1, :]
    first = lax.broadcasted_iota(jnp.int32, (POOL, 256), 0)
    second = lax.broadcasted_iota(jnp.int32, (POOL, 256), 1)
    column = jnp.sum(jnp.where(first == second, line, 0), 1, keepdims=True)
    rank = jnp.sum(jnp.where((column == line) & (first < second), 1, 0), 0, keepdims=True)
    held[...] = jnp.zeros_like(held)
    held[POOL : POOL + 1, :] = (line * CAP + rank).astype(F32)
    for block in range(16):
        held[0:POOL, :] = rows_ref[:, block * 256 : (block + 1) * 256].astype(F32)
        out_ref[block] = held[...].astype(BF16)


def embed_kernel(places_ref, arrived_ref, weight_ref, out0, out1, out2, out3, label_ref, held):
    for far, out in enumerate((out0, out1, out2, out3)):
        for near in range(SIDE):
            place = far * SIDE + near
            block = arrived_ref[places_ref[place]].astype(F32)
            held[near * POOL : (near + 1) * POOL, :] = block[0:POOL]
            label_ref[place : place + 1, :] = block[POOL : POOL + 1]
        out[...] = jnp.dot(
            held[...].astype(BF16), weight_ref[...], preferred_element_type=F32
        ).astype(BF16)


def middle_kernel(in0, in1, in2, in3, out0, out1, out2, out3, held):
    held[...] = total_of((in0, in1, in2, in3))
    part = out0.shape[0]
    for place, out in enumerate((out0, out1, out2, out3)):
        out[...] = held[place * part : (place + 1) * part, :].astype(BF16)


def both_middle_kernel(*refs):
    held = refs[12]
    held[...] = total_of(refs[4:8])
    total = total_of(refs[0:4])
    for place, out in enumerate(refs[8:12]):
        out[0:32, :] = total[place * 32 : (place + 1) * 32].astype(BF16)
        out[32 : 32 + POOL, :] = held[place * POOL : (place + 1) * POOL, :].astype(BF16)


def join_kernel(start, in0, in1, in2, in3, out_ref, held):
    part = out_ref.shape[0] // SIDE
    for place, piece in enumerate((in0, in1, in2, in3)):
        held[place * part : (place + 1) * part, :] = piece[start : start + part, :].astype(F32)
    out_ref[...] = held[...].astype(BF16)


def repeat_mod_kernel(mod_ref, out_ref):
    out_ref[...] = jnp.zeros_like(out_ref)
    for own in range(2):
        for place in range(6):
            line = mod_ref[own, place, 1:2, :]
            for group in range(8):
                out_ref[group, own, place : place + 1, :] = line


def row_mod_kernel(index_ref, mod_ref, out_ref):
    for row in range(POOL):
        values = mod_ref[index_ref[row]]
        for place in range(6):
            out_ref[place, row : row + 1, :] = values[place : place + 1]


def total_of(parts):
    return functools.reduce(jnp.add, [part[...].astype(F32) for part in parts])


def embed_norm_kernel(in0, in1, in2, in3, mod_ref, embedded_ref, out_ref):
    embedded = total_of((in0, in1, in2, in3)).astype(BF16)
    embedded_ref[...] = embedded
    out_ref[...] = (normed(embedded.astype(F32)) * (1.0 + mod_ref[1]) + mod_ref[0]).astype(BF16)


def both_norm_kernel(
    image_ref, embedded_ref, in0, in1, in2, in3, img_mod_ref, txt_mod_ref,
    img_ref, txt_ref, out_ref,
):
    projected = total_of((in0, in1, in2, in3))
    gate, shift, scale = img_mod_ref[2:3, :], img_mod_ref[3:4, :], img_mod_ref[4:5, :]
    mixed = (image_ref[...].astype(F32) + gate * projected[0:32]).astype(BF16)
    img_ref[...] = mixed
    out_ref[0:32, :] = (normed(mixed.astype(F32)) * (1.0 + scale) + shift).astype(BF16)
    mixed = (embedded_ref[...].astype(F32) + txt_mod_ref[2] * projected[32:]).astype(BF16)
    txt_ref[...] = mixed
    hidden = normed(mixed.astype(F32)) * (1.0 + txt_mod_ref[4]) + txt_mod_ref[3]
    out_ref[32 : 32 + POOL, :] = hidden.astype(BF16)


def one_hot(slot_ref, count):
    line = slot_ref[...]
    shape = (count, line.shape[1])
    return jnp.where(lax.broadcasted_iota(jnp.int32, shape, 0) == line, 1.0, 0.0)


def with_keep(values, keep):
    first = low_half(values.shape)
    return jnp.where(first, values, keep), jnp.where(first, keep, values)


def project(rows, weight_ref):
    both = jnp.concatenate([weight_ref[0], weight_ref[1]], -1)
    first = jnp.dot(rows, both, preferred_element_type=F32)
    return first, jnp.dot(rows, weight_ref[2], preferred_element_type=F32)


def txt_qkv_kernel(in0, in1, in2, in3, weight_ref, gain_ref, slot_ref, out_ref, held, rows_ref):
    part = in0.shape[0]
    for place, piece in enumerate((in0, in1, in2, in3)):
        rows_ref[place * part : (place + 1) * part, :] = piece[...]
    projected, values = project(rows_ref[...], weight_ref)
    held[:, 0:128] = head_norm(projected[:, 0:128], gain_ref[0:1, :]).astype(BF16)
    held[:, 128:256] = head_norm(projected[:, 128:256], gain_ref[1:2, :]).astype(BF16)
    held[:, 256:384] = values.astype(BF16)
    hot = one_hot(slot_ref, 512)
    keep = jnp.sum(hot, -1, keepdims=True)
    slots = jnp.dot(hot.astype(BF16), held[...], preferred_element_type=F32)
    val0, val1 = with_keep(slots[:, 256:384], keep)
    out_ref[:, 0:256] = slots[:, 0:256].astype(BF16)
    out_ref[:, 256:384] = val0.astype(BF16)
    out_ref[:, 384:512] = val1.astype(BF16)


def img_project_kernel(image_ref, mod_ref, weight_ref, out_ref, projected_ref):
    rows = image_ref[...].astype(F32)
    modded = (normed(rows) * (1.0 + mod_ref[0, 1, 0:1, :]) + mod_ref[0, 0, 0:1, :]).astype(BF16)
    out_ref[...] = modded
    projected, values = project(modded, weight_ref)
    projected_ref[:, 0:256] = projected
    projected_ref[:, 256:384] = values


def low_part_kernel(adapter_ref, tp_ref, mod_ref, down_ref, out_ref, wide):
    depth = down_ref.shape[1]
    wide[...] = jnp.zeros_like(wide)
    start = pl.multiple_of(tp_ref[0] * depth, 8)
    wide[pl.ds(start, depth), :] = down_ref[0].astype(F32)
    low = jnp.dot(mod_ref[...], wide[...].astype(BF16), preferred_element_type=F32)
    for block in range(8):
        out_ref[block] = low[block * 32 : (block + 1) * 32].astype(BF16)


def low_sum_kernel(part_ref, out_ref):
    total = part_ref[0].astype(F32)
    for block in range(1, 16):
        total = total + part_ref[block].astype(F32)
    for block in range(16):
        out_ref[block] = total.astype(BF16)


def img_adapt_kernel(adapter_ref, low_ref, projected_ref, up_ref, gain_ref, out_ref, lift):
    lift[...] = jnp.zeros_like(lift)
    for part in range(3):
        lift[part * 64 : (part + 1) * 64, part * 128 : (part + 1) * 128] = up_ref[0, part]
    projected = projected_ref[...] + ADAPTER_SCALE * jnp.dot(
        low_ref[...], lift[...], preferred_element_type=F32
    )
    out_ref[:, 0:128] = head_norm(projected[:, 0:128], gain_ref[0:1, :]).astype(BF16)
    out_ref[:, 128:256] = head_norm(projected[:, 128:256], gain_ref[1:2, :]).astype(BF16)
    val0, val1 = with_keep(projected[:, 256:384], 1.0)
    out_ref[:, 256:384] = val0.astype(BF16)
    out_ref[:, 384:512] = val1.astype(BF16)


def attend(queries, tokens):
    scaled = queries.astype(F32) * HEAD_DIM ** (-0.5)
    first = low_half(scaled.shape)
    keys = tokens[:, 128:256]
    results = []
    for head in range(2):
        own = jnp.where(first if head == 0 else ~first, scaled, 0.0).astype(BF16)
        scores = lax.dot_general(
            own, keys, (((1,), (1,)), ((), ())), preferred_element_type=F32
        )
        weights = jnp.exp(scores).astype(BF16)
        summed = jnp.dot(
            weights, tokens[:, 256 + head * 128 : 384 + head * 128], preferred_element_type=F32
        )
        results.append(summed / pltpu.roll(summed, HEAD_DIM, 1))
    return jnp.where(first, results[0], results[1]).astype(BF16)


def img_attend_kernel(
    places_ref, img_ref, slot_ref, weight_ref,
    out0, out1, out2, out3, token_ref, tokens, held, ranked,
):
    for own in range(2):
        tokens[own, 0:256, :] = img_ref[own * 256 : (own + 1) * 256, :]
        for source in range(8):
            start = 256 + source * 32
            tokens[own, start : start + 32, :] = slot_ref[source, own * 32 : (own + 1) * 32, :]
    token_ref[...] = tokens[...]
    for own in range(2):
        held[own * 256 : (own + 1) * 256, :] = attend(tokens[own, 0:256, 0:128], tokens[own])
    for place in range(16):
        start = pl.multiple_of(places_ref[place] * 32, 32)
        ranked[place * 32 : (place + 1) * 32, :] = held[pl.ds(start, 32), :]
    result = jnp.dot(ranked[...], weight_ref[...], preferred_element_type=F32)
    for place, out in enumerate((out0, out1, out2, out3)):
        out[...] = result[place * 128 : (place + 1) * 128].astype(BF16)


def txt_attend_kernel(token_ref, out_ref):
    for own in range(2):
        attended = attend(token_ref[own, 256:512, 0:128], token_ref[own])
        for source in range(8):
            start = source * 32
            out_ref[source, own * 32 : (own + 1) * 32, :] = attended[start : start + 32]


def txt_project_kernel(att_ref, slot_ref, weight_ref, out0, out1, out2, out3):
    hot = one_hot(slot_ref, 512).astype(BF16)
    rows = lax.dot_general(
        hot, att_ref[...], (((0,), (0,)), ((), ())), preferred_element_type=F32
    ).astype(BF16)
    part = out0.shape[0]
    result = jnp.dot(rows, weight_ref[...], preferred_element_type=F32)
    for place, out in enumerate((out0, out1, out2, out3)):
        out[...] = result[place * part : (place + 1) * part].astype(BF16)


def feed_kernel(in0, in1, in2, in3, win_ref, wout_ref, out0, out1, out2, out3, rows_ref):
    part = in0.shape[0]
    for place, piece in enumerate((in0, in1, in2, in3)):
        rows_ref[place * part : (place + 1) * part, :] = piece[...]
    hidden = lax.dot_general(
        rows_ref[...], win_ref[0], (((1,), (1,)), ((), ())), preferred_element_type=F32
    )
    hidden = jax.nn.gelu(hidden, approximate=True).astype(BF16)
    result = jnp.dot(hidden, wout_ref[0], preferred_element_type=F32)
    for place, out in enumerate((out0, out1, out2, out3)):
        out[...] = result[place * part : (place + 1) * part].astype(BF16)


def both_final_kernel(
    img_ref, txt_ref, in0, in1, in2, in3, img_mod_ref, txt_mod_ref, slot_ref, out_ref, placed_ref
):
    total = total_of((in0, in1, in2, in3))
    out_ref[...] = (img_ref[...].astype(F32) + img_mod_ref[5:6, :] * total[0:32]).astype(BF16)
    rows = txt_ref[...].astype(F32) + txt_mod_ref[5] * total[32:]
    hot = one_hot(slot_ref, 32).astype(BF16)
    placed_ref[...] = jnp.dot(hot, rows.astype(BF16), preferred_element_type=F32).astype(BF16)


def middle(parts, after=()):
    rows, width = parts[0].shape
    return run(
        middle_kernel,
        [like((rows // SIDE, width))] * SIDE,
        parts,
        scratch=[pltpu.VMEM((rows, width), F32)],
        after=after,
    )


def both_middle(img_parts, txt_parts):
    rows, width = txt_parts[0].shape
    return run(
        both_middle_kernel,
        [like((32 + POOL, width))] * SIDE,
        (*img_parts, *txt_parts),
        scratch=[pltpu.VMEM((rows, width), F32)],
    )


def join(parts, start, count, after=()):
    width = parts[0].shape[1]
    return run(
        functools.partial(join_kernel, start),
        like((SIDE * count, width)),
        parts,
        scratch=[pltpu.VMEM((SIDE * count, width), F32)],
        after=after,
    )


def feed(parts, weight_in, weight_out, stream):
    rows, width = parts[0].shape
    hidden = weight_in.shape[1]
    plain = pl.BlockSpec((rows, width), lambda i: (0, 0))
    return pl.pallas_call(
        feed_kernel,
        grid=(1,),
        out_shape=[like((rows, width))] * SIDE,
        in_specs=[plain] * SIDE
        + [
            pl.BlockSpec((1, hidden, width), lambda i: (stream, 0, 0)),
            pl.BlockSpec((1, hidden, width), lambda i: (stream, 0, 0)),
        ],
        out_specs=[plain] * SIDE,
        scratch_shapes=[pltpu.VMEM((rows * SIDE, width), BF16)],
        compiler_params=pltpu.CompilerParams(vmem_limit_bytes=40 << 20),
        cost_estimate=pl.CostEstimate(
            flops=rows * SIDE * width * hidden * 4,
            bytes_accessed=width * hidden * 4 + rows * width * 16,
            transcendentals=rows * SIDE * hidden,
        ),
    )(*parts, weight_in, weight_out)


def shards(
    image,
    prompt_encoder_rows,
    prompt_row_request,
    request_adapter,
    modulation,
    query_key_gain,
    prompt_embed_weight,
    image_query_key_value,
    prompt_query_key_value,
    image_out_weight,
    prompt_out_weight,
    feed_in_weight,
    feed_out_weight,
    adapter_down,
    adapter_up,
):
    grp = lax.axis_index("grp")
    tp = lax.axis_index("tp")
    chip, core = grp // 2, grp % 2
    z, y = tp // SIDE, tp % SIDE
    width = image.shape[1]

    steps = jnp.arange(16)
    far, near = steps // SIDE, steps % SIDE
    places = jnp.where(
        core == 0,
        ((z + far) % SIDE) * SIDE + (y + near) % SIDE,
        ((z + near) % SIDE) * SIDE + (y + far) % SIDE,
    ).astype(jnp.int32)
    gains = jnp.concatenate([query_key_gain, query_key_gain], -1)

    request = prompt_row_request[:, 0]
    outgoing = run(
        pack_kernel,
        like((16, 32, 256)),
        (prompt_encoder_rows, prompt_row_request.reshape(1, POOL)),
        scratch=[pltpu.VMEM((32, 256), F32), pltpu.VMEM((8, 256), jnp.int32)],
    )
    arrived = lax.all_to_all(outgoing, "tp", 0, 0, tiled=True)
    blocks = 4
    block = image.shape[0] // blocks
    img_mod, img_projected = pl.pallas_call(
        img_project_kernel,
        grid=(blocks,),
        out_shape=[like(image.shape), like((image.shape[0], 384), F32)],
        in_specs=[
            pl.BlockSpec((block, width), lambda i: (i, 0)),
            pl.BlockSpec((1, 6, 2, width), lambda i: (i // 2, 0, 0, 0)),
            pl.BlockSpec((3, width, 128), lambda i: (0, 0, 0)),
        ],
        out_specs=[
            pl.BlockSpec((block, width), lambda i: (i, 0)),
            pl.BlockSpec((block, 384), lambda i: (i, 0)),
        ],
        compiler_params=pltpu.CompilerParams(vmem_limit_bytes=32 << 20),
        cost_estimate=pl.CostEstimate(
            flops=512 * width * 384 * 2, bytes_accessed=7 << 20, transcendentals=0
        ),
    )(image, modulation.transpose(0, 2, 1, 3), image_query_key_value.transpose(1, 0, 2))
    half = image.shape[0] // 2
    low_part = pl.pallas_call(
        low_part_kernel,
        grid_spec=pltpu.PrefetchScalarGridSpec(
            num_scalar_prefetch=2,
            grid=(2,),
            in_specs=[
                pl.BlockSpec((half, width), lambda i, *_: (i, 0)),
                pl.BlockSpec((1, *adapter_down.shape[1:]), lambda i, ids, _: (ids[i], 0, 0)),
            ],
            out_specs=pl.BlockSpec((8, 32, 192), lambda i, *_: (i, 0, 0)),
            scratch_shapes=[pltpu.VMEM((width, 192), F32)],
        ),
        out_shape=like((16, 32, 192)),
        compiler_params=pltpu.CompilerParams(vmem_limit_bytes=32 << 20),
        cost_estimate=pl.CostEstimate(
            flops=512 * width * 192 * 2, bytes_accessed=3 << 20, transcendentals=0
        ),
    )(request_adapter, tp.reshape(1).astype(jnp.int32), img_mod, adapter_down)
    low_sum = run(
        low_sum_kernel,
        like((16, 32, 192)),
        (lax.all_to_all(low_part, "tp", 0, 0, tiled=True),),
    )
    low = lax.all_to_all(low_sum, "tp", 0, 0, tiled=True).reshape(2 * half, 192)

    mod_all = run(
        repeat_mod_kernel, like((8, 2, 8, width), F32), (modulation.transpose(0, 2, 1, 3),)
    )
    mod_all = lax.all_to_all(mod_all, "grp", 0, 0, tiled=True).reshape(16, 8, width)
    row_mod = run(row_mod_kernel, like((6, POOL, width), F32), (request, mod_all), smem=1)

    *embed_parts, labels = run(
        embed_kernel,
        [like((SIDE * POOL, width))] * SIDE + [like((16, 256), F32)],
        (places, arrived, prompt_embed_weight),
        smem=1,
        scratch=[pltpu.VMEM((SIDE * POOL, 256), F32)],
        flops=320 * 256 * width * 2,
        after=(img_projected,),
    )
    embed_sums = exchange(middle(exchange(embed_parts, 1), after=(low_part,)), 0)
    embedded, txt_mod = run(
        embed_norm_kernel,
        [like((POOL, width))] * 2,
        (*embed_sums, row_mod),
        after=(low_sum,),
    )
    txt_mods = spread(join(spread(txt_mod, 0), 0, POOL), 1)

    target = labels[:, :POOL].astype(jnp.int32)
    slots_all = target // 4 * 64 + target // 2 % 2 * 32 + target % 2
    slots_all = (slots_all + 2 * steps[:, None]).reshape(1, 16 * POOL).astype(jnp.int32)
    earlier = (request[:, None] == request[None, :]) & (
        jnp.arange(POOL)[None, :] < jnp.arange(POOL)[:, None]
    )
    ranked = jnp.sum(earlier.astype(jnp.int32), 1)
    slots_own = (request * CAP + ranked).reshape(1, POOL).astype(jnp.int32)

    img_parts = pl.pallas_call(
        img_adapt_kernel,
        grid_spec=pltpu.PrefetchScalarGridSpec(
            num_scalar_prefetch=1,
            grid=(2,),
            in_specs=[
                pl.BlockSpec((half, 192), lambda i, _: (i, 0)),
                pl.BlockSpec((half, 384), lambda i, _: (i, 0)),
                pl.BlockSpec((1, 3, 64, 128), lambda i, ids: (ids[i], 0, 0, 0)),
                pl.BlockSpec((2, 128), lambda i, _: (0, 0)),
            ],
            out_specs=pl.BlockSpec((half, 512), lambda i, _: (i, 0)),
            scratch_shapes=[pltpu.VMEM((192, 384), BF16)],
        ),
        out_shape=like((image.shape[0], 512)),
        cost_estimate=pl.CostEstimate(
            flops=512 * 384 * 192 * 2, bytes_accessed=2 << 20, transcendentals=0
        ),
    )(request_adapter, low, img_projected, adapter_up, gains[0])

    slot_parts = run(
        txt_qkv_kernel,
        like((512, 512)),
        (*txt_mods, prompt_query_key_value.transpose(1, 0, 2), gains[1], slots_all),
        scratch=[pltpu.VMEM((16 * POOL, 384), BF16), pltpu.VMEM((16 * POOL, width), BF16)],
        flops=320 * width * 384 * 2,
        after=(img_parts,),
    )
    slot_parts = lax.all_to_all(slot_parts.reshape(8, 64, 512), "grp", 0, 0, tiled=True)

    *img_terms, tokens = run(
        img_attend_kernel,
        [like((128, width))] * SIDE + [like((2, 512, 512))],
        (places, img_parts, slot_parts, image_out_weight),
        smem=1,
        scratch=[
            pltpu.VMEM((2, 512, 512), BF16),
            pltpu.VMEM((512, 128), BF16),
            pltpu.VMEM((512, 128), BF16),
        ],
        flops=1 << 30,
    )
    img_sums = exchange(img_terms, 1)
    att_parts = run(txt_attend_kernel, like((8, 64, 128)), (tokens,), flops=1 << 29)
    att_parts = lax.all_to_all(att_parts, "grp", 0, 0, tiled=True).reshape(512, 128)
    txt_terms = run(
        txt_project_kernel,
        [like((SIDE * POOL, width))] * SIDE,
        (att_parts, slots_all, prompt_out_weight),
        flops=320 * 128 * width * 2,
        after=(img_sums[1], img_sums[3]),
    )
    txt_sums = exchange(txt_terms, 1)

    own_mod = lax.dynamic_index_in_dim(modulation[:, 0], tp // 8, 0, keepdims=False)
    own_image = lax.dynamic_slice_in_dim(image, tp * 32, 32, 0)
    sums = exchange(both_middle(img_sums, txt_sums), 0)
    mixed_img, mixed_txt, norm_rows = run(
        both_norm_kernel,
        [like((32, width)), like((POOL, width)), like((32 + POOL, width))],
        (own_image, embedded, *sums, own_mod, row_mod),
    )
    near_rows = spread(norm_rows, 0)
    img_rows = spread(join(near_rows, 0, 32), 1)
    txt_rows = spread(join(near_rows, 32, POOL, after=(img_rows[1], img_rows[3])), 1)
    weight_in = feed_in_weight.transpose(0, 2, 1)
    img_terms = feed(img_rows, weight_in, feed_out_weight, 0)
    txt_terms = feed(txt_rows, weight_in, feed_out_weight, 1)
    sums = exchange(both_middle(exchange(img_terms, 1), exchange(txt_terms, 1)), 0)
    image_out, placed = run(
        both_final_kernel,
        [like((32, width))] * 2,
        (mixed_img, mixed_txt, *sums, own_mod, row_mod, slots_own),
    )

    placed = lax.all_to_all(placed.reshape(8, 4, width), "grp", 0, 0, tiled=True)
    prompt_out = placed.reshape(32, width)

    return (image_out, prompt_out)


def solution(mesh):
    placed = (
        P("grp", None),
        P(("grp", "tp"), None),
        P(("grp", "tp"), None),
        P("grp"),
        P("grp", None, None, None),
        P(),
        P("tp", None),
        P(None, None, "tp"),
        P(None, None, "tp"),
        P("tp", None),
        P("tp", None),
        P(None, None, "tp"),
        P(None, "tp", None),
        P(None, "tp", None),
        P(None, None, None, "tp"),
    )
    return jax.shard_map(
        shards,
        mesh=mesh,
        in_specs=placed,
        out_specs=(P(("grp", "tp"), None), P(("grp", "tp"), None)),
        check_vma=False,
    )
```

```python
import functools

import jax
import jax.numpy as jnp
from jax import lax
from jax.experimental import pallas as pl
from jax.experimental.pallas import tpu as pltpu
from jax.sharding import PartitionSpec as P

HEAD_DIM = 64
CAP = 2
EPSILON = 1e-06
ADAPTER_SCALE = 0.5
SIDE = 4
POOL = 20
F32 = jnp.float32
BF16 = jnp.bfloat16


def torus_shift(values, stage, step):
    pairs = []
    for grp in range(8):
        for tp in range(16):
            z, y = divmod(tp, SIDE)
            if (grp + stage) % 2 == 0:
                y = (y + step) % SIDE
            else:
                z = (z + step) % SIDE
            pairs.append((grp * 16 + tp, grp * 16 + z * SIDE + y))
    return lax.ppermute(values, ("grp", "tp"), pairs)


def spread(rows, stage):
    return [
        rows,
        torus_shift(rows, stage, -1),
        torus_shift(rows, stage, 2),
        torus_shift(rows, stage, 1),
    ]


def exchange(parts, stage):
    return [
        parts[0],
        torus_shift(parts[3], stage, -1),
        torus_shift(parts[2], stage, 2),
        torus_shift(parts[1], stage, 1),
    ]


def run(kernel, outs, args, smem=0, scratch=(), flops=0, limit=16, after=()):
    specs = [pl.BlockSpec(memory_space=pltpu.SMEM)] * smem
    specs += [pl.BlockSpec(memory_space=pltpu.VMEM)] * (len(args) - smem)
    specs += [pl.BlockSpec(memory_space=pl.ANY)] * len(after)
    count = len(args)
    single = not isinstance(outs, list)
    shapes = [outs] if single else outs
    moved = sum(a.size * a.dtype.itemsize for a in args)
    moved += sum(s.size * s.dtype.itemsize for s in shapes)

    def body(*refs):
        kernel(*refs[:count], *refs[count + len(after) :])

    result = pl.pallas_call(
        body,
        out_shape=shapes,
        in_specs=specs,
        out_specs=[pl.BlockSpec(memory_space=pltpu.VMEM)] * len(shapes),
        scratch_shapes=list(scratch),
        compiler_params=pltpu.CompilerParams(vmem_limit_bytes=limit << 20),
        cost_estimate=pl.CostEstimate(flops=flops, bytes_accessed=moved, transcendentals=0),
    )(*args, *after)
    return result[0] if single else result


def like(shape, dtype=BF16):
    return jax.ShapeDtypeStruct(shape, dtype)


def normed(values):
    centred = values - jnp.mean(values, -1, keepdims=True)
    return centred * lax.rsqrt(jnp.mean(centred * centred, -1, keepdims=True) + EPSILON)


def low_half(shape):
    return lax.broadcasted_iota(jnp.int32, shape, len(shape) - 1) < HEAD_DIM


def head_norm(values, gains):
    first = low_half(values.shape)
    squares = values * values
    head0 = jnp.sum(jnp.where(first, squares, 0.0), -1, keepdims=True)
    head1 = jnp.sum(jnp.where(first, 0.0, squares), -1, keepdims=True)
    scale = jnp.where(
        first,
        lax.rsqrt(head0 * (1.0 / HEAD_DIM) + EPSILON),
        lax.rsqrt(head1 * (1.0 / HEAD_DIM) + EPSILON),
    )
    return values * scale * gains


def pack_kernel(rows_ref, line_ref, out_ref, held, wide):
    wide[...] = jnp.full(wide.shape, -1, jnp.int32)
    wide[0:1, 0:POOL] = line_ref[...]
    line = wide[0:1, :]
    first = lax.broadcasted_iota(jnp.int32, (POOL, 256), 0)
    second = lax.broadcasted_iota(jnp.int32, (POOL, 256), 1)
    column = jnp.sum(jnp.where(first == second, line, 0), 1, keepdims=True)
    rank = jnp.sum(jnp.where((column == line) & (first < second), 1, 0), 0, keepdims=True)
    held[...] = jnp.zeros_like(held)
    held[POOL : POOL + 1, :] = (line * CAP + rank).astype(F32)
    for block in range(16):
        held[0:POOL, :] = rows_ref[:, block * 256 : (block + 1) * 256].astype(F32)
        out_ref[block] = held[...].astype(BF16)


def embed_kernel(places_ref, arrived_ref, weight_ref, out0, out1, out2, out3, label_ref, held):
    for far, out in enumerate((out0, out1, out2, out3)):
        for near in range(SIDE):
            place = far * SIDE + near
            block = arrived_ref[places_ref[place]].astype(F32)
            held[near * POOL : (near + 1) * POOL, :] = block[0:POOL]
            label_ref[place : place + 1, :] = block[POOL : POOL + 1]
        out[...] = jnp.dot(
            held[...].astype(BF16), weight_ref[...], preferred_element_type=F32
        ).astype(BF16)


def middle_kernel(in0, in1, in2, in3, out0, out1, out2, out3, held):
    held[...] = total_of((in0, in1, in2, in3))
    part = out0.shape[0]
    for place, out in enumerate((out0, out1, out2, out3)):
        out[...] = held[place * part : (place + 1) * part, :].astype(BF16)


def both_middle_kernel(*refs):
    held = refs[12]
    held[...] = total_of(refs[4:8])
    total = total_of(refs[0:4])
    for place, out in enumerate(refs[8:12]):
        out[0:32, :] = total[place * 32 : (place + 1) * 32].astype(BF16)
        out[32 : 32 + POOL, :] = held[place * POOL : (place + 1) * POOL, :].astype(BF16)


def join_kernel(start, in0, in1, in2, in3, out_ref, held):
    part = out_ref.shape[0] // SIDE
    for place, piece in enumerate((in0, in1, in2, in3)):
        held[place * part : (place + 1) * part, :] = piece[start : start + part, :].astype(F32)
    out_ref[...] = held[...].astype(BF16)


def repeat_mod_kernel(mod_ref, out_ref):
    out_ref[...] = jnp.zeros_like(out_ref)
    for own in range(2):
        for place in range(6):
            line = mod_ref[own, place, 1:2, :]
            for group in range(8):
                out_ref[group, own, place : place + 1, :] = line


def row_mod_kernel(index_ref, mod_ref, out_ref):
    for row in range(POOL):
        values = mod_ref[index_ref[row]]
        for place in range(6):
            out_ref[place, row : row + 1, :] = values[place : place + 1]


def total_of(parts):
    return functools.reduce(jnp.add, [part[...].astype(F32) for part in parts])


def embed_norm_kernel(in0, in1, in2, in3, mod_ref, embedded_ref, out_ref):
    embedded = total_of((in0, in1, in2, in3)).astype(BF16)
    embedded_ref[...] = embedded
    out_ref[...] = (normed(embedded.astype(F32)) * (1.0 + mod_ref[1]) + mod_ref[0]).astype(BF16)


def both_norm_kernel(
    image_ref, embedded_ref, in0, in1, in2, in3, img_mod_ref, txt_mod_ref,
    img_ref, txt_ref, out_ref,
):
    projected = total_of((in0, in1, in2, in3))
    gate, shift, scale = img_mod_ref[2:3, :], img_mod_ref[3:4, :], img_mod_ref[4:5, :]
    mixed = (image_ref[...].astype(F32) + gate * projected[0:32]).astype(BF16)
    img_ref[...] = mixed
    out_ref[0:32, :] = (normed(mixed.astype(F32)) * (1.0 + scale) + shift).astype(BF16)
    mixed = (embedded_ref[...].astype(F32) + txt_mod_ref[2] * projected[32:]).astype(BF16)
    txt_ref[...] = mixed
    hidden = normed(mixed.astype(F32)) * (1.0 + txt_mod_ref[4]) + txt_mod_ref[3]
    out_ref[32 : 32 + POOL, :] = hidden.astype(BF16)


def one_hot(slot_ref, count):
    line = slot_ref[...]
    shape = (count, line.shape[1])
    return jnp.where(lax.broadcasted_iota(jnp.int32, shape, 0) == line, 1.0, 0.0)


def with_keep(values, keep):
    first = low_half(values.shape)
    return jnp.where(first, values, keep), jnp.where(first, keep, values)


def project(rows, weight_ref):
    both = jnp.concatenate([weight_ref[0], weight_ref[1]], -1)
    first = jnp.dot(rows, both, preferred_element_type=F32)
    return first, jnp.dot(rows, weight_ref[2], preferred_element_type=F32)


def txt_qkv_kernel(in0, in1, in2, in3, weight_ref, gain_ref, slot_ref, out_ref, held, rows_ref):
    part = in0.shape[0]
    for place, piece in enumerate((in0, in1, in2, in3)):
        rows_ref[place * part : (place + 1) * part, :] = piece[...]
    projected, values = project(rows_ref[...], weight_ref)
    held[:, 0:128] = head_norm(projected[:, 0:128], gain_ref[0:1, :]).astype(BF16)
    held[:, 128:256] = head_norm(projected[:, 128:256], gain_ref[1:2, :]).astype(BF16)
    held[:, 256:384] = values.astype(BF16)
    hot = one_hot(slot_ref, 512)
    keep = jnp.sum(hot, -1, keepdims=True)
    slots = jnp.dot(hot.astype(BF16), held[...], preferred_element_type=F32)
    val0, val1 = with_keep(slots[:, 256:384], keep)
    out_ref[:, 0:256] = slots[:, 0:256].astype(BF16)
    out_ref[:, 256:384] = val0.astype(BF16)
    out_ref[:, 384:512] = val1.astype(BF16)


def img_project_kernel(image_ref, mod_ref, weight_ref, _, out_ref, projected_ref):
    rows = image_ref[...].astype(F32)
    modded = (normed(rows) * (1.0 + mod_ref[0, 1, 0:1, :]) + mod_ref[0, 0, 0:1, :]).astype(BF16)
    out_ref[...] = modded
    projected, values = project(modded, weight_ref)
    projected_ref[:, 0:256] = projected
    projected_ref[:, 256:384] = values


def low_part_kernel(adapter_ref, tp_ref, mod_ref, down_ref, _, out_ref, wide):
    depth = down_ref.shape[1]
    wide[...] = jnp.zeros_like(wide)
    start = pl.multiple_of(tp_ref[0] * depth, 8)
    wide[pl.ds(start, depth), :] = down_ref[0].astype(F32)
    low = jnp.dot(mod_ref[...], wide[...].astype(BF16), preferred_element_type=F32)
    for block in range(8):
        out_ref[block] = low[block * 32 : (block + 1) * 32].astype(BF16)


def low_sum_kernel(part_ref, out_ref):
    total = part_ref[0].astype(F32)
    for block in range(1, 16):
        total = total + part_ref[block].astype(F32)
    for block in range(16):
        out_ref[block] = total.astype(BF16)


def img_adapt_kernel(adapter_ref, low_ref, projected_ref, up_ref, gain_ref, out_ref, lift):
    lift[...] = jnp.zeros_like(lift)
    for part in range(3):
        lift[part * 64 : (part + 1) * 64, part * 128 : (part + 1) * 128] = up_ref[0, part]
    projected = projected_ref[...] + ADAPTER_SCALE * jnp.dot(
        low_ref[...], lift[...], preferred_element_type=F32
    )
    out_ref[:, 0:128] = head_norm(projected[:, 0:128], gain_ref[0:1, :]).astype(BF16)
    out_ref[:, 128:256] = head_norm(projected[:, 128:256], gain_ref[1:2, :]).astype(BF16)
    val0, val1 = with_keep(projected[:, 256:384], 1.0)
    out_ref[:, 256:384] = val0.astype(BF16)
    out_ref[:, 384:512] = val1.astype(BF16)


def attend(queries, tokens):
    scaled = queries.astype(F32) * HEAD_DIM ** (-0.5)
    first = low_half(scaled.shape)
    keys = tokens[:, 128:256]
    results = []
    for head in range(2):
        own = jnp.where(first if head == 0 else ~first, scaled, 0.0).astype(BF16)
        scores = lax.dot_general(
            own, keys, (((1,), (1,)), ((), ())), preferred_element_type=F32
        )
        weights = jnp.exp(scores).astype(BF16)
        summed = jnp.dot(
            weights, tokens[:, 256 + head * 128 : 384 + head * 128], preferred_element_type=F32
        )
        results.append(summed / pltpu.roll(summed, HEAD_DIM, 1))
    return jnp.where(first, results[0], results[1]).astype(BF16)


def img_attend_kernel(
    places_ref, img_ref, slot_ref, weight_ref,
    out0, out1, out2, out3, token_ref, tokens, held, ranked,
):
    for own in range(2):
        tokens[own, 0:256, :] = img_ref[own * 256 : (own + 1) * 256, :]
        for source in range(8):
            start = 256 + source * 32
            tokens[own, start : start + 32, :] = slot_ref[source, own * 32 : (own + 1) * 32, :]
    token_ref[...] = tokens[...]
    for own in range(2):
        held[own * 256 : (own + 1) * 256, :] = attend(tokens[own, 0:256, 0:128], tokens[own])
    for place in range(16):
        start = pl.multiple_of(places_ref[place] * 32, 32)
        ranked[place * 32 : (place + 1) * 32, :] = held[pl.ds(start, 32), :]
    result = jnp.dot(ranked[...], weight_ref[...], preferred_element_type=F32)
    for place, out in enumerate((out0, out1, out2, out3)):
        out[...] = result[place * 128 : (place + 1) * 128].astype(BF16)


def txt_attend_kernel(token_ref, out_ref):
    for own in range(2):
        attended = attend(token_ref[own, 256:512, 0:128], token_ref[own])
        for source in range(8):
            start = source * 32
            out_ref[source, own * 32 : (own + 1) * 32, :] = attended[start : start + 32]


def txt_project_kernel(att_ref, slot_ref, weight_ref, out0, out1, out2, out3):
    hot = one_hot(slot_ref, 512).astype(BF16)
    rows = lax.dot_general(
        hot, att_ref[...], (((0,), (0,)), ((), ())), preferred_element_type=F32
    ).astype(BF16)
    part = out0.shape[0]
    result = jnp.dot(rows, weight_ref[...], preferred_element_type=F32)
    for place, out in enumerate((out0, out1, out2, out3)):
        out[...] = result[place * part : (place + 1) * part].astype(BF16)


def feed_kernel(in0, in1, in2, in3, win_ref, wout_ref, out0, out1, out2, out3, rows_ref):
    part = in0.shape[0]
    for place, piece in enumerate((in0, in1, in2, in3)):
        rows_ref[place * part : (place + 1) * part, :] = piece[...]
    hidden = lax.dot_general(
        rows_ref[...], win_ref[0], (((1,), (1,)), ((), ())), preferred_element_type=F32
    )
    hidden = jax.nn.gelu(hidden, approximate=True).astype(BF16)
    result = jnp.dot(hidden, wout_ref[0], preferred_element_type=F32)
    for place, out in enumerate((out0, out1, out2, out3)):
        out[...] = result[place * part : (place + 1) * part].astype(BF16)


def both_final_kernel(
    img_ref, txt_ref, in0, in1, in2, in3, img_mod_ref, txt_mod_ref, slot_ref, out_ref, placed_ref
):
    total = total_of((in0, in1, in2, in3))
    out_ref[...] = (img_ref[...].astype(F32) + img_mod_ref[5:6, :] * total[0:32]).astype(BF16)
    rows = txt_ref[...].astype(F32) + txt_mod_ref[5] * total[32:]
    hot = one_hot(slot_ref, 32).astype(BF16)
    placed_ref[...] = jnp.dot(hot, rows.astype(BF16), preferred_element_type=F32).astype(BF16)


def middle(parts, after=()):
    rows, width = parts[0].shape
    return run(
        middle_kernel,
        [like((rows // SIDE, width))] * SIDE,
        parts,
        scratch=[pltpu.VMEM((rows, width), F32)],
        after=after,
    )


def both_middle(img_parts, txt_parts):
    rows, width = txt_parts[0].shape
    return run(
        both_middle_kernel,
        [like((32 + POOL, width))] * SIDE,
        (*img_parts, *txt_parts),
        scratch=[pltpu.VMEM((rows, width), F32)],
    )


def join(parts, start, count, after=()):
    width = parts[0].shape[1]
    return run(
        functools.partial(join_kernel, start),
        like((SIDE * count, width)),
        parts,
        scratch=[pltpu.VMEM((SIDE * count, width), F32)],
        after=after,
    )


def feed(parts, weight_in, weight_out, stream):
    rows, width = parts[0].shape
    hidden = weight_in.shape[1]
    plain = pl.BlockSpec((rows, width), lambda i: (0, 0))
    return pl.pallas_call(
        feed_kernel,
        grid=(1,),
        out_shape=[like((rows, width))] * SIDE,
        in_specs=[plain] * SIDE
        + [
            pl.BlockSpec((1, hidden, width), lambda i: (stream, 0, 0)),
            pl.BlockSpec((1, hidden, width), lambda i: (stream, 0, 0)),
        ],
        out_specs=[plain] * SIDE,
        scratch_shapes=[pltpu.VMEM((rows * SIDE, width), BF16)],
        compiler_params=pltpu.CompilerParams(vmem_limit_bytes=32 << 20),
        cost_estimate=pl.CostEstimate(
            flops=rows * SIDE * width * hidden * 4,
            bytes_accessed=width * hidden * 4 + rows * width * 16,
            transcendentals=rows * SIDE * hidden,
        ),
    )(*parts, weight_in, weight_out)


def shards(
    image,
    prompt_encoder_rows,
    prompt_row_request,
    request_adapter,
    modulation,
    query_key_gain,
    prompt_embed_weight,
    image_query_key_value,
    prompt_query_key_value,
    image_out_weight,
    prompt_out_weight,
    feed_in_weight,
    feed_out_weight,
    adapter_down,
    adapter_up,
):
    grp = lax.axis_index("grp")
    tp = lax.axis_index("tp")
    chip, core = grp // 2, grp % 2
    z, y = tp // SIDE, tp % SIDE
    width = image.shape[1]

    steps = jnp.arange(16)
    far, near = steps // SIDE, steps % SIDE
    places = jnp.where(
        core == 0,
        ((z + far) % SIDE) * SIDE + (y + near) % SIDE,
        ((z + near) % SIDE) * SIDE + (y + far) % SIDE,
    ).astype(jnp.int32)
    gains = jnp.concatenate([query_key_gain, query_key_gain], -1)

    request = prompt_row_request[:, 0]
    outgoing = run(
        pack_kernel,
        like((16, 32, 256)),
        (prompt_encoder_rows, prompt_row_request.reshape(1, POOL)),
        scratch=[pltpu.VMEM((32, 256), F32), pltpu.VMEM((8, 256), jnp.int32)],
    )
    arrived = lax.all_to_all(outgoing, "tp", 0, 0, tiled=True)
    blocks = 4
    block = image.shape[0] // blocks
    img_mod, img_projected = pl.pallas_call(
        img_project_kernel,
        grid=(blocks,),
        out_shape=[like(image.shape), like((image.shape[0], 384), F32)],
        in_specs=[
            pl.BlockSpec((block, width), lambda i: (i, 0)),
            pl.BlockSpec((1, 6, 2, width), lambda i: (i // 2, 0, 0, 0)),
            pl.BlockSpec((3, width, 128), lambda i: (0, 0, 0)),
            pl.BlockSpec(memory_space=pl.ANY),
        ],
        out_specs=[
            pl.BlockSpec((block, width), lambda i: (i, 0)),
            pl.BlockSpec((block, 384), lambda i: (i, 0)),
        ],
        compiler_params=pltpu.CompilerParams(vmem_limit_bytes=24 << 20),
        cost_estimate=pl.CostEstimate(
            flops=512 * width * 384 * 2, bytes_accessed=7 << 20, transcendentals=0
        ),
    )(
        image,
        modulation.transpose(0, 2, 1, 3),
        image_query_key_value.transpose(1, 0, 2),
        outgoing,
    )
    *embed_parts, labels = run(
        embed_kernel,
        [like((SIDE * POOL, width))] * SIDE + [like((16, 256), F32)],
        (places, arrived, prompt_embed_weight),
        smem=1,
        scratch=[pltpu.VMEM((SIDE * POOL, 256), F32)],
        flops=320 * 256 * width * 2,
        after=(img_projected,),
    )
    half = image.shape[0] // 2
    low_part = pl.pallas_call(
        low_part_kernel,
        grid_spec=pltpu.PrefetchScalarGridSpec(
            num_scalar_prefetch=2,
            grid=(2,),
            in_specs=[
                pl.BlockSpec((half, width), lambda i, *_: (i, 0)),
                pl.BlockSpec((1, *adapter_down.shape[1:]), lambda i, ids, _: (ids[i], 0, 0)),
                pl.BlockSpec(memory_space=pl.ANY),
            ],
            out_specs=pl.BlockSpec((8, 32, 192), lambda i, *_: (i, 0, 0)),
            scratch_shapes=[pltpu.VMEM((width, 192), F32)],
        ),
        out_shape=like((16, 32, 192)),
        compiler_params=pltpu.CompilerParams(vmem_limit_bytes=24 << 20),
        cost_estimate=pl.CostEstimate(
            flops=512 * width * 192 * 2, bytes_accessed=3 << 20, transcendentals=0
        ),
    )(request_adapter, tp.reshape(1).astype(jnp.int32), img_mod, adapter_down, embed_parts[0])
    low_sum = run(
        low_sum_kernel,
        like((16, 32, 192)),
        (lax.all_to_all(low_part, "tp", 0, 0, tiled=True),),
    )
    low = lax.all_to_all(low_sum, "tp", 0, 0, tiled=True).reshape(2 * half, 192)

    mod_all = run(
        repeat_mod_kernel, like((8, 2, 8, width), F32), (modulation.transpose(0, 2, 1, 3),),
        after=(embed_parts[0],),
    )
    mod_all = lax.all_to_all(mod_all, "grp", 0, 0, tiled=True).reshape(16, 8, width)
    row_mod = run(row_mod_kernel, like((6, POOL, width), F32), (request, mod_all), smem=1)

    embed_sums = exchange(middle(exchange(embed_parts, 1), after=(low_part,)), 0)
    embedded, txt_mod = run(
        embed_norm_kernel,
        [like((POOL, width))] * 2,
        (*embed_sums, row_mod),
        after=(low_sum,),
    )
    txt_mods = spread(join(spread(txt_mod, 0), 0, POOL, after=(low,)), 1)

    target = labels[:, :POOL].astype(jnp.int32)
    slots_all = target // 4 * 64 + target // 2 % 2 * 32 + target % 2
    slots_all = (slots_all + 2 * steps[:, None]).reshape(1, 16 * POOL).astype(jnp.int32)
    earlier = (request[:, None] == request[None, :]) & (
        jnp.arange(POOL)[None, :] < jnp.arange(POOL)[:, None]
    )
    ranked = jnp.sum(earlier.astype(jnp.int32), 1)
    slots_own = (request * CAP + ranked).reshape(1, POOL).astype(jnp.int32)

    img_parts = pl.pallas_call(
        img_adapt_kernel,
        grid_spec=pltpu.PrefetchScalarGridSpec(
            num_scalar_prefetch=1,
            grid=(2,),
            in_specs=[
                pl.BlockSpec((half, 192), lambda i, _: (i, 0)),
                pl.BlockSpec((half, 384), lambda i, _: (i, 0)),
                pl.BlockSpec((1, 3, 64, 128), lambda i, ids: (ids[i], 0, 0, 0)),
                pl.BlockSpec((2, 128), lambda i, _: (0, 0)),
            ],
            out_specs=pl.BlockSpec((half, 512), lambda i, _: (i, 0)),
            scratch_shapes=[pltpu.VMEM((192, 384), BF16)],
        ),
        out_shape=like((image.shape[0], 512)),
        cost_estimate=pl.CostEstimate(
            flops=512 * 384 * 192 * 2, bytes_accessed=2 << 20, transcendentals=0
        ),
    )(request_adapter, low, img_projected, adapter_up, gains[0])

    slot_parts = run(
        txt_qkv_kernel,
        like((512, 512)),
        (*txt_mods, prompt_query_key_value.transpose(1, 0, 2), gains[1], slots_all),
        scratch=[pltpu.VMEM((16 * POOL, 384), BF16), pltpu.VMEM((16 * POOL, width), BF16)],
        flops=320 * width * 384 * 2,
        after=(img_parts,),
    )
    slot_parts = lax.all_to_all(slot_parts.reshape(8, 64, 512), "grp", 0, 0, tiled=True)

    *img_terms, tokens = run(
        img_attend_kernel,
        [like((128, width))] * SIDE + [like((2, 512, 512))],
        (places, img_parts, slot_parts, image_out_weight),
        smem=1,
        scratch=[
            pltpu.VMEM((2, 512, 512), BF16),
            pltpu.VMEM((512, 128), BF16),
            pltpu.VMEM((512, 128), BF16),
        ],
        flops=1 << 30,
    )
    img_sums = exchange(img_terms, 1)
    att_parts = run(txt_attend_kernel, like((8, 64, 128)), (tokens,), flops=1 << 29)
    att_parts = lax.all_to_all(att_parts, "grp", 0, 0, tiled=True).reshape(512, 128)
    txt_terms = run(
        txt_project_kernel,
        [like((SIDE * POOL, width))] * SIDE,
        (att_parts, slots_all, prompt_out_weight),
        flops=320 * 128 * width * 2,
        after=(img_sums[1],),
    )
    txt_sums = exchange(txt_terms, 1)

    own_mod = lax.dynamic_index_in_dim(modulation[:, 0], tp // 8, 0, keepdims=False)
    own_image = lax.dynamic_slice_in_dim(image, tp * 32, 32, 0)
    sums = exchange(both_middle(img_sums, txt_sums), 0)
    mixed_img, mixed_txt, norm_rows = run(
        both_norm_kernel,
        [like((32, width)), like((POOL, width)), like((32 + POOL, width))],
        (own_image, embedded, *sums, own_mod, row_mod),
    )
    near_rows = spread(norm_rows, 0)
    txt_rows = spread(join(near_rows, 32, POOL), 1)
    img_rows = spread(join(near_rows, 0, 32, after=(txt_rows[1],)), 1)
    weight_in = feed_in_weight.transpose(0, 2, 1)
    img_terms = feed(img_rows, weight_in, feed_out_weight, 0)
    txt_terms = feed(txt_rows, weight_in, feed_out_weight, 1)
    sums = exchange(both_middle(exchange(img_terms, 1), exchange(txt_terms, 1)), 0)
    image_out, placed = run(
        both_final_kernel,
        [like((32, width))] * 2,
        (mixed_img, mixed_txt, *sums, own_mod, row_mod, slots_own),
    )

    placed = lax.all_to_all(placed.reshape(8, 4, width), "grp", 0, 0, tiled=True)
    prompt_out = placed.reshape(32, width)

    return (image_out, prompt_out)


def solution(mesh):
    placed = (
        P("grp", None),
        P(("grp", "tp"), None),
        P(("grp", "tp"), None),
        P("grp"),
        P("grp", None, None, None),
        P(),
        P("tp", None),
        P(None, None, "tp"),
        P(None, None, "tp"),
        P("tp", None),
        P("tp", None),
        P(None, None, "tp"),
        P(None, "tp", None),
        P(None, "tp", None),
        P(None, None, None, "tp"),
    )
    return jax.shard_map(
        shards,
        mesh=mesh,
        in_specs=placed,
        out_specs=(P(("grp", "tp"), None), P(("grp", "tp"), None)),
        check_vma=False,
    )
```

```python
import functools

import jax
import jax.numpy as jnp
from jax import lax
from jax.experimental import pallas as pl
from jax.experimental.pallas import tpu as pltpu
from jax.sharding import PartitionSpec as P

HEAD_DIM = 64
CAP = 2
EPSILON = 1e-06
ADAPTER_SCALE = 0.5
SIDE = 4
POOL = 20
WIDTH = 2432
EXTRA = 512
F32 = jnp.float32
BF16 = jnp.bfloat16


def torus_shift(values, stage, step):
    pairs = []
    for grp in range(8):
        for tp in range(16):
            z, y = divmod(tp, SIDE)
            if (grp + stage) % 2 == 0:
                y = (y + step) % SIDE
            else:
                z = (z + step) % SIDE
            pairs.append((grp * 16 + tp, grp * 16 + z * SIDE + y))
    return lax.ppermute(values, ("grp", "tp"), pairs)


def spread(rows, stage):
    return [
        rows,
        torus_shift(rows, stage, -1),
        torus_shift(rows, stage, 2),
        torus_shift(rows, stage, 1),
    ]


def exchange(parts, stage):
    return [
        parts[0],
        torus_shift(parts[3], stage, -1),
        torus_shift(parts[2], stage, 2),
        torus_shift(parts[1], stage, 1),
    ]


def run(kernel, outs, args, smem=0, scratch=(), flops=0, limit=16, after=()):
    specs = [pl.BlockSpec(memory_space=pltpu.SMEM)] * smem
    specs += [pl.BlockSpec(memory_space=pltpu.VMEM)] * (len(args) - smem)
    specs += [pl.BlockSpec(memory_space=pl.ANY)] * len(after)
    count = len(args)
    single = not isinstance(outs, list)
    shapes = [outs] if single else outs
    moved = sum(a.size * a.dtype.itemsize for a in args)
    moved += sum(s.size * s.dtype.itemsize for s in shapes)

    def body(*refs):
        kernel(*refs[:count], *refs[count + len(after) :])

    result = pl.pallas_call(
        body,
        out_shape=shapes,
        in_specs=specs,
        out_specs=[pl.BlockSpec(memory_space=pltpu.VMEM)] * len(shapes),
        scratch_shapes=list(scratch),
        compiler_params=pltpu.CompilerParams(vmem_limit_bytes=limit << 20),
        cost_estimate=pl.CostEstimate(flops=flops, bytes_accessed=moved, transcendentals=0),
    )(*args, *after)
    return result[0] if single else result


def like(shape, dtype=BF16):
    return jax.ShapeDtypeStruct(shape, dtype)


def normed(values):
    centred = values - jnp.mean(values, -1, keepdims=True)
    return centred * lax.rsqrt(jnp.mean(centred * centred, -1, keepdims=True) + EPSILON)


def low_half(shape):
    return lax.broadcasted_iota(jnp.int32, shape, len(shape) - 1) < HEAD_DIM


def head_norm(values, gains):
    first = low_half(values.shape)
    squares = values * values
    head0 = jnp.sum(jnp.where(first, squares, 0.0), -1, keepdims=True)
    head1 = jnp.sum(jnp.where(first, 0.0, squares), -1, keepdims=True)
    scale = jnp.where(
        first,
        lax.rsqrt(head0 * (1.0 / HEAD_DIM) + EPSILON),
        lax.rsqrt(head1 * (1.0 / HEAD_DIM) + EPSILON),
    )
    return values * scale * gains


def pack_kernel(rows_ref, line_ref, out_ref, held, wide):
    wide[...] = jnp.full(wide.shape, -1, jnp.int32)
    wide[0:1, 0:POOL] = line_ref[...]
    line = wide[0:1, :]
    first = lax.broadcasted_iota(jnp.int32, (POOL, 256), 0)
    second = lax.broadcasted_iota(jnp.int32, (POOL, 256), 1)
    column = jnp.sum(jnp.where(first == second, line, 0), 1, keepdims=True)
    rank = jnp.sum(jnp.where((column == line) & (first < second), 1, 0), 0, keepdims=True)
    held[...] = jnp.zeros_like(held)
    held[POOL : POOL + 1, :] = (line * CAP + rank).astype(F32)
    for block in range(16):
        held[0:POOL, :] = rows_ref[:, block * 256 : (block + 1) * 256].astype(F32)
        out_ref[block] = held[...].astype(BF16)


def embed_kernel(
    places_ref, arrived_ref, weight_ref, low_ref, out0, out1, out2, out3, label_ref, held
):
    for far, out in enumerate((out0, out1, out2, out3)):
        for near in range(SIDE):
            place = far * SIDE + near
            block = arrived_ref[places_ref[place]].astype(F32)
            held[near * POOL : (near + 1) * POOL, :] = block[0:POOL]
            label_ref[place : place + 1, :] = block[POOL : POOL + 1]
        out[:, 0:WIDTH] = jnp.dot(
            held[...].astype(BF16), weight_ref[...], preferred_element_type=F32
        ).astype(BF16)
        out[:, WIDTH:] = jnp.zeros((SIDE * POOL, EXTRA), BF16)
        for near in range(SIDE):
            left = WIDTH + near // 2 * 256
            top = near % 2 * 32
            out[top : top + 32, left : left + 192] = low_ref[places_ref[far * SIDE + near]]


def middle_kernel(in0, in1, in2, in3, out0, out1, out2, out3, held):
    held[...] = total_of((in0, in1, in2, in3))
    for near, out in enumerate((out0, out1, out2, out3)):
        out[:, 0:WIDTH] = held[near * POOL : (near + 1) * POOL, 0:WIDTH].astype(BF16)
        left = WIDTH + near // 2 * 256
        for half in range(2):
            top = near % 2 * 32 + half * 16
            out[0:16, WIDTH + half * 256 : WIDTH + half * 256 + 256] = held[
                top : top + 16, left : left + 256
            ].astype(BF16)
        out[16:POOL, WIDTH:] = jnp.zeros((POOL - 16, EXTRA), BF16)


def both_middle_kernel(*refs):
    inputs, outs = refs[0:8], refs[8:12]
    img, txt, held, sems = refs[12:16]
    copies = []
    for place in range(8):
        target = img.at[place] if place < SIDE else txt.at[place - SIDE]
        copies.append(pltpu.make_async_copy(inputs[place], target, sems.at[place]))
    for copy in copies:
        copy.start()
    for copy in copies[0:SIDE]:
        copy.wait()
    for near, out in enumerate(outs):
        rows = slice(near * 32, (near + 1) * 32)
        total = img[0, rows, :].astype(F32) + img[1, rows, :].astype(F32)
        total = total + (img[2, rows, :].astype(F32) + img[3, rows, :].astype(F32))
        out[0:32, :] = total.astype(BF16)
    for copy in copies[SIDE:]:
        copy.wait()
    total = txt[0].astype(F32) + txt[1].astype(F32)
    held[...] = total + (txt[2].astype(F32) + txt[3].astype(F32))
    for near, out in enumerate(outs):
        out[32 : 32 + POOL, :] = held[near * POOL : (near + 1) * POOL, :].astype(BF16)


def join_kernel(in0, in1, in2, in3, out_ref, held):
    for place, piece in enumerate((in0, in1, in2, in3)):
        held[place * POOL : (place + 1) * POOL, :] = piece[...].astype(F32)
    out_ref[...] = held[...].astype(BF16)


def both_join_kernel(in0, in1, in2, in3, out_ref, held):
    for place, piece in enumerate((in0, in1, in2, in3)):
        out_ref[place * 32 : (place + 1) * 32, :] = piece[0:32, :]
        held[place * POOL : (place + 1) * POOL, :] = piece[32:, :].astype(F32)
    out_ref[128:, :] = held[...].astype(BF16)


def repeat_mod_kernel(mod_ref, out_ref):
    out_ref[...] = jnp.zeros_like(out_ref)
    for own in range(2):
        for place in range(6):
            line = mod_ref[own, place, 1:2, :]
            for group in range(8):
                out_ref[group, own, place : place + 1, :] = line


def row_mod_kernel(index_ref, mod_ref, out_ref):
    for row in range(POOL):
        values = mod_ref[index_ref[row]]
        for place in range(6):
            out_ref[place, row : row + 1, :] = values[place : place + 1]


def total_of(parts):
    return functools.reduce(jnp.add, [part[...].astype(F32) for part in parts])


def embed_norm_kernel(in0, in1, in2, in3, mod_ref, embedded_ref, out_ref):
    total = total_of((in0, in1, in2, in3))
    embedded = total[:, 0:WIDTH].astype(BF16)
    embedded_ref[...] = embedded
    modded = normed(embedded.astype(F32)) * (1.0 + mod_ref[1]) + mod_ref[0]
    out_ref[:, 0:WIDTH] = modded.astype(BF16)
    out_ref[:, WIDTH:] = total[:, WIDTH:].astype(BF16)


def both_norm_kernel(
    image_ref, embedded_ref, in0, in1, in2, in3, img_mod_ref, txt_mod_ref,
    img_ref, txt_ref, out_ref,
):
    projected = total_of((in0, in1, in2, in3))
    gate, shift, scale = img_mod_ref[2:3, :], img_mod_ref[3:4, :], img_mod_ref[4:5, :]
    mixed = (image_ref[...].astype(F32) + gate * projected[0:32]).astype(BF16)
    img_ref[...] = mixed
    out_ref[0:32, :] = (normed(mixed.astype(F32)) * (1.0 + scale) + shift).astype(BF16)
    mixed = (embedded_ref[...].astype(F32) + txt_mod_ref[2] * projected[32:]).astype(BF16)
    txt_ref[...] = mixed
    hidden = normed(mixed.astype(F32)) * (1.0 + txt_mod_ref[4]) + txt_mod_ref[3]
    out_ref[32 : 32 + POOL, :] = hidden.astype(BF16)


def one_hot(slot_ref, count):
    line = slot_ref[...]
    shape = (count, line.shape[1])
    return jnp.where(lax.broadcasted_iota(jnp.int32, shape, 0) == line, 1.0, 0.0)


def with_keep(values, keep):
    first = low_half(values.shape)
    return jnp.where(first, values, keep), jnp.where(first, keep, values)


def project(rows, weight_ref):
    both = jnp.concatenate([weight_ref[0], weight_ref[1]], -1)
    first = jnp.dot(rows, both, preferred_element_type=F32)
    return first, jnp.dot(rows, weight_ref[2], preferred_element_type=F32)


def txt_qkv_kernel(in0, in1, in2, in3, weight_ref, gain_ref, slot_ref, out_ref, held, rows_ref):
    part = in0.shape[0]
    for place, piece in enumerate((in0, in1, in2, in3)):
        rows_ref[place * part : (place + 1) * part, :] = piece[:, 0:WIDTH]
    projected, values = project(rows_ref[...], weight_ref)
    held[:, 0:128] = head_norm(projected[:, 0:128], gain_ref[0:1, :]).astype(BF16)
    held[:, 128:256] = head_norm(projected[:, 128:256], gain_ref[1:2, :]).astype(BF16)
    held[:, 256:384] = values.astype(BF16)
    hot = one_hot(slot_ref, 512)
    keep = jnp.sum(hot, -1, keepdims=True)
    slots = jnp.dot(hot.astype(BF16), held[...], preferred_element_type=F32)
    val0, val1 = with_keep(slots[:, 256:384], keep)
    out_ref[:, 0:256] = slots[:, 0:256].astype(BF16)
    out_ref[:, 256:384] = val0.astype(BF16)
    out_ref[:, 384:512] = val1.astype(BF16)


def img_project_kernel(image_ref, mod_ref, weight_ref, _, out_ref, projected_ref):
    rows = image_ref[...].astype(F32)
    modded = (normed(rows) * (1.0 + mod_ref[0, 1, 0:1, :]) + mod_ref[0, 0, 0:1, :]).astype(BF16)
    out_ref[...] = modded
    projected, values = project(modded, weight_ref)
    projected_ref[:, 0:256] = projected
    projected_ref[:, 256:384] = values


def low_part_kernel(adapter_ref, tp_ref, mod_ref, down_ref, out_ref, wide):
    depth = down_ref.shape[1]
    wide[...] = jnp.zeros_like(wide)
    start = pl.multiple_of(tp_ref[0] * depth, 8)
    wide[pl.ds(start, depth), :] = down_ref[0].astype(F32)
    low = jnp.dot(mod_ref[...], wide[...].astype(BF16), preferred_element_type=F32)
    for block in range(8):
        out_ref[block] = low[block * 32 : (block + 1) * 32].astype(BF16)


def img_adapt_kernel(
    places_ref, in0, in1, in2, in3, projected_ref, up0_ref, up1_ref, gain_ref,
    out_ref, low, lift,
):
    for far, piece in enumerate((in0, in1, in2, in3)):
        wide = piece[:, WIDTH:].astype(F32)
        for near in range(SIDE):
            rows = wide[near * POOL : near * POOL + 16]
            start = pl.multiple_of(places_ref[far * SIDE + near] * 32, 32)
            low[pl.ds(start, 16), :] = rows[:, 0:192]
            low[pl.ds(start + 16, 16), :] = rows[:, 256:448]
    for own, up_ref in enumerate((up0_ref, up1_ref)):
        lift[...] = jnp.zeros_like(lift)
        for part in range(3):
            lift[part * 64 : (part + 1) * 64, part * 128 : (part + 1) * 128] = up_ref[0, part]
        rows = slice(own * 256, (own + 1) * 256)
        projected = projected_ref[rows, :] + ADAPTER_SCALE * jnp.dot(
            low[rows, :].astype(BF16), lift[...], preferred_element_type=F32
        )
        out_ref[rows, 0:128] = head_norm(projected[:, 0:128], gain_ref[0:1, :]).astype(BF16)
        out_ref[rows, 128:256] = head_norm(projected[:, 128:256], gain_ref[1:2, :]).astype(BF16)
        val0, val1 = with_keep(projected[:, 256:384], 1.0)
        out_ref[rows, 256:384] = val0.astype(BF16)
        out_ref[rows, 384:512] = val1.astype(BF16)


def attend(queries, tokens):
    scaled = queries.astype(F32) * HEAD_DIM ** (-0.5)
    first = low_half(scaled.shape)
    keys = tokens[:, 128:256]
    results = []
    for head in range(2):
        own = jnp.where(first if head == 0 else ~first, scaled, 0.0).astype(BF16)
        scores = lax.dot_general(
            own, keys, (((1,), (1,)), ((), ())), preferred_element_type=F32
        )
        weights = jnp.exp(scores).astype(BF16)
        summed = jnp.dot(
            weights, tokens[:, 256 + head * 128 : 384 + head * 128], preferred_element_type=F32
        )
        results.append(summed / pltpu.roll(summed, HEAD_DIM, 1))
    return jnp.where(first, results[0], results[1]).astype(BF16)


def img_attend_kernel(
    places_ref, img_ref, slot_ref, weight_ref,
    out0, out1, out2, out3, token_ref, tokens, held, ranked,
):
    for own in range(2):
        tokens[own, 0:256, :] = img_ref[own * 256 : (own + 1) * 256, :]
        for source in range(8):
            start = 256 + source * 32
            tokens[own, start : start + 32, :] = slot_ref[source, own * 32 : (own + 1) * 32, :]
    token_ref[...] = tokens[...]
    for own in range(2):
        held[own * 256 : (own + 1) * 256, :] = attend(tokens[own, 0:256, 0:128], tokens[own])
    for place in range(16):
        start = pl.multiple_of(places_ref[place] * 32, 32)
        ranked[place * 32 : (place + 1) * 32, :] = held[pl.ds(start, 32), :]
    result = jnp.dot(ranked[...], weight_ref[...], preferred_element_type=F32)
    for place, out in enumerate((out0, out1, out2, out3)):
        out[...] = result[place * 128 : (place + 1) * 128].astype(BF16)


def txt_attend_kernel(token_ref, out_ref):
    for own in range(2):
        attended = attend(token_ref[own, 256:512, 0:128], token_ref[own])
        for source in range(8):
            start = source * 32
            out_ref[source, own * 32 : (own + 1) * 32, :] = attended[start : start + 32]


def txt_project_kernel(att_ref, slot_ref, weight_ref, out0, out1, out2, out3):
    hot = one_hot(slot_ref, 512).astype(BF16)
    rows = lax.dot_general(
        hot, att_ref[...], (((0,), (0,)), ((), ())), preferred_element_type=F32
    ).astype(BF16)
    part = out0.shape[0]
    result = jnp.dot(rows, weight_ref[...], preferred_element_type=F32)
    for place, out in enumerate((out0, out1, out2, out3)):
        out[...] = result[place * part : (place + 1) * part].astype(BF16)


def feed_kernel(
    start, in0, in1, in2, in3, win_ref, wout_ref, _, out0, out1, out2, out3, rows_ref
):
    part = out0.shape[0]
    for place, piece in enumerate((in0, in1, in2, in3)):
        rows_ref[place * part : (place + 1) * part, :] = piece[start : start + part, :]
    hidden = lax.dot_general(
        rows_ref[...], win_ref[0], (((1,), (1,)), ((), ())), preferred_element_type=F32
    )
    hidden = jax.nn.gelu(hidden, approximate=True).astype(BF16)
    result = jnp.dot(hidden, wout_ref[0], preferred_element_type=F32)
    for place, out in enumerate((out0, out1, out2, out3)):
        out[...] = result[place * part : (place + 1) * part].astype(BF16)


def both_final_kernel(
    img_ref, txt_ref, in0, in1, in2, in3, img_mod_ref, txt_mod_ref, slot_ref, out_ref, placed_ref
):
    total = total_of((in0, in1, in2, in3))
    out_ref[...] = (img_ref[...].astype(F32) + img_mod_ref[5:6, :] * total[0:32]).astype(BF16)
    rows = txt_ref[...].astype(F32) + txt_mod_ref[5] * total[32:]
    hot = one_hot(slot_ref, 32).astype(BF16)
    placed_ref[...] = jnp.dot(hot, rows.astype(BF16), preferred_element_type=F32).astype(BF16)


def middle(parts):
    rows, width = parts[0].shape
    return run(
        middle_kernel,
        [like((rows // SIDE, width))] * SIDE,
        parts,
        scratch=[pltpu.VMEM((rows, width), F32)],
    )


def both_middle(img_parts, txt_parts):
    parts = (*img_parts, *txt_parts)
    rows, width = txt_parts[0].shape
    return pl.pallas_call(
        both_middle_kernel,
        out_shape=[like((32 + POOL, width))] * SIDE,
        in_specs=[pl.BlockSpec(memory_space=pl.ANY)] * len(parts),
        out_specs=[pl.BlockSpec(memory_space=pltpu.VMEM)] * SIDE,
        scratch_shapes=[
            pltpu.VMEM((SIDE, *img_parts[0].shape), BF16),
            pltpu.VMEM((SIDE, rows, width), BF16),
            pltpu.VMEM((rows, width), F32),
            pltpu.SemaphoreType.DMA((8,)),
        ],
        compiler_params=pltpu.CompilerParams(vmem_limit_bytes=16 << 20),
        cost_estimate=pl.CostEstimate(flops=0, bytes_accessed=6 << 20, transcendentals=0),
    )(*parts)


def join(kernel, parts):
    width = parts[0].shape[1]
    return run(
        kernel,
        like((SIDE * parts[0].shape[0], width)),
        parts,
        scratch=[pltpu.VMEM((SIDE * POOL, width), F32)],
    )


def feed(parts, start, rows, weight_in, weight_out, stream, after):
    count, width = parts[0].shape
    hidden = weight_in.shape[1]
    return pl.pallas_call(
        functools.partial(feed_kernel, start),
        grid=(1,),
        out_shape=[like((rows, width))] * SIDE,
        in_specs=[pl.BlockSpec((count, width), lambda i: (0, 0))] * SIDE
        + [
            pl.BlockSpec((1, hidden, width), lambda i: (stream, 0, 0)),
            pl.BlockSpec((1, hidden, width), lambda i: (stream, 0, 0)),
            pl.BlockSpec(memory_space=pl.ANY),
        ],
        out_specs=[pl.BlockSpec((rows, width), lambda i: (0, 0))] * SIDE,
        scratch_shapes=[pltpu.VMEM((rows * SIDE, width), BF16)],
        compiler_params=pltpu.CompilerParams(vmem_limit_bytes=36 << 20),
        cost_estimate=pl.CostEstimate(
            flops=rows * SIDE * width * hidden * 4,
            bytes_accessed=width * hidden * 4 + rows * width * 16,
            transcendentals=rows * SIDE * hidden,
        ),
    )(*parts, weight_in, weight_out, after)


def shards(
    image,
    prompt_encoder_rows,
    prompt_row_request,
    request_adapter,
    modulation,
    query_key_gain,
    prompt_embed_weight,
    image_query_key_value,
    prompt_query_key_value,
    image_out_weight,
    prompt_out_weight,
    feed_in_weight,
    feed_out_weight,
    adapter_down,
    adapter_up,
):
    grp = lax.axis_index("grp")
    tp = lax.axis_index("tp")
    chip, core = grp // 2, grp % 2
    z, y = tp // SIDE, tp % SIDE
    width = image.shape[1]

    steps = jnp.arange(16)
    far, near = steps // SIDE, steps % SIDE
    places = jnp.where(
        core == 0,
        ((z + far) % SIDE) * SIDE + (y + near) % SIDE,
        ((z + near) % SIDE) * SIDE + (y + far) % SIDE,
    ).astype(jnp.int32)
    gains = jnp.concatenate([query_key_gain, query_key_gain], -1)

    request = prompt_row_request[:, 0]
    outgoing = run(
        pack_kernel,
        like((16, 32, 256)),
        (prompt_encoder_rows, prompt_row_request.reshape(1, POOL)),
        scratch=[pltpu.VMEM((32, 256), F32), pltpu.VMEM((8, 256), jnp.int32)],
    )
    arrived = lax.all_to_all(outgoing, "tp", 0, 0, tiled=True)
    blocks = 4
    block = image.shape[0] // blocks
    img_mod, img_projected = pl.pallas_call(
        img_project_kernel,
        grid=(blocks,),
        out_shape=[like(image.shape), like((image.shape[0], 384), F32)],
        in_specs=[
            pl.BlockSpec((block, width), lambda i: (i, 0)),
            pl.BlockSpec((1, 6, 2, width), lambda i: (i // 2, 0, 0, 0)),
            pl.BlockSpec((3, width, 128), lambda i: (0, 0, 0)),
            pl.BlockSpec(memory_space=pl.ANY),
        ],
        out_specs=[
            pl.BlockSpec((block, width), lambda i: (i, 0)),
            pl.BlockSpec((block, 384), lambda i: (i, 0)),
        ],
        compiler_params=pltpu.CompilerParams(vmem_limit_bytes=24 << 20),
        cost_estimate=pl.CostEstimate(
            flops=512 * width * 384 * 2, bytes_accessed=7 << 20, transcendentals=0
        ),
    )(
        image,
        modulation.transpose(0, 2, 1, 3),
        image_query_key_value.transpose(1, 0, 2),
        outgoing,
    )
    half = image.shape[0] // 2
    low_part = pl.pallas_call(
        low_part_kernel,
        grid_spec=pltpu.PrefetchScalarGridSpec(
            num_scalar_prefetch=2,
            grid=(2,),
            in_specs=[
                pl.BlockSpec((half, width), lambda i, *_: (i, 0)),
                pl.BlockSpec((1, *adapter_down.shape[1:]), lambda i, ids, _: (ids[i], 0, 0)),
            ],
            out_specs=pl.BlockSpec((8, 32, 192), lambda i, *_: (i, 0, 0)),
            scratch_shapes=[pltpu.VMEM((width, 192), F32)],
        ),
        out_shape=like((16, 32, 192)),
        compiler_params=pltpu.CompilerParams(vmem_limit_bytes=24 << 20),
        cost_estimate=pl.CostEstimate(
            flops=512 * width * 192 * 2, bytes_accessed=3 << 20, transcendentals=0
        ),
    )(request_adapter, tp.reshape(1).astype(jnp.int32), img_mod, adapter_down)
    *embed_parts, labels = run(
        embed_kernel,
        [like((SIDE * POOL, width + EXTRA))] * SIDE + [like((16, 256), F32)],
        (places, arrived, prompt_embed_weight, low_part),
        smem=1,
        scratch=[pltpu.VMEM((SIDE * POOL, 256), F32)],
        flops=320 * 256 * width * 2,
    )
    mod_all = run(
        repeat_mod_kernel, like((8, 2, 8, width), F32), (modulation.transpose(0, 2, 1, 3),),
        after=(embed_parts[0],),
    )
    mod_all = lax.all_to_all(mod_all, "grp", 0, 0, tiled=True).reshape(16, 8, width)
    row_mod = run(row_mod_kernel, like((6, POOL, width), F32), (request, mod_all), smem=1)

    embed_sums = exchange(middle(exchange(embed_parts, 1)), 0)
    embedded, txt_mod = run(
        embed_norm_kernel,
        [like((POOL, width)), like((POOL, width + EXTRA))],
        (*embed_sums, row_mod),
    )
    txt_mods = spread(join(join_kernel, spread(txt_mod, 0)), 1)

    target = labels[:, :POOL].astype(jnp.int32)
    slots_all = target // 4 * 64 + target // 2 % 2 * 32 + target % 2
    slots_all = (slots_all + 2 * steps[:, None]).reshape(1, 16 * POOL).astype(jnp.int32)
    earlier = (request[:, None] == request[None, :]) & (
        jnp.arange(POOL)[None, :] < jnp.arange(POOL)[:, None]
    )
    ranked = jnp.sum(earlier.astype(jnp.int32), 1)
    slots_own = (request * CAP + ranked).reshape(1, POOL).astype(jnp.int32)

    up_specs = [
        pl.BlockSpec((1, 3, 64, 128), lambda i, ids, _: (ids[0], 0, 0, 0)),
        pl.BlockSpec((1, 3, 64, 128), lambda i, ids, _: (ids[1], 0, 0, 0)),
    ]
    img_parts = pl.pallas_call(
        lambda ids_ref, *refs: img_adapt_kernel(*refs),
        grid_spec=pltpu.PrefetchScalarGridSpec(
            num_scalar_prefetch=2,
            grid=(1,),
            in_specs=[pl.BlockSpec(txt_mods[0].shape, lambda i, *_: (0, 0))] * SIDE
            + [pl.BlockSpec(img_projected.shape, lambda i, *_: (0, 0))]
            + up_specs
            + [pl.BlockSpec((2, 128), lambda i, *_: (0, 0))],
            out_specs=pl.BlockSpec((2 * half, 512), lambda i, *_: (0, 0)),
            scratch_shapes=[pltpu.VMEM((2 * half, 192), F32), pltpu.VMEM((192, 384), BF16)],
        ),
        out_shape=like((2 * half, 512)),
        compiler_params=pltpu.CompilerParams(vmem_limit_bytes=24 << 20),
        cost_estimate=pl.CostEstimate(
            flops=512 * 384 * 192 * 2, bytes_accessed=4 << 20, transcendentals=0
        ),
    )(request_adapter, places, *txt_mods, img_projected, adapter_up, adapter_up, gains[0])

    slot_parts = run(
        txt_qkv_kernel,
        like((512, 512)),
        (*txt_mods, prompt_query_key_value.transpose(1, 0, 2), gains[1], slots_all),
        scratch=[pltpu.VMEM((16 * POOL, 384), BF16), pltpu.VMEM((16 * POOL, width), BF16)],
        flops=320 * width * 384 * 2,
    )
    slot_parts = lax.all_to_all(slot_parts.reshape(8, 64, 512), "grp", 0, 0, tiled=True)

    *img_terms, tokens = run(
        img_attend_kernel,
        [like((128, width))] * SIDE + [like((2, 512, 512))],
        (places, img_parts, slot_parts, image_out_weight),
        smem=1,
        scratch=[
            pltpu.VMEM((2, 512, 512), BF16),
            pltpu.VMEM((512, 128), BF16),
            pltpu.VMEM((512, 128), BF16),
        ],
        flops=1 << 30,
    )
    img_sums = exchange(img_terms, 1)
    att_parts = run(txt_attend_kernel, like((8, 64, 128)), (tokens,), flops=1 << 29)
    att_parts = lax.all_to_all(att_parts, "grp", 0, 0, tiled=True).reshape(512, 128)
    txt_terms = run(
        txt_project_kernel,
        [like((SIDE * POOL, width))] * SIDE,
        (att_parts, slots_all, prompt_out_weight),
        flops=320 * 128 * width * 2,
        after=(img_sums[1],),
    )
    txt_sums = exchange(txt_terms, 1)

    own_mod = lax.dynamic_index_in_dim(modulation[:, 0], tp // 8, 0, keepdims=False)
    own_image = lax.dynamic_slice_in_dim(image, tp * 32, 32, 0)
    sums = exchange(both_middle(img_sums, txt_sums), 0)
    mixed_img, mixed_txt, norm_rows = run(
        both_norm_kernel,
        [like((32, width)), like((POOL, width)), like((32 + POOL, width))],
        (own_image, embedded, *sums, own_mod, row_mod),
    )
    rows = spread(join(both_join_kernel, spread(norm_rows, 0)), 1)
    weight_in = feed_in_weight.transpose(0, 2, 1)
    img_terms = feed(rows, 0, 128, weight_in, feed_out_weight, 0, rows[1])
    txt_terms = feed(
        rows, 128, SIDE * POOL, weight_in, feed_out_weight, 1, img_terms[0]
    )
    sums = exchange(both_middle(exchange(img_terms, 1), exchange(txt_terms, 1)), 0)
    image_out, placed = run(
        both_final_kernel,
        [like((32, width))] * 2,
        (mixed_img, mixed_txt, *sums, own_mod, row_mod, slots_own),
    )

    placed = lax.all_to_all(placed.reshape(8, 4, width), "grp", 0, 0, tiled=True)
    prompt_out = placed.reshape(32, width)

    return (image_out, prompt_out)


def solution(mesh):
    placed = (
        P("grp", None),
        P(("grp", "tp"), None),
        P(("grp", "tp"), None),
        P("grp"),
        P("grp", None, None, None),
        P(),
        P("tp", None),
        P(None, None, "tp"),
        P(None, None, "tp"),
        P("tp", None),
        P("tp", None),
        P(None, None, "tp"),
        P(None, "tp", None),
        P(None, "tp", None),
        P(None, None, None, "tp"),
    )
    return jax.shard_map(
        shards,
        mesh=mesh,
        in_specs=placed,
        out_specs=(P(("grp", "tp"), None), P(("grp", "tp"), None)),
        check_vma=False,
    )
```

```python
import functools

import jax
import jax.numpy as jnp
from jax import lax
from jax.experimental import pallas as pl
from jax.experimental.pallas import tpu as pltpu
from jax.sharding import PartitionSpec as P

HEAD_DIM = 64
CAP = 2
EPSILON = 1e-06
ADAPTER_SCALE = 0.5
SIDE = 4
POOL = 20
WIDTH = 2432
EXTRA = 512
F32 = jnp.float32
BF16 = jnp.bfloat16


def torus_shift(values, stage, step):
    pairs = []
    for grp in range(8):
        for tp in range(16):
            z, y = divmod(tp, SIDE)
            if (grp + stage) % 2 == 0:
                y = (y + step) % SIDE
            else:
                z = (z + step) % SIDE
            pairs.append((grp * 16 + tp, grp * 16 + z * SIDE + y))
    return lax.ppermute(values, ("grp", "tp"), pairs)


def core_swap(values):
    return lax.ppermute(values, "grp", [(grp, grp ^ 1) for grp in range(8)])


def chip_swap(values, far):
    pairs = []
    for grp in range(8):
        chip = 3 - grp // 2 if far else (grp // 2) ^ 1
        pairs.append((grp, chip * 2 + grp % 2))
    return lax.ppermute(values, "grp", pairs)


def spread(rows, stage):
    return [
        rows,
        torus_shift(rows, stage, -1),
        torus_shift(rows, stage, 2),
        torus_shift(rows, stage, 1),
    ]


def exchange(parts, stage):
    return [
        parts[0],
        torus_shift(parts[3], stage, -1),
        torus_shift(parts[2], stage, 2),
        torus_shift(parts[1], stage, 1),
    ]


def run(kernel, outs, args, smem=0, scratch=(), flops=0, limit=8, after=(), hbm=()):
    count = len(args)
    spaces = [pltpu.SMEM] * smem + [pltpu.VMEM] * (count - smem)
    for index in hbm:
        spaces[index] = pl.ANY
    specs = [pl.BlockSpec(memory_space=space) for space in spaces]
    specs += [pl.BlockSpec(memory_space=pl.ANY)] * len(after)
    single = not isinstance(outs, list)
    shapes = [outs] if single else outs
    moved = sum(a.size * a.dtype.itemsize for a in args)
    moved += sum(s.size * s.dtype.itemsize for s in shapes)

    def body(*refs):
        kernel(*refs[:count], *refs[count + len(after) :])

    result = pl.pallas_call(
        body,
        out_shape=shapes,
        in_specs=specs,
        out_specs=[pl.BlockSpec(memory_space=pltpu.VMEM)] * len(shapes),
        scratch_shapes=list(scratch),
        compiler_params=pltpu.CompilerParams(vmem_limit_bytes=limit << 20),
        cost_estimate=pl.CostEstimate(flops=flops, bytes_accessed=moved, transcendentals=0),
    )(*args, *after)
    return result[0] if single else result


def like(shape, dtype=BF16):
    return jax.ShapeDtypeStruct(shape, dtype)


def normed(values):
    centred = values - jnp.mean(values, -1, keepdims=True)
    return centred * lax.rsqrt(jnp.mean(centred * centred, -1, keepdims=True) + EPSILON)


def low_half(shape):
    return lax.broadcasted_iota(jnp.int32, shape, len(shape) - 1) < HEAD_DIM


def head_norm(values, gains):
    first = low_half(values.shape)
    squares = values * values
    head0 = jnp.sum(jnp.where(first, squares, 0.0), -1, keepdims=True)
    head1 = jnp.sum(jnp.where(first, 0.0, squares), -1, keepdims=True)
    scale = jnp.where(
        first,
        lax.rsqrt(head0 * (1.0 / HEAD_DIM) + EPSILON),
        lax.rsqrt(head1 * (1.0 / HEAD_DIM) + EPSILON),
    )
    return values * scale * gains


def pack_kernel(rows_ref, line_ref, out_ref, slot_ref, held, wide):
    wide[...] = jnp.full(wide.shape, -1, jnp.int32)
    wide[0:1, 0:POOL] = line_ref[...]
    line = wide[0:1, :]
    first = lax.broadcasted_iota(jnp.int32, (POOL, 256), 0)
    second = lax.broadcasted_iota(jnp.int32, (POOL, 256), 1)
    column = jnp.sum(jnp.where(first == second, line, 0), 1, keepdims=True)
    rank = jnp.sum(jnp.where((column == line) & (first < second), 1, 0), 0, keepdims=True)
    slot_ref[...] = line * CAP + rank
    held[...] = jnp.zeros_like(held)
    held[POOL : POOL + 1, :] = (line * CAP + rank).astype(F32)
    for block in range(16):
        held[0:POOL, :] = rows_ref[:, block * 256 : (block + 1) * 256].astype(F32)
        out_ref[block] = held[...].astype(BF16)


def embed_kernel(
    places_ref, arrived_ref, weight_ref, low_ref, out0, out1, out2, out3, slot_ref, held, label
):
    for far, out in enumerate((out0, out1, out2, out3)):
        for near in range(SIDE):
            place = far * SIDE + near
            block = arrived_ref[places_ref[place]].astype(F32)
            held[near * POOL : (near + 1) * POOL, :] = block[0:POOL]
            label[place : place + 1, :] = block[POOL : POOL + 1, 0:128]
        out[:, 0:WIDTH] = jnp.dot(
            held[...].astype(BF16), weight_ref[...], preferred_element_type=F32
        ).astype(BF16)
        out[:, WIDTH:] = jnp.zeros((SIDE * POOL, EXTRA), BF16)
        for near in range(SIDE):
            left = WIDTH + near // 2 * 256
            top = near % 2 * 32
            out[top : top + 32, left : left + 192] = low_ref[places_ref[far * SIDE + near]]
    line = (128, 16 * POOL)
    offset = lax.broadcasted_iota(jnp.int32, line, 1) - lax.broadcasted_iota(jnp.int32, line, 0)
    taken = offset == 0
    for place in range(1, 16):
        taken = taken | (offset == place * POOL)
    taken = taken & (lax.broadcasted_iota(jnp.int32, line, 0) < POOL)
    spot = jnp.dot(
        label[...].astype(BF16),
        jnp.where(taken, 1.0, 0.0).astype(BF16),
        preferred_element_type=F32,
    )
    place = lax.broadcasted_iota(jnp.int32, spot.shape, 0)
    start = place * POOL
    column = lax.broadcasted_iota(jnp.int32, spot.shape, 1)
    inside = (column >= start) & (column < start + POOL)
    target = jnp.sum(jnp.where(inside, spot, 0.0), 0, keepdims=True).astype(jnp.int32)
    block = jnp.sum(jnp.where(inside, place, 0), 0, keepdims=True)
    slot_ref[...] = (
        (target >> 2) * 64 + ((target >> 1) & 1) * 32 + (target & 1) + 2 * block
    )


def middle_kernel(in0, in1, in2, in3, out0, out1, out2, out3, held):
    held[...] = total_of((in0, in1, in2, in3))
    for near, out in enumerate((out0, out1, out2, out3)):
        out[:, 0:WIDTH] = held[near * POOL : (near + 1) * POOL, 0:WIDTH].astype(BF16)
        left = WIDTH + near // 2 * 256
        for half in range(2):
            top = near % 2 * 32 + half * 16
            out[0:16, WIDTH + half * 256 : WIDTH + half * 256 + 256] = held[
                top : top + 16, left : left + 256
            ].astype(BF16)
        out[16:POOL, WIDTH:] = jnp.zeros((POOL - 16, EXTRA), BF16)


def both_middle_kernel(*refs):
    img, txt, outs, held = refs[0:4], refs[4:8], refs[8:12], refs[12]
    held[...] = total_of(txt)
    for near, out in enumerate(outs):
        rows = slice(near * 32, (near + 1) * 32)
        out[0:32, :] = functools.reduce(
            jnp.add, [piece[rows, :].astype(F32) for piece in img]
        ).astype(BF16)
        out[32 : 32 + POOL, :] = held[near * POOL : (near + 1) * POOL, :].astype(BF16)


def join_kernel(in0, in1, in2, in3, out_ref, held):
    for place, piece in enumerate((in0, in1, in2, in3)):
        held[place * POOL : (place + 1) * POOL, :] = piece[...].astype(F32)
    out_ref[...] = held[...].astype(BF16)


def both_join_kernel(in0, in1, in2, in3, out_ref, held):
    for place, piece in enumerate((in0, in1, in2, in3)):
        out_ref[place * 32 : (place + 1) * 32, :] = piece[0:32, :]
        held[place * POOL : (place + 1) * POOL, :] = piece[32:, :].astype(F32)
    out_ref[128:, :] = held[...].astype(BF16)


def prompt_mod_kernel(mod_ref, out_ref):
    for own in range(2):
        for place in range(6):
            out_ref[own, place : place + 1, :] = mod_ref[own, place, 1:2, :]
        out_ref[own, 6:8, :] = jnp.zeros((2, out_ref.shape[2]), F32)


def mod_pair_kernel(first_ref, second_ref, out_ref):
    count = first_ref.shape[0]
    out_ref[0:count] = first_ref[...]
    out_ref[count : 2 * count] = second_ref[...]


def row_mod_kernel(index_ref, near_ref, far_ref, out_ref):
    for row in range(POOL):
        index = index_ref[row]
        within = lax.rem(index, 8)
        values = jnp.where(index < 8, near_ref[within], far_ref[within])
        for place in range(6):
            out_ref[place, row : row + 1, :] = values[place : place + 1]


def total_of(parts):
    return functools.reduce(jnp.add, [part[...].astype(F32) for part in parts])


def embed_norm_kernel(in0, in1, in2, in3, mod_ref, embedded_ref, out_ref):
    total = total_of((in0, in1, in2, in3))
    embedded = total[:, 0:WIDTH].astype(BF16)
    embedded_ref[...] = embedded
    modded = normed(embedded.astype(F32)) * (1.0 + mod_ref[1]) + mod_ref[0]
    out_ref[:, 0:WIDTH] = modded.astype(BF16)
    out_ref[:, WIDTH:] = total[:, WIDTH:].astype(BF16)


def both_norm_kernel(
    image_ref, embedded_ref, in0, in1, in2, in3, img_mod_ref, txt_mod_ref,
    img_ref, txt_ref, out_ref,
):
    projected = total_of((in0, in1, in2, in3))
    gate, shift, scale = img_mod_ref[2:3, :], img_mod_ref[3:4, :], img_mod_ref[4:5, :]
    mixed = (image_ref[...].astype(F32) + gate * projected[0:32]).astype(BF16)
    img_ref[...] = mixed
    out_ref[0:32, :] = (normed(mixed.astype(F32)) * (1.0 + scale) + shift).astype(BF16)
    mixed = (embedded_ref[...].astype(F32) + txt_mod_ref[2] * projected[32:]).astype(BF16)
    txt_ref[...] = mixed
    hidden = normed(mixed.astype(F32)) * (1.0 + txt_mod_ref[4]) + txt_mod_ref[3]
    out_ref[32 : 32 + POOL, :] = hidden.astype(BF16)


def one_hot(line, count):
    shape = (count, line.shape[1])
    return jnp.where(lax.broadcasted_iota(jnp.int32, shape, 0) == line, 1.0, 0.0)


def with_keep(values, keep):
    first = low_half(values.shape)
    return jnp.where(first, values, keep), jnp.where(first, keep, values)


def project(rows, weight_ref):
    both = jnp.concatenate([weight_ref[0], weight_ref[1]], -1)
    first = jnp.dot(rows, both, preferred_element_type=F32)
    return first, jnp.dot(rows, weight_ref[2], preferred_element_type=F32)


def txt_qkv_kernel(
    places_ref, in0, in1, in2, in3, weight_ref, gain_ref, slot_ref, out_ref, low_ref, held, rows_ref
):
    part = in0.shape[0]
    for place, piece in enumerate((in0, in1, in2, in3)):
        rows_ref[place * part : (place + 1) * part, :] = piece[:, 0:WIDTH]
        wide = piece[:, WIDTH:].astype(F32)
        for near in range(SIDE):
            rows = wide[near * POOL : near * POOL + 16]
            start = pl.multiple_of(places_ref[place * SIDE + near] * 32, 32)
            low_ref[pl.ds(start, 16), :] = rows[:, 0:192]
            low_ref[pl.ds(start + 16, 16), :] = rows[:, 256:448]
    projected, values = project(rows_ref[...], weight_ref)
    held[:, 0:128] = head_norm(projected[:, 0:128], gain_ref[0:1, :]).astype(BF16)
    held[:, 128:256] = head_norm(projected[:, 128:256], gain_ref[1:2, :]).astype(BF16)
    held[:, 256:384] = values.astype(BF16)
    hot = one_hot(slot_ref[...], 512)
    keep = jnp.sum(hot, -1, keepdims=True)
    slots = jnp.dot(hot.astype(BF16), held[...], preferred_element_type=F32)
    val0, val1 = with_keep(slots[:, 256:384], keep)
    out_ref[:, 0:256] = slots[:, 0:256].astype(BF16)
    out_ref[:, 256:384] = val0.astype(BF16)
    out_ref[:, 384:512] = val1.astype(BF16)


def img_project_kernel(
    ids_ref, tp_ref, image_hbm, mod_ref, weight_hbm, down_hbm,
    projected_ref, low_ref, own_ref, own_mod_ref, image, weight, down, wide, modded, sems,
):
    copies = [pltpu.make_async_copy(image_hbm, image, sems.at[0])]
    copies.append(pltpu.make_async_copy(weight_hbm, weight, sems.at[1]))
    for own in range(2):
        copies.append(
            pltpu.make_async_copy(down_hbm.at[ids_ref[own]], down.at[own], sems.at[2 + own])
        )
    for copy in copies:
        copy.start()
    copies[0].wait()
    depth = down.shape[1]
    tp = tp_ref[0]
    own_ref[...] = image[pl.ds(pl.multiple_of(tp * 32, 32), 32), :]
    for place in range(6):
        own_mod_ref[place : place + 1, :] = mod_ref[tp // 8, place, 0:1, :]
    for own in range(2):
        for part in range(2):
            rows = image[own * 256 + part * 128 : own * 256 + (part + 1) * 128, :].astype(F32)
            scaled = normed(rows) * (1.0 + mod_ref[own, 1, 0:1, :]) + mod_ref[own, 0, 0:1, :]
            modded[part * 128 : (part + 1) * 128, :] = scaled.astype(BF16)
        if own == 0:
            copies[1].wait()
        copies[2 + own].wait()
        wide[...] = jnp.zeros_like(wide)
        start = pl.multiple_of(tp * depth, 8)
        wide[pl.ds(start, depth), :] = down[own].astype(F32)
        projected, values = project(modded[...], weight)
        projected_ref[own * 256 : (own + 1) * 256, 0:256] = projected
        projected_ref[own * 256 : (own + 1) * 256, 256:384] = values
        low = jnp.dot(modded[...], wide[...].astype(BF16), preferred_element_type=F32)
        for block in range(8):
            low_ref[own * 8 + block] = low[block * 32 : (block + 1) * 32].astype(BF16)


def img_adapt_kernel(ids_ref, low_ref, projected_ref, up_hbm, gain_ref, out_ref, up, lift, sems):
    copies = []
    for own in range(2):
        copies.append(
            pltpu.make_async_copy(up_hbm.at[ids_ref[own]], up.at[own], sems.at[own])
        )
        copies[own].start()
    for own in range(2):
        copies[own].wait()
        lift[...] = jnp.zeros_like(lift)
        for part in range(3):
            lift[part * 64 : (part + 1) * 64, part * 128 : (part + 1) * 128] = up[own, part]
        rows = slice(own * 256, (own + 1) * 256)
        projected = projected_ref[rows, :] + ADAPTER_SCALE * jnp.dot(
            low_ref[rows, :].astype(BF16), lift[...], preferred_element_type=F32
        )
        out_ref[rows, 0:128] = head_norm(projected[:, 0:128], gain_ref[0:1, :]).astype(BF16)
        out_ref[rows, 128:256] = head_norm(projected[:, 128:256], gain_ref[1:2, :]).astype(BF16)
        val0, val1 = with_keep(projected[:, 256:384], 1.0)
        out_ref[rows, 256:384] = val0.astype(BF16)
        out_ref[rows, 384:512] = val1.astype(BF16)


def attend(queries, tokens):
    scaled = queries.astype(F32) * HEAD_DIM ** (-0.5)
    first = low_half(scaled.shape)
    keys = tokens[:, 128:256]
    results = []
    for head in range(2):
        own = jnp.where(first if head == 0 else ~first, scaled, 0.0).astype(BF16)
        scores = lax.dot_general(
            own, keys, (((1,), (1,)), ((), ())), preferred_element_type=F32
        )
        weights = jnp.exp(scores).astype(BF16)
        summed = jnp.dot(
            weights, tokens[:, 256 + head * 128 : 384 + head * 128], preferred_element_type=F32
        )
        results.append(summed / pltpu.roll(summed, HEAD_DIM, 1))
    return jnp.where(first, results[0], results[1]).astype(BF16)


def img_attend_kernel(
    places_ref, img_ref, slot_ref, weight_ref,
    out0, out1, out2, out3, token_ref, tokens, held, ranked,
):
    for own in range(2):
        tokens[own, 0:256, :] = img_ref[own * 256 : (own + 1) * 256, :]
        for source in range(8):
            start = 256 + source * 32
            tokens[own, start : start + 32, :] = slot_ref[source, own * 32 : (own + 1) * 32, :]
    token_ref[...] = tokens[...]
    for own in range(2):
        held[own * 256 : (own + 1) * 256, :] = attend(tokens[own, 0:256, 0:128], tokens[own])
    for place in range(16):
        start = pl.multiple_of(places_ref[place] * 32, 32)
        ranked[place * 32 : (place + 1) * 32, :] = held[pl.ds(start, 32), :]
    result = jnp.dot(ranked[...], weight_ref[...], preferred_element_type=F32)
    for place, out in enumerate((out0, out1, out2, out3)):
        out[...] = result[place * 128 : (place + 1) * 128].astype(BF16)


def txt_attend_kernel(token_ref, out_ref):
    for own in range(2):
        attended = attend(token_ref[own, 256:512, 0:128], token_ref[own])
        for source in range(8):
            start = source * 32
            out_ref[source, own * 32 : (own + 1) * 32, :] = attended[start : start + 32]


def txt_project_kernel(att_ref, slot_ref, weight_ref, out0, out1, out2, out3):
    hot = one_hot(slot_ref[...], 512).astype(BF16)
    rows = lax.dot_general(
        hot, att_ref[...], (((0,), (0,)), ((), ())), preferred_element_type=F32
    ).astype(BF16)
    part = out0.shape[0]
    result = jnp.dot(rows, weight_ref[...], preferred_element_type=F32)
    for place, out in enumerate((out0, out1, out2, out3)):
        out[...] = result[place * part : (place + 1) * part].astype(BF16)


def feed_kernel(
    start, stream, in0, in1, in2, in3, win_ref, wout_ref, out0, out1, out2, out3, rows_ref
):
    part, width = out0.shape
    for place, piece in enumerate((in0, in1, in2, in3)):
        rows_ref[place * part : (place + 1) * part, :] = piece[start : start + part, :]
    hidden = lax.dot_general(
        rows_ref[...], win_ref[stream], (((1,), (1,)), ((), ())), preferred_element_type=F32
    )
    hidden = jax.nn.gelu(hidden, approximate=True).astype(BF16)
    for columns in (slice(0, 1280), slice(1280, width)):
        result = jnp.dot(hidden, wout_ref[stream, :, columns], preferred_element_type=F32)
        for place, out in enumerate((out0, out1, out2, out3)):
            out[:, columns] = result[place * part : (place + 1) * part].astype(BF16)


def both_final_kernel(
    img_ref, txt_ref, in0, in1, in2, in3, img_mod_ref, txt_mod_ref, slot_ref, out_ref, placed_ref
):
    total = total_of((in0, in1, in2, in3))
    out_ref[...] = (img_ref[...].astype(F32) + img_mod_ref[5:6, :] * total[0:32]).astype(BF16)
    rows = txt_ref[...].astype(F32) + txt_mod_ref[5] * total[32:]
    hot = one_hot(slot_ref[:, 0:POOL], 32).astype(BF16)
    placed_ref[...] = jnp.dot(hot, rows.astype(BF16), preferred_element_type=F32).astype(BF16)


def middle(parts):
    rows, width = parts[0].shape
    return run(
        middle_kernel,
        [like((rows // SIDE, width))] * SIDE,
        parts,
        scratch=[pltpu.VMEM((rows, width), F32)],
    )


def both_middle(img_parts, txt_parts):
    rows, width = txt_parts[0].shape
    return run(
        both_middle_kernel,
        [like((32 + POOL, width))] * SIDE,
        (*img_parts, *txt_parts),
        scratch=[pltpu.VMEM((rows, width), F32)],
    )


def join(kernel, parts):
    width = parts[0].shape[1]
    return run(
        kernel,
        like((SIDE * parts[0].shape[0], width)),
        parts,
        scratch=[pltpu.VMEM((SIDE * POOL, width), F32)],
    )


def feed(parts, start, rows, weight_in, weight_out, stream, after=()):
    width = parts[0].shape[1]
    return run(
        functools.partial(feed_kernel, start, stream),
        [like((rows, width))] * SIDE,
        (*parts, weight_in, weight_out),
        scratch=[pltpu.VMEM((rows * SIDE, width), BF16)],
        flops=rows * SIDE * width * weight_in.shape[1] * 4,
        limit=14,
        after=after,
    )


def shards(
    image,
    prompt_encoder_rows,
    prompt_row_request,
    request_adapter,
    modulation,
    query_key_gain,
    prompt_embed_weight,
    image_query_key_value,
    prompt_query_key_value,
    image_out_weight,
    prompt_out_weight,
    feed_in_weight,
    feed_out_weight,
    adapter_down,
    adapter_up,
):
    grp = lax.axis_index("grp")
    tp = lax.axis_index("tp")
    chip, core = grp // 2, grp % 2
    z, y = tp // SIDE, tp % SIDE
    width = image.shape[1]

    steps = jnp.arange(16)
    far, near = steps // SIDE, steps % SIDE
    places = jnp.where(
        core == 0,
        ((z + far) % SIDE) * SIDE + (y + near) % SIDE,
        ((z + near) % SIDE) * SIDE + (y + far) % SIDE,
    ).astype(jnp.int32)
    gains = jnp.concatenate([query_key_gain, query_key_gain], -1)

    request = prompt_row_request[:, 0]
    outgoing, slots_own = run(
        pack_kernel,
        [like((16, 32, 256)), like((1, 256), jnp.int32)],
        (prompt_encoder_rows, prompt_row_request.reshape(1, POOL)),
        scratch=[pltpu.VMEM((32, 256), F32), pltpu.VMEM((8, 256), jnp.int32)],
    )
    arrived = lax.all_to_all(outgoing, "tp", 0, 0, tiled=True)
    img_projected, low_part, own_image, own_mod = run(
        img_project_kernel,
        [
            like((512, 384), F32),
            like((16, 32, 192)),
            like((32, width)),
            like((6, width), F32),
        ],
        (
            request_adapter,
            tp.reshape(1).astype(jnp.int32),
            image,
            modulation.transpose(0, 2, 1, 3),
            image_query_key_value.transpose(1, 0, 2),
            adapter_down,
        ),
        smem=2,
        scratch=[
            pltpu.VMEM(image.shape, BF16),
            pltpu.VMEM((3, width, 128), BF16),
            pltpu.VMEM((2, *adapter_down.shape[1:]), BF16),
            pltpu.VMEM((width, 192), F32),
            pltpu.VMEM((256, width), BF16),
            pltpu.SemaphoreType.DMA((4,)),
        ],
        flops=512 * width * 576 * 2,
        limit=56,
        after=(outgoing,),
        hbm=(2, 4, 5),
    )
    prompt_mod = run(
        prompt_mod_kernel, like((2, 8, width), F32), (modulation.transpose(0, 2, 1, 3),)
    )
    mod_own = run(
        mod_pair_kernel, like((4, 8, width), F32), (prompt_mod, core_swap(prompt_mod))
    )
    home = request // 4
    row_index = jnp.where(
        home == chip, 0, jnp.where(home == (chip ^ 1), 1, jnp.where(home == 3 - chip, 2, 3))
    )
    row_index = row_index * 4 + (request // 2 % 2 + core) % 2 * 2 + request % 2

    *embed_parts, slots_all = run(
        embed_kernel,
        [like((SIDE * POOL, width + EXTRA))] * SIDE + [like((1, 16 * POOL), jnp.int32)],
        (places, arrived, prompt_embed_weight, low_part),
        smem=1,
        scratch=[pltpu.VMEM((SIDE * POOL, 256), F32), pltpu.VMEM((16, 128), F32)],
        flops=320 * 256 * width * 2,
        after=(mod_own,),
    )
    embed_pieces = exchange(embed_parts, 1)

    embed_sums = exchange(middle(embed_pieces), 0)
    mod_near = run(
        mod_pair_kernel, like((8, 8, width), F32), (mod_own, chip_swap(mod_own, False))
    )
    row_mod = run(
        row_mod_kernel,
        like((6, POOL, width), F32),
        (row_index, mod_near, chip_swap(mod_near, True)),
        smem=1,
    )
    embedded, txt_mod = run(
        embed_norm_kernel,
        [like((POOL, width)), like((POOL, width + EXTRA))],
        (*embed_sums, row_mod),
    )
    txt_mods = spread(join(join_kernel, spread(txt_mod, 0)), 1)

    slot_parts, low = run(
        txt_qkv_kernel,
        [like((512, 512)), like((512, 192), F32)],
        (places, *txt_mods, prompt_query_key_value.transpose(1, 0, 2), gains[1], slots_all),
        smem=1,
        scratch=[pltpu.VMEM((16 * POOL, 384), BF16), pltpu.VMEM((16 * POOL, width), BF16)],
        flops=320 * width * 384 * 2,
        limit=14,
    )
    img_parts = run(
        img_adapt_kernel,
        like((512, 512)),
        (request_adapter, low, img_projected, adapter_up, gains[0]),
        smem=1,
        scratch=[
            pltpu.VMEM((2, 3, 64, 128), BF16),
            pltpu.VMEM((192, 384), BF16),
            pltpu.SemaphoreType.DMA((2,)),
        ],
        flops=512 * 384 * 192 * 2,
        hbm=(3,),
    )
    slot_parts = lax.all_to_all(slot_parts.reshape(8, 64, 512), "grp", 0, 0, tiled=True)

    *img_terms, tokens = run(
        img_attend_kernel,
        [like((128, width))] * SIDE + [like((2, 512, 512))],
        (places, img_parts, slot_parts, image_out_weight),
        smem=1,
        scratch=[
            pltpu.VMEM((2, 512, 512), BF16),
            pltpu.VMEM((512, 128), BF16),
            pltpu.VMEM((512, 128), BF16),
        ],
        flops=1 << 30,
        limit=16,
    )
    img_sums = exchange(img_terms, 1)
    att_parts = run(txt_attend_kernel, like((8, 64, 128)), (tokens,), flops=1 << 29)
    att_parts = lax.all_to_all(att_parts, "grp", 0, 0, tiled=True).reshape(512, 128)
    txt_terms = run(
        txt_project_kernel,
        [like((SIDE * POOL, width))] * SIDE,
        (att_parts, slots_all, prompt_out_weight),
        flops=320 * 128 * width * 2,
        after=(img_sums[1],),
    )
    txt_sums = exchange(txt_terms, 1)

    sums = exchange(both_middle(img_sums, txt_sums), 0)
    mixed_img, mixed_txt, norm_rows = run(
        both_norm_kernel,
        [like((32, width)), like((POOL, width)), like((32 + POOL, width))],
        (own_image, embedded, *sums, own_mod, row_mod),
    )
    rows = spread(join(both_join_kernel, spread(norm_rows, 0)), 1)
    weight_in = feed_in_weight.transpose(0, 2, 1)
    img_terms = feed(rows, 0, 128, weight_in, feed_out_weight, 0)
    txt_terms = feed(
        rows, 128, SIDE * POOL, weight_in, feed_out_weight, 1, (img_terms[0],)
    )
    sums = exchange(both_middle(exchange(img_terms, 1), exchange(txt_terms, 1)), 0)
    image_out, placed = run(
        both_final_kernel,
        [like((32, width))] * 2,
        (mixed_img, mixed_txt, *sums, own_mod, row_mod, slots_own),
    )

    placed = lax.all_to_all(placed.reshape(8, 4, width), "grp", 0, 0, tiled=True)
    prompt_out = placed.reshape(32, width)

    return (image_out, prompt_out)


def solution(mesh):
    placed = (
        P("grp", None),
        P(("grp", "tp"), None),
        P(("grp", "tp"), None),
        P("grp"),
        P("grp", None, None, None),
        P(),
        P("tp", None),
        P(None, None, "tp"),
        P(None, None, "tp"),
        P("tp", None),
        P("tp", None),
        P(None, None, "tp"),
        P(None, "tp", None),
        P(None, "tp", None),
        P(None, None, None, "tp"),
    )
    return jax.shard_map(
        shards,
        mesh=mesh,
        in_specs=placed,
        out_specs=(P(("grp", "tp"), None), P(("grp", "tp"), None)),
        check_vma=False,
    )
```

```python
import functools

import jax
import jax.numpy as jnp
from jax import lax
from jax.experimental import pallas as pl
from jax.experimental.pallas import tpu as pltpu
from jax.sharding import PartitionSpec as P

HEAD_DIM = 64
CAP = 2
EPSILON = 1e-06
ADAPTER_SCALE = 0.5
SIDE = 4
POOL = 20
WIDTH = 2432
EXTRA = 512
F32 = jnp.float32
BF16 = jnp.bfloat16


def torus_shift(values, stage, step):
    pairs = []
    for grp in range(8):
        for tp in range(16):
            z, y = divmod(tp, SIDE)
            if (grp + stage) % 2 == 0:
                y = (y + step) % SIDE
            else:
                z = (z + step) % SIDE
            pairs.append((grp * 16 + tp, grp * 16 + z * SIDE + y))
    return lax.ppermute(values, ("grp", "tp"), pairs)


def core_swap(values):
    return lax.ppermute(values, "grp", [(grp, grp ^ 1) for grp in range(8)])


def chip_swap(values, far):
    pairs = []
    for grp in range(8):
        chip = 3 - grp // 2 if far else (grp // 2) ^ 1
        pairs.append((grp, chip * 2 + grp % 2))
    return lax.ppermute(values, "grp", pairs)


def spread(rows, stage):
    return [
        rows,
        torus_shift(rows, stage, -1),
        torus_shift(rows, stage, 2),
        torus_shift(rows, stage, 1),
    ]


def exchange(parts, stage):
    return [
        parts[0],
        torus_shift(parts[3], stage, -1),
        torus_shift(parts[2], stage, 2),
        torus_shift(parts[1], stage, 1),
    ]


def run(kernel, outs, args, smem=0, scratch=(), flops=0, limit=8, after=(), hbm=()):
    count = len(args)
    spaces = [pltpu.SMEM] * smem + [pltpu.VMEM] * (count - smem)
    for index in hbm:
        spaces[index] = pl.ANY
    specs = [pl.BlockSpec(memory_space=space) for space in spaces]
    specs += [pl.BlockSpec(memory_space=pl.ANY)] * len(after)
    single = not isinstance(outs, list)
    shapes = [outs] if single else outs
    moved = sum(a.size * a.dtype.itemsize for a in args)
    moved += sum(s.size * s.dtype.itemsize for s in shapes)

    def body(*refs):
        kernel(*refs[:count], *refs[count + len(after) :])

    result = pl.pallas_call(
        body,
        out_shape=shapes,
        in_specs=specs,
        out_specs=[pl.BlockSpec(memory_space=pltpu.VMEM)] * len(shapes),
        scratch_shapes=list(scratch),
        compiler_params=pltpu.CompilerParams(vmem_limit_bytes=limit << 20),
        cost_estimate=pl.CostEstimate(flops=flops, bytes_accessed=moved, transcendentals=0),
    )(*args, *after)
    return result[0] if single else result


def like(shape, dtype=BF16):
    return jax.ShapeDtypeStruct(shape, dtype)


def normed(values):
    centred = values - jnp.mean(values, -1, keepdims=True)
    return centred * lax.rsqrt(jnp.mean(centred * centred, -1, keepdims=True) + EPSILON)


def low_half(shape):
    return lax.broadcasted_iota(jnp.int32, shape, len(shape) - 1) < HEAD_DIM


def head_norm(values, gains):
    first = low_half(values.shape)
    squares = values * values
    head0 = jnp.sum(jnp.where(first, squares, 0.0), -1, keepdims=True)
    head1 = jnp.sum(jnp.where(first, 0.0, squares), -1, keepdims=True)
    scale = jnp.where(
        first,
        lax.rsqrt(head0 * (1.0 / HEAD_DIM) + EPSILON),
        lax.rsqrt(head1 * (1.0 / HEAD_DIM) + EPSILON),
    )
    return values * scale * gains


def pack_kernel(rows_ref, line_ref, out_ref, slot_ref, held, wide):
    wide[...] = jnp.full(wide.shape, -1, jnp.int32)
    wide[0:1, 0:POOL] = line_ref[...]
    line = wide[0:1, :]
    first = lax.broadcasted_iota(jnp.int32, (POOL, 256), 0)
    second = lax.broadcasted_iota(jnp.int32, (POOL, 256), 1)
    column = jnp.sum(jnp.where(first == second, line, 0), 1, keepdims=True)
    rank = jnp.sum(jnp.where((column == line) & (first < second), 1, 0), 0, keepdims=True)
    slot_ref[...] = line * CAP + rank
    held[...] = jnp.zeros_like(held)
    held[POOL : POOL + 1, :] = (line * CAP + rank).astype(F32)
    for block in range(16):
        held[0:POOL, :] = rows_ref[:, block * 256 : (block + 1) * 256].astype(F32)
        out_ref[block] = held[...].astype(BF16)


def embed_kernel(
    places_ref, arrived_ref, weight_ref, low_ref, out0, out1, out2, out3, slot_ref, held, label
):
    for far, out in enumerate((out0, out1, out2, out3)):
        for near in range(SIDE):
            place = far * SIDE + near
            block = arrived_ref[places_ref[place]].astype(F32)
            held[near * POOL : (near + 1) * POOL, :] = block[0:POOL]
            label[place : place + 1, :] = block[POOL : POOL + 1, 0:128]
        out[:, 0:WIDTH] = jnp.dot(
            held[...].astype(BF16), weight_ref[...], preferred_element_type=F32
        ).astype(BF16)
        out[:, WIDTH:] = jnp.zeros((SIDE * POOL, EXTRA), BF16)
        for near in range(SIDE):
            left = WIDTH + near // 2 * 256
            top = near % 2 * 32
            out[top : top + 32, left : left + 192] = low_ref[places_ref[far * SIDE + near]]
    line = (128, 16 * POOL)
    offset = lax.broadcasted_iota(jnp.int32, line, 1) - lax.broadcasted_iota(jnp.int32, line, 0)
    taken = offset == 0
    for place in range(1, 16):
        taken = taken | (offset == place * POOL)
    taken = taken & (lax.broadcasted_iota(jnp.int32, line, 0) < POOL)
    spot = jnp.dot(
        label[...].astype(BF16),
        jnp.where(taken, 1.0, 0.0).astype(BF16),
        preferred_element_type=F32,
    )
    place = lax.broadcasted_iota(jnp.int32, spot.shape, 0)
    start = place * POOL
    column = lax.broadcasted_iota(jnp.int32, spot.shape, 1)
    inside = (column >= start) & (column < start + POOL)
    target = jnp.sum(jnp.where(inside, spot, 0.0), 0, keepdims=True).astype(jnp.int32)
    block = jnp.sum(jnp.where(inside, place, 0), 0, keepdims=True)
    slot_ref[...] = (
        (target >> 2) * 64 + ((target >> 1) & 1) * 32 + (target & 1) + 2 * block
    )


def middle_kernel(in0, in1, in2, in3, out0, out1, out2, out3, held):
    held[...] = total_of((in0, in1, in2, in3))
    for near, out in enumerate((out0, out1, out2, out3)):
        out[:, 0:WIDTH] = held[near * POOL : (near + 1) * POOL, 0:WIDTH].astype(BF16)
        left = WIDTH + near // 2 * 256
        for half in range(2):
            top = near % 2 * 32 + half * 16
            out[0:16, WIDTH + half * 256 : WIDTH + half * 256 + 256] = held[
                top : top + 16, left : left + 256
            ].astype(BF16)
        out[16:POOL, WIDTH:] = jnp.zeros((POOL - 16, EXTRA), BF16)


def both_middle_kernel(*refs):
    img, txt, outs, held = refs[0:4], refs[4:8], refs[8:12], refs[12]
    held[...] = total_of(txt)
    for near, out in enumerate(outs):
        rows = slice(near * 32, (near + 1) * 32)
        out[0:32, :] = functools.reduce(
            jnp.add, [piece[rows, :].astype(F32) for piece in img]
        ).astype(BF16)
        out[32 : 32 + POOL, :] = held[near * POOL : (near + 1) * POOL, :].astype(BF16)


def part_middle_kernel(
    in0, in1, in2, in3, txt0, txt1, txt2, txt3, img0, img1, img2, img3, held
):
    pieces = (in0, in1, in2, in3)
    held[...] = functools.reduce(jnp.add, [piece[128:, :].astype(F32) for piece in pieces])
    for near, out in enumerate((txt0, txt1, txt2, txt3)):
        out[...] = held[near * POOL : (near + 1) * POOL, :].astype(BF16)
    for near, out in enumerate((img0, img1, img2, img3)):
        rows = slice(near * 32, (near + 1) * 32)
        out[...] = functools.reduce(
            jnp.add, [piece[rows, :].astype(F32) for piece in pieces]
        ).astype(BF16)


def join_kernel(in0, in1, in2, in3, out_ref, held):
    for place, piece in enumerate((in0, in1, in2, in3)):
        held[place * POOL : (place + 1) * POOL, :] = piece[...].astype(F32)
    out_ref[...] = held[...].astype(BF16)


def both_join_kernel(in0, in1, in2, in3, out_ref, held):
    for place, piece in enumerate((in0, in1, in2, in3)):
        out_ref[place * 32 : (place + 1) * 32, :] = piece[0:32, :]
        held[place * POOL : (place + 1) * POOL, :] = piece[32:, :].astype(F32)
    out_ref[128:, :] = held[...].astype(BF16)


def prompt_mod_kernel(mod_ref, out_ref):
    for own in range(2):
        for place in range(6):
            out_ref[own, place : place + 1, :] = mod_ref[own, place, 1:2, :]
        out_ref[own, 6:8, :] = jnp.zeros((2, out_ref.shape[2]), F32)


def mod_pair_kernel(first_ref, second_ref, out_ref):
    count = first_ref.shape[0]
    out_ref[0:count] = first_ref[...]
    out_ref[count : 2 * count] = second_ref[...]


def row_mod_kernel(index_ref, near_ref, far_ref, out_ref):
    for row in range(POOL):
        index = index_ref[row]
        within = lax.rem(index, 8)
        values = jnp.where(index < 8, near_ref[within], far_ref[within])
        for place in range(6):
            out_ref[place, row : row + 1, :] = values[place : place + 1]


def total_of(parts):
    return functools.reduce(jnp.add, [part[...].astype(F32) for part in parts])


def embed_norm_kernel(in0, in1, in2, in3, mod_ref, embedded_ref, out_ref):
    total = total_of((in0, in1, in2, in3))
    embedded = total[:, 0:WIDTH].astype(BF16)
    embedded_ref[...] = embedded
    modded = normed(embedded.astype(F32)) * (1.0 + mod_ref[1]) + mod_ref[0]
    out_ref[:, 0:WIDTH] = modded.astype(BF16)
    out_ref[:, WIDTH:] = total[:, WIDTH:].astype(BF16)


def both_norm_kernel(
    image_ref, embedded_ref, in0, in1, in2, in3, img_mod_ref, txt_mod_ref,
    img_ref, txt_ref, out_ref,
):
    projected = total_of((in0, in1, in2, in3))
    gate, shift, scale = img_mod_ref[2:3, :], img_mod_ref[3:4, :], img_mod_ref[4:5, :]
    mixed = (image_ref[...].astype(F32) + gate * projected[0:32]).astype(BF16)
    img_ref[...] = mixed
    out_ref[0:32, :] = (normed(mixed.astype(F32)) * (1.0 + scale) + shift).astype(BF16)
    mixed = (embedded_ref[...].astype(F32) + txt_mod_ref[2] * projected[32:]).astype(BF16)
    txt_ref[...] = mixed
    hidden = normed(mixed.astype(F32)) * (1.0 + txt_mod_ref[4]) + txt_mod_ref[3]
    out_ref[32 : 32 + POOL, :] = hidden.astype(BF16)


def one_hot(line, count):
    shape = (count, line.shape[1])
    return jnp.where(lax.broadcasted_iota(jnp.int32, shape, 0) == line, 1.0, 0.0)


def with_keep(values, keep):
    first = low_half(values.shape)
    return jnp.where(first, values, keep), jnp.where(first, keep, values)


def project(rows, weight_ref):
    both = jnp.concatenate([weight_ref[0], weight_ref[1]], -1)
    first = jnp.dot(rows, both, preferred_element_type=F32)
    return first, jnp.dot(rows, weight_ref[2], preferred_element_type=F32)


def txt_qkv_kernel(
    places_ref, in0, in1, in2, in3, weight_ref, gain_ref, slot_ref, out_ref, low_ref, held, rows_ref
):
    part = in0.shape[0]
    for place, piece in enumerate((in0, in1, in2, in3)):
        rows_ref[place * part : (place + 1) * part, :] = piece[:, 0:WIDTH]
        wide = piece[:, WIDTH:].astype(F32)
        for near in range(SIDE):
            rows = wide[near * POOL : near * POOL + 16]
            start = pl.multiple_of(places_ref[place * SIDE + near] * 32, 32)
            low_ref[pl.ds(start, 16), :] = rows[:, 0:192]
            low_ref[pl.ds(start + 16, 16), :] = rows[:, 256:448]
    projected, values = project(rows_ref[...], weight_ref)
    held[:, 0:128] = head_norm(projected[:, 0:128], gain_ref[0:1, :]).astype(BF16)
    held[:, 128:256] = head_norm(projected[:, 128:256], gain_ref[1:2, :]).astype(BF16)
    held[:, 256:384] = values.astype(BF16)
    hot = one_hot(slot_ref[...], 512)
    keep = jnp.sum(hot, -1, keepdims=True)
    slots = jnp.dot(hot.astype(BF16), held[...], preferred_element_type=F32)
    val0, val1 = with_keep(slots[:, 256:384], keep)
    out_ref[:, 0:256] = slots[:, 0:256].astype(BF16)
    out_ref[:, 256:384] = val0.astype(BF16)
    out_ref[:, 384:512] = val1.astype(BF16)


def img_project_kernel(
    ids_ref, tp_ref, image_hbm, mod_ref, weight_hbm, down_hbm,
    projected_ref, low_ref, own_ref, own_mod_ref, image, weight, down, wide, modded, sems,
):
    copies = [pltpu.make_async_copy(image_hbm, image, sems.at[0])]
    copies.append(pltpu.make_async_copy(weight_hbm, weight, sems.at[1]))
    for own in range(2):
        copies.append(
            pltpu.make_async_copy(down_hbm.at[ids_ref[own]], down.at[own], sems.at[2 + own])
        )
    for copy in copies:
        copy.start()
    copies[0].wait()
    depth = down.shape[1]
    tp = tp_ref[0]
    own_ref[...] = image[pl.ds(pl.multiple_of(tp * 32, 32), 32), :]
    for place in range(6):
        own_mod_ref[place : place + 1, :] = mod_ref[tp // 8, place, 0:1, :]
    for own in range(2):
        for part in range(2):
            rows = image[own * 256 + part * 128 : own * 256 + (part + 1) * 128, :].astype(F32)
            scaled = normed(rows) * (1.0 + mod_ref[own, 1, 0:1, :]) + mod_ref[own, 0, 0:1, :]
            modded[part * 128 : (part + 1) * 128, :] = scaled.astype(BF16)
        if own == 0:
            copies[1].wait()
        copies[2 + own].wait()
        wide[...] = jnp.zeros_like(wide)
        start = pl.multiple_of(tp * depth, 8)
        wide[pl.ds(start, depth), :] = down[own].astype(F32)
        projected, values = project(modded[...], weight)
        projected_ref[own * 256 : (own + 1) * 256, 0:256] = projected
        projected_ref[own * 256 : (own + 1) * 256, 256:384] = values
        low = jnp.dot(modded[...], wide[...].astype(BF16), preferred_element_type=F32)
        for block in range(8):
            low_ref[own * 8 + block] = low[block * 32 : (block + 1) * 32].astype(BF16)


def img_adapt_kernel(ids_ref, low_ref, projected_ref, up_hbm, gain_ref, out_ref, up, lift, sems):
    copies = []
    for own in range(2):
        copies.append(
            pltpu.make_async_copy(up_hbm.at[ids_ref[own]], up.at[own], sems.at[own])
        )
        copies[own].start()
    for own in range(2):
        copies[own].wait()
        lift[...] = jnp.zeros_like(lift)
        for part in range(3):
            lift[part * 64 : (part + 1) * 64, part * 128 : (part + 1) * 128] = up[own, part]
        rows = slice(own * 256, (own + 1) * 256)
        projected = projected_ref[rows, :] + ADAPTER_SCALE * jnp.dot(
            low_ref[rows, :].astype(BF16), lift[...], preferred_element_type=F32
        )
        out_ref[rows, 0:128] = head_norm(projected[:, 0:128], gain_ref[0:1, :]).astype(BF16)
        out_ref[rows, 128:256] = head_norm(projected[:, 128:256], gain_ref[1:2, :]).astype(BF16)
        val0, val1 = with_keep(projected[:, 256:384], 1.0)
        out_ref[rows, 256:384] = val0.astype(BF16)
        out_ref[rows, 384:512] = val1.astype(BF16)


def attend(queries, tokens):
    scaled = queries.astype(F32) * HEAD_DIM ** (-0.5)
    first = low_half(scaled.shape)
    keys = tokens[:, 128:256]
    results = []
    for head in range(2):
        own = jnp.where(first if head == 0 else ~first, scaled, 0.0).astype(BF16)
        scores = lax.dot_general(
            own, keys, (((1,), (1,)), ((), ())), preferred_element_type=F32
        )
        weights = jnp.exp(scores).astype(BF16)
        summed = jnp.dot(
            weights, tokens[:, 256 + head * 128 : 384 + head * 128], preferred_element_type=F32
        )
        results.append(summed / pltpu.roll(summed, HEAD_DIM, 1))
    return jnp.where(first, results[0], results[1]).astype(BF16)


def img_attend_kernel(
    places_ref, img_ref, slot_ref, weight_ref,
    out0, out1, out2, out3, token_ref, tokens, held, ranked,
):
    for own in range(2):
        tokens[own, 0:256, :] = img_ref[own * 256 : (own + 1) * 256, :]
        for source in range(8):
            start = 256 + source * 32
            tokens[own, start : start + 32, :] = slot_ref[source, own * 32 : (own + 1) * 32, :]
    token_ref[...] = tokens[...]
    for own in range(2):
        held[own * 256 : (own + 1) * 256, :] = attend(tokens[own, 0:256, 0:128], tokens[own])
    for place in range(16):
        start = pl.multiple_of(places_ref[place] * 32, 32)
        ranked[place * 32 : (place + 1) * 32, :] = held[pl.ds(start, 32), :]
    result = jnp.dot(ranked[...], weight_ref[...], preferred_element_type=F32)
    for place, out in enumerate((out0, out1, out2, out3)):
        out[...] = result[place * 128 : (place + 1) * 128].astype(BF16)


def txt_attend_kernel(token_ref, out_ref):
    for own in range(2):
        attended = attend(token_ref[own, 256:512, 0:128], token_ref[own])
        for source in range(8):
            start = source * 32
            out_ref[source, own * 32 : (own + 1) * 32, :] = attended[start : start + 32]


def txt_project_kernel(att_ref, slot_ref, weight_ref, out0, out1, out2, out3):
    hot = one_hot(slot_ref[...], 512).astype(BF16)
    rows = lax.dot_general(
        hot, att_ref[...], (((0,), (0,)), ((), ())), preferred_element_type=F32
    ).astype(BF16)
    part = out0.shape[0]
    result = jnp.dot(rows, weight_ref[...], preferred_element_type=F32)
    for place, out in enumerate((out0, out1, out2, out3)):
        out[...] = result[place * part : (place + 1) * part].astype(BF16)


def feed_kernel(in0, in1, in2, in3, win_ref, wout_ref, out0, out1, out2, out3, rows_ref):
    pieces, outs = (in0, in1, in2, in3), (out0, out1, out2, out3)
    width = out0.shape[1]
    for stream, (start, part) in enumerate(((0, 128), (128, SIDE * POOL))):
        for place, piece in enumerate(pieces):
            rows_ref[place * part : (place + 1) * part, :] = piece[start : start + part, :]
        hidden = lax.dot_general(
            rows_ref[0 : SIDE * part, :],
            win_ref[stream],
            (((1,), (1,)), ((), ())),
            preferred_element_type=F32,
        )
        hidden = jax.nn.gelu(hidden, approximate=True).astype(BF16)
        for columns in (slice(0, 1280), slice(1280, width)):
            result = jnp.dot(hidden, wout_ref[stream, :, columns], preferred_element_type=F32)
            for place, out in enumerate(outs):
                out[start : start + part, columns] = result[
                    place * part : (place + 1) * part
                ].astype(BF16)


def img_final_kernel(mixed_ref, in0, in1, in2, in3, mod_ref, out_ref):
    total = total_of((in0, in1, in2, in3))
    out_ref[...] = (mixed_ref[...].astype(F32) + mod_ref[5:6, :] * total).astype(BF16)


def txt_final_kernel(mixed_ref, in0, in1, in2, in3, mod_ref, slot_ref, placed_ref):
    total = total_of((in0, in1, in2, in3))
    rows = mixed_ref[...].astype(F32) + mod_ref[5] * total
    hot = one_hot(slot_ref[:, 0:POOL], 32).astype(BF16)
    placed_ref[...] = jnp.dot(hot, rows.astype(BF16), preferred_element_type=F32).astype(BF16)


def middle(parts):
    rows, width = parts[0].shape
    return run(
        middle_kernel,
        [like((rows // SIDE, width))] * SIDE,
        parts,
        scratch=[pltpu.VMEM((rows, width), F32)],
    )


def both_middle(img_parts, txt_parts):
    rows, width = txt_parts[0].shape
    return run(
        both_middle_kernel,
        [like((32 + POOL, width))] * SIDE,
        (*img_parts, *txt_parts),
        scratch=[pltpu.VMEM((rows, width), F32)],
    )


def join(kernel, parts):
    width = parts[0].shape[1]
    return run(
        kernel,
        like((SIDE * parts[0].shape[0], width)),
        parts,
        scratch=[pltpu.VMEM((SIDE * POOL, width), F32)],
    )


def feed(parts, weight_in, weight_out):
    rows, width = parts[0].shape
    return run(
        feed_kernel,
        [like((rows, width))] * SIDE,
        (*parts, weight_in, weight_out),
        scratch=[pltpu.VMEM((SIDE * 128, width), BF16)],
        flops=rows * SIDE * width * weight_in.shape[1] * 4,
        limit=14,
    )


def shards(
    image,
    prompt_encoder_rows,
    prompt_row_request,
    request_adapter,
    modulation,
    query_key_gain,
    prompt_embed_weight,
    image_query_key_value,
    prompt_query_key_value,
    image_out_weight,
    prompt_out_weight,
    feed_in_weight,
    feed_out_weight,
    adapter_down,
    adapter_up,
):
    grp = lax.axis_index("grp")
    tp = lax.axis_index("tp")
    chip, core = grp // 2, grp % 2
    z, y = tp // SIDE, tp % SIDE
    width = image.shape[1]

    steps = jnp.arange(16)
    far, near = steps // SIDE, steps % SIDE
    places = jnp.where(
        core == 0,
        ((z + far) % SIDE) * SIDE + (y + near) % SIDE,
        ((z + near) % SIDE) * SIDE + (y + far) % SIDE,
    ).astype(jnp.int32)
    gains = jnp.concatenate([query_key_gain, query_key_gain], -1)

    request = prompt_row_request[:, 0]
    outgoing, slots_own = run(
        pack_kernel,
        [like((16, 32, 256)), like((1, 256), jnp.int32)],
        (prompt_encoder_rows, prompt_row_request.reshape(1, POOL)),
        scratch=[pltpu.VMEM((32, 256), F32), pltpu.VMEM((8, 256), jnp.int32)],
    )
    arrived = lax.all_to_all(outgoing, "tp", 0, 0, tiled=True)
    img_projected, low_part, own_image, own_mod = run(
        img_project_kernel,
        [
            like((512, 384), F32),
            like((16, 32, 192)),
            like((32, width)),
            like((6, width), F32),
        ],
        (
            request_adapter,
            tp.reshape(1).astype(jnp.int32),
            image,
            modulation.transpose(0, 2, 1, 3),
            image_query_key_value.transpose(1, 0, 2),
            adapter_down,
        ),
        smem=2,
        scratch=[
            pltpu.VMEM(image.shape, BF16),
            pltpu.VMEM((3, width, 128), BF16),
            pltpu.VMEM((2, *adapter_down.shape[1:]), BF16),
            pltpu.VMEM((width, 192), F32),
            pltpu.VMEM((256, width), BF16),
            pltpu.SemaphoreType.DMA((4,)),
        ],
        flops=512 * width * 576 * 2,
        limit=56,
        after=(outgoing,),
        hbm=(2, 4, 5),
    )
    prompt_mod = run(
        prompt_mod_kernel, like((2, 8, width), F32), (modulation.transpose(0, 2, 1, 3),)
    )
    mod_own = run(
        mod_pair_kernel, like((4, 8, width), F32), (prompt_mod, core_swap(prompt_mod))
    )
    home = request // 4
    row_index = jnp.where(
        home == chip, 0, jnp.where(home == (chip ^ 1), 1, jnp.where(home == 3 - chip, 2, 3))
    )
    row_index = row_index * 4 + (request // 2 % 2 + core) % 2 * 2 + request % 2

    *embed_parts, slots_all = run(
        embed_kernel,
        [like((SIDE * POOL, width + EXTRA))] * SIDE + [like((1, 16 * POOL), jnp.int32)],
        (places, arrived, prompt_embed_weight, low_part),
        smem=1,
        scratch=[pltpu.VMEM((SIDE * POOL, 256), F32), pltpu.VMEM((16, 128), F32)],
        flops=320 * 256 * width * 2,
        after=(mod_own,),
    )
    embed_pieces = exchange(embed_parts, 1)

    embed_sums = exchange(middle(embed_pieces), 0)
    mod_near = run(
        mod_pair_kernel, like((8, 8, width), F32), (mod_own, chip_swap(mod_own, False))
    )
    row_mod = run(
        row_mod_kernel,
        like((6, POOL, width), F32),
        (row_index, mod_near, chip_swap(mod_near, True)),
        smem=1,
    )
    embedded, txt_mod = run(
        embed_norm_kernel,
        [like((POOL, width)), like((POOL, width + EXTRA))],
        (*embed_sums, row_mod),
    )
    txt_mods = spread(join(join_kernel, spread(txt_mod, 0)), 1)

    slot_parts, low = run(
        txt_qkv_kernel,
        [like((512, 512)), like((512, 192), F32)],
        (places, *txt_mods, prompt_query_key_value.transpose(1, 0, 2), gains[1], slots_all),
        smem=1,
        scratch=[pltpu.VMEM((16 * POOL, 384), BF16), pltpu.VMEM((16 * POOL, width), BF16)],
        flops=320 * width * 384 * 2,
        limit=14,
    )
    img_parts = run(
        img_adapt_kernel,
        like((512, 512)),
        (request_adapter, low, img_projected, adapter_up, gains[0]),
        smem=1,
        scratch=[
            pltpu.VMEM((2, 3, 64, 128), BF16),
            pltpu.VMEM((192, 384), BF16),
            pltpu.SemaphoreType.DMA((2,)),
        ],
        flops=512 * 384 * 192 * 2,
        hbm=(3,),
    )
    slot_parts = lax.all_to_all(slot_parts.reshape(8, 64, 512), "grp", 0, 0, tiled=True)

    *img_terms, tokens = run(
        img_attend_kernel,
        [like((128, width))] * SIDE + [like((2, 512, 512))],
        (places, img_parts, slot_parts, image_out_weight),
        smem=1,
        scratch=[
            pltpu.VMEM((2, 512, 512), BF16),
            pltpu.VMEM((512, 128), BF16),
            pltpu.VMEM((512, 128), BF16),
        ],
        flops=1 << 30,
        limit=16,
    )
    img_sums = exchange(img_terms, 1)
    att_parts = run(txt_attend_kernel, like((8, 64, 128)), (tokens,), flops=1 << 29)
    att_parts = lax.all_to_all(att_parts, "grp", 0, 0, tiled=True).reshape(512, 128)
    txt_terms = run(
        txt_project_kernel,
        [like((SIDE * POOL, width))] * SIDE,
        (att_parts, slots_all, prompt_out_weight),
        flops=320 * 128 * width * 2,
        after=(img_sums[1],),
    )
    txt_sums = exchange(txt_terms, 1)

    sums = exchange(both_middle(img_sums, txt_sums), 0)
    mixed_img, mixed_txt, norm_rows = run(
        both_norm_kernel,
        [like((32, width)), like((POOL, width)), like((32 + POOL, width))],
        (own_image, embedded, *sums, own_mod, row_mod),
    )
    rows = spread(join(both_join_kernel, spread(norm_rows, 0)), 1)
    weight_in = feed_in_weight.transpose(0, 2, 1)
    pieces = exchange(feed(rows, weight_in, feed_out_weight), 1)
    parts = run(
        part_middle_kernel,
        [like((POOL, width))] * SIDE + [like((32, width))] * SIDE,
        pieces,
        scratch=[pltpu.VMEM((SIDE * POOL, width), F32)],
    )

    placed = run(
        txt_final_kernel,
        like((32, width)),
        (mixed_txt, *exchange(parts[:SIDE], 0), row_mod, slots_own),
    )
    image_out = run(
        img_final_kernel, like((32, width)), (mixed_img, *exchange(parts[SIDE:], 0), own_mod)
    )
    placed = lax.all_to_all(placed.reshape(8, 4, width), "grp", 0, 0, tiled=True)
    prompt_out = placed.reshape(32, width)

    return (image_out, prompt_out)


def solution(mesh):
    placed = (
        P("grp", None),
        P(("grp", "tp"), None),
        P(("grp", "tp"), None),
        P("grp"),
        P("grp", None, None, None),
        P(),
        P("tp", None),
        P(None, None, "tp"),
        P(None, None, "tp"),
        P("tp", None),
        P("tp", None),
        P(None, None, "tp"),
        P(None, "tp", None),
        P(None, "tp", None),
        P(None, None, None, "tp"),
    )
    return jax.shard_map(
        shards,
        mesh=mesh,
        in_specs=placed,
        out_specs=(P(("grp", "tp"), None), P(("grp", "tp"), None)),
        check_vma=False,
    )
```

```python
import functools

import jax
import jax.numpy as jnp
from jax import lax
from jax.experimental import pallas as pl
from jax.experimental.pallas import tpu as pltpu
from jax.sharding import PartitionSpec as P

HEAD_DIM = 64
CAP = 2
EPSILON = 1e-06
ADAPTER_SCALE = 0.5
SIDE = 4
POOL = 20
WIDTH = 2432
EXTRA = 512
F32 = jnp.float32
BF16 = jnp.bfloat16


def torus_shift(values, stage, step):
    pairs = []
    for grp in range(8):
        for tp in range(16):
            z, y = divmod(tp, SIDE)
            if (grp + stage) % 2 == 0:
                y = (y + step) % SIDE
            else:
                z = (z + step) % SIDE
            pairs.append((grp * 16 + tp, grp * 16 + z * SIDE + y))
    return lax.ppermute(values, ("grp", "tp"), pairs)


def core_swap(values):
    return lax.ppermute(values, "grp", [(grp, grp ^ 1) for grp in range(8)])


def chip_swap(values, far):
    pairs = []
    for grp in range(8):
        chip = 3 - grp // 2 if far else (grp // 2) ^ 1
        pairs.append((grp, chip * 2 + grp % 2))
    return lax.ppermute(values, "grp", pairs)


def spread(rows, stage):
    return [
        rows,
        torus_shift(rows, stage, -1),
        torus_shift(rows, stage, 2),
        torus_shift(rows, stage, 1),
    ]


def exchange(parts, stage):
    return [
        parts[0],
        torus_shift(parts[3], stage, -1),
        torus_shift(parts[2], stage, 2),
        torus_shift(parts[1], stage, 1),
    ]


def run(kernel, outs, args, smem=0, scratch=(), flops=0, limit=8, after=(), hbm=()):
    count = len(args)
    spaces = [pltpu.SMEM] * smem + [pltpu.VMEM] * (count - smem)
    for index in hbm:
        spaces[index] = pl.ANY
    specs = [pl.BlockSpec(memory_space=space) for space in spaces]
    specs += [pl.BlockSpec(memory_space=pl.ANY)] * len(after)
    single = not isinstance(outs, list)
    shapes = [outs] if single else outs
    moved = sum(a.size * a.dtype.itemsize for a in args)
    moved += sum(s.size * s.dtype.itemsize for s in shapes)

    def body(*refs):
        kernel(*refs[:count], *refs[count + len(after) :])

    result = pl.pallas_call(
        body,
        out_shape=shapes,
        in_specs=specs,
        out_specs=[pl.BlockSpec(memory_space=pltpu.VMEM)] * len(shapes),
        scratch_shapes=list(scratch),
        compiler_params=pltpu.CompilerParams(vmem_limit_bytes=limit << 20),
        cost_estimate=pl.CostEstimate(flops=flops, bytes_accessed=moved, transcendentals=0),
    )(*args, *after)
    return result[0] if single else result


def like(shape, dtype=BF16):
    return jax.ShapeDtypeStruct(shape, dtype)


def normed(values):
    centred = values - jnp.mean(values, -1, keepdims=True)
    return centred * lax.rsqrt(jnp.mean(centred * centred, -1, keepdims=True) + EPSILON)


def low_half(shape):
    return lax.broadcasted_iota(jnp.int32, shape, len(shape) - 1) < HEAD_DIM


def head_norm(values, gains):
    first = low_half(values.shape)
    squares = values * values
    head0 = jnp.sum(jnp.where(first, squares, 0.0), -1, keepdims=True)
    head1 = jnp.sum(jnp.where(first, 0.0, squares), -1, keepdims=True)
    scale = jnp.where(
        first,
        lax.rsqrt(head0 * (1.0 / HEAD_DIM) + EPSILON),
        lax.rsqrt(head1 * (1.0 / HEAD_DIM) + EPSILON),
    )
    return values * scale * gains


def pack_kernel(rows_ref, line_ref, out_ref, slot_ref, held, wide):
    wide[...] = jnp.full(wide.shape, -1, jnp.int32)
    wide[0:1, 0:POOL] = line_ref[...]
    line = wide[0:1, :]
    first = lax.broadcasted_iota(jnp.int32, (POOL, 256), 0)
    second = lax.broadcasted_iota(jnp.int32, (POOL, 256), 1)
    column = jnp.sum(jnp.where(first == second, line, 0), 1, keepdims=True)
    rank = jnp.sum(jnp.where((column == line) & (first < second), 1, 0), 0, keepdims=True)
    slot_ref[...] = line * CAP + rank
    held[...] = jnp.zeros_like(held)
    held[POOL : POOL + 1, :] = (line * CAP + rank).astype(F32)
    for block in range(16):
        held[0:POOL, :] = rows_ref[:, block * 256 : (block + 1) * 256].astype(F32)
        out_ref[block] = held[...].astype(BF16)


def embed_kernel(
    places_ref, arrived_ref, weight_ref, low_ref, out0, out1, out2, out3, slot_ref, held, label
):
    for far, out in enumerate((out0, out1, out2, out3)):
        for near in range(SIDE):
            place = far * SIDE + near
            block = arrived_ref[places_ref[place]].astype(F32)
            held[near * POOL : (near + 1) * POOL, :] = block[0:POOL]
            label[place : place + 1, :] = block[POOL : POOL + 1, 0:128]
        out[:, 0:WIDTH] = jnp.dot(
            held[...].astype(BF16), weight_ref[...], preferred_element_type=F32
        ).astype(BF16)
        out[:, WIDTH:] = jnp.zeros((SIDE * POOL, EXTRA), BF16)
        for near in range(SIDE):
            left = WIDTH + near // 2 * 256
            top = near % 2 * 32
            out[top : top + 32, left : left + 192] = low_ref[places_ref[far * SIDE + near]]
    line = (128, 16 * POOL)
    offset = lax.broadcasted_iota(jnp.int32, line, 1) - lax.broadcasted_iota(jnp.int32, line, 0)
    taken = offset == 0
    for place in range(1, 16):
        taken = taken | (offset == place * POOL)
    taken = taken & (lax.broadcasted_iota(jnp.int32, line, 0) < POOL)
    spot = jnp.dot(
        label[...].astype(BF16),
        jnp.where(taken, 1.0, 0.0).astype(BF16),
        preferred_element_type=F32,
    )
    place = lax.broadcasted_iota(jnp.int32, spot.shape, 0)
    start = place * POOL
    column = lax.broadcasted_iota(jnp.int32, spot.shape, 1)
    inside = (column >= start) & (column < start + POOL)
    target = jnp.sum(jnp.where(inside, spot, 0.0), 0, keepdims=True).astype(jnp.int32)
    block = jnp.sum(jnp.where(inside, place, 0), 0, keepdims=True)
    slot_ref[...] = (
        (target >> 2) * 64 + ((target >> 1) & 1) * 32 + (target & 1) + 2 * block
    )


def middle_kernel(in0, in1, in2, in3, out0, out1, out2, out3, held):
    held[...] = total_of((in0, in1, in2, in3))
    for near, out in enumerate((out0, out1, out2, out3)):
        out[:, 0:WIDTH] = held[near * POOL : (near + 1) * POOL, 0:WIDTH].astype(BF16)
        left = WIDTH + near // 2 * 256
        for half in range(2):
            top = near % 2 * 32 + half * 16
            out[0:16, WIDTH + half * 256 : WIDTH + half * 256 + 256] = held[
                top : top + 16, left : left + 256
            ].astype(BF16)
        out[16:POOL, WIDTH:] = jnp.zeros((POOL - 16, EXTRA), BF16)


def both_middle_kernel(*refs):
    img, txt, outs, held = refs[0:4], refs[4:8], refs[8:12], refs[12]
    held[...] = total_of(txt)
    for near, out in enumerate(outs):
        rows = slice(near * 32, (near + 1) * 32)
        out[0:32, :] = functools.reduce(
            jnp.add, [piece[rows, :].astype(F32) for piece in img]
        ).astype(BF16)
        out[32 : 32 + POOL, :] = held[near * POOL : (near + 1) * POOL, :].astype(BF16)


def part_middle_kernel(
    in0, in1, in2, in3, txt0, txt1, txt2, txt3, img0, img1, img2, img3, held
):
    pieces = (in0, in1, in2, in3)
    held[...] = functools.reduce(jnp.add, [piece[128:, :].astype(F32) for piece in pieces])
    for near, out in enumerate((txt0, txt1, txt2, txt3)):
        out[...] = held[near * POOL : (near + 1) * POOL, :].astype(BF16)
    for near, out in enumerate((img0, img1, img2, img3)):
        rows = slice(near * 32, (near + 1) * 32)
        out[...] = functools.reduce(
            jnp.add, [piece[rows, :].astype(F32) for piece in pieces]
        ).astype(BF16)


def join_kernel(in0, in1, in2, in3, out_ref, held):
    for place, piece in enumerate((in0, in1, in2, in3)):
        held[place * POOL : (place + 1) * POOL, :] = piece[...].astype(F32)
    out_ref[...] = held[...].astype(BF16)


def both_join_kernel(in0, in1, in2, in3, out_ref, held):
    for place, piece in enumerate((in0, in1, in2, in3)):
        out_ref[place * 32 : (place + 1) * 32, :] = piece[0:32, :]
        held[place * POOL : (place + 1) * POOL, :] = piece[32:, :].astype(F32)
    out_ref[128:, :] = held[...].astype(BF16)


def prompt_mod_kernel(mod_ref, out_ref):
    for own in range(2):
        for place in range(6):
            out_ref[own, place : place + 1, :] = mod_ref[own, place, 1:2, :]
        out_ref[own, 6:8, :] = jnp.zeros((2, out_ref.shape[2]), F32)


def mod_pair_kernel(first_ref, second_ref, out_ref):
    count = first_ref.shape[0]
    out_ref[0:count] = first_ref[...]
    out_ref[count : 2 * count] = second_ref[...]


def row_mod_kernel(index_ref, near_ref, far_ref, out_ref):
    for row in range(POOL):
        index = index_ref[row]
        within = lax.rem(index, 8)
        values = jnp.where(index < 8, near_ref[within], far_ref[within])
        for place in range(6):
            out_ref[place, row : row + 1, :] = values[place : place + 1]


def total_of(parts):
    return functools.reduce(jnp.add, [part[...].astype(F32) for part in parts])


def embed_norm_kernel(in0, in1, in2, in3, mod_ref, embedded_ref, out_ref):
    total = total_of((in0, in1, in2, in3))
    embedded = total[:, 0:WIDTH].astype(BF16)
    embedded_ref[...] = embedded
    modded = normed(embedded.astype(F32)) * (1.0 + mod_ref[1]) + mod_ref[0]
    out_ref[:, 0:WIDTH] = modded.astype(BF16)
    out_ref[:, WIDTH:] = total[:, WIDTH:].astype(BF16)


def both_norm_kernel(
    image_ref, embedded_ref, in0, in1, in2, in3, img_mod_ref, txt_mod_ref,
    img_ref, txt_ref, out_ref,
):
    projected = total_of((in0, in1, in2, in3))
    gate, shift, scale = img_mod_ref[2:3, :], img_mod_ref[3:4, :], img_mod_ref[4:5, :]
    mixed = (image_ref[...].astype(F32) + gate * projected[0:32]).astype(BF16)
    img_ref[...] = mixed
    out_ref[0:32, :] = (normed(mixed.astype(F32)) * (1.0 + scale) + shift).astype(BF16)
    mixed = (embedded_ref[...].astype(F32) + txt_mod_ref[2] * projected[32:]).astype(BF16)
    txt_ref[...] = mixed
    hidden = normed(mixed.astype(F32)) * (1.0 + txt_mod_ref[4]) + txt_mod_ref[3]
    out_ref[32 : 32 + POOL, :] = hidden.astype(BF16)


def one_hot(line, count):
    shape = (count, line.shape[1])
    return jnp.where(lax.broadcasted_iota(jnp.int32, shape, 0) == line, 1.0, 0.0)


def with_keep(values, keep):
    first = low_half(values.shape)
    return jnp.where(first, values, keep), jnp.where(first, keep, values)


def project(rows, weight_ref):
    both = jnp.concatenate([weight_ref[0], weight_ref[1]], -1)
    first = jnp.dot(rows, both, preferred_element_type=F32)
    return first, jnp.dot(rows, weight_ref[2], preferred_element_type=F32)


def txt_qkv_kernel(
    places_ref, in0, in1, in2, in3, weight_ref, gain_ref, slot_ref, out_ref, low_ref, held, rows_ref
):
    part = in0.shape[0]
    for place, piece in enumerate((in0, in1, in2, in3)):
        rows_ref[place * part : (place + 1) * part, :] = piece[:, 0:WIDTH]
        wide = piece[:, WIDTH:].astype(F32)
        for near in range(SIDE):
            rows = wide[near * POOL : near * POOL + 16]
            start = pl.multiple_of(places_ref[place * SIDE + near] * 32, 32)
            low_ref[pl.ds(start, 16), :] = rows[:, 0:192]
            low_ref[pl.ds(start + 16, 16), :] = rows[:, 256:448]
    projected, values = project(rows_ref[...], weight_ref)
    held[:, 0:128] = head_norm(projected[:, 0:128], gain_ref[0:1, :]).astype(BF16)
    held[:, 128:256] = head_norm(projected[:, 128:256], gain_ref[1:2, :]).astype(BF16)
    held[:, 256:384] = values.astype(BF16)
    hot = one_hot(slot_ref[...], 512)
    keep = jnp.sum(hot, -1, keepdims=True)
    slots = jnp.dot(hot.astype(BF16), held[...], preferred_element_type=F32)
    val0, val1 = with_keep(slots[:, 256:384], keep)
    out_ref[:, 0:256] = slots[:, 0:256].astype(BF16)
    out_ref[:, 256:384] = val0.astype(BF16)
    out_ref[:, 384:512] = val1.astype(BF16)


def img_project_kernel(
    ids_ref, tp_ref, image_hbm, mod_ref, weight_hbm, down_hbm,
    projected_ref, low_ref, own_ref, own_mod_ref, image, weight, down, wide, modded, sems,
):
    copies = [pltpu.make_async_copy(image_hbm, image, sems.at[0])]
    copies.append(pltpu.make_async_copy(weight_hbm, weight, sems.at[1]))
    for own in range(2):
        copies.append(
            pltpu.make_async_copy(down_hbm.at[ids_ref[own]], down.at[own], sems.at[2 + own])
        )
    for copy in copies:
        copy.start()
    copies[0].wait()
    depth = down.shape[1]
    tp = tp_ref[0]
    own_ref[...] = image[pl.ds(pl.multiple_of(tp * 32, 32), 32), :]
    for place in range(6):
        own_mod_ref[place : place + 1, :] = mod_ref[tp // 8, place, 0:1, :]
    for own in range(2):
        for part in range(2):
            rows = image[own * 256 + part * 128 : own * 256 + (part + 1) * 128, :].astype(F32)
            scaled = normed(rows) * (1.0 + mod_ref[own, 1, 0:1, :]) + mod_ref[own, 0, 0:1, :]
            modded[part * 128 : (part + 1) * 128, :] = scaled.astype(BF16)
        if own == 0:
            copies[1].wait()
        copies[2 + own].wait()
        wide[...] = jnp.zeros_like(wide)
        start = pl.multiple_of(tp * depth, 8)
        wide[pl.ds(start, depth), :] = down[own].astype(F32)
        projected, values = project(modded[...], weight)
        projected_ref[own * 256 : (own + 1) * 256, 0:256] = projected
        projected_ref[own * 256 : (own + 1) * 256, 256:384] = values
        low = jnp.dot(modded[...], wide[...].astype(BF16), preferred_element_type=F32)
        for block in range(8):
            low_ref[own * 8 + block] = low[block * 32 : (block + 1) * 32].astype(BF16)


def img_adapt_kernel(ids_ref, low_ref, projected_ref, up_hbm, gain_ref, out_ref, up, lift, sems):
    copies = []
    for own in range(2):
        copies.append(
            pltpu.make_async_copy(up_hbm.at[ids_ref[own]], up.at[own], sems.at[own])
        )
        copies[own].start()
    for own in range(2):
        copies[own].wait()
        lift[...] = jnp.zeros_like(lift)
        for part in range(3):
            lift[part * 64 : (part + 1) * 64, part * 128 : (part + 1) * 128] = up[own, part]
        rows = slice(own * 256, (own + 1) * 256)
        projected = projected_ref[rows, :] + ADAPTER_SCALE * jnp.dot(
            low_ref[rows, :].astype(BF16), lift[...], preferred_element_type=F32
        )
        out_ref[rows, 0:128] = head_norm(projected[:, 0:128], gain_ref[0:1, :]).astype(BF16)
        out_ref[rows, 128:256] = head_norm(projected[:, 128:256], gain_ref[1:2, :]).astype(BF16)
        val0, val1 = with_keep(projected[:, 256:384], 1.0)
        out_ref[rows, 256:384] = val0.astype(BF16)
        out_ref[rows, 384:512] = val1.astype(BF16)


def attend(queries, tokens):
    scaled = queries.astype(F32) * HEAD_DIM ** (-0.5)
    first = low_half(scaled.shape)
    keys = tokens[:, 128:256]
    results = []
    for head in range(2):
        own = jnp.where(first if head == 0 else ~first, scaled, 0.0).astype(BF16)
        scores = lax.dot_general(
            own, keys, (((1,), (1,)), ((), ())), preferred_element_type=F32
        )
        weights = jnp.exp(scores).astype(BF16)
        summed = jnp.dot(
            weights, tokens[:, 256 + head * 128 : 384 + head * 128], preferred_element_type=F32
        )
        results.append(summed / pltpu.roll(summed, HEAD_DIM, 1))
    return jnp.where(first, results[0], results[1]).astype(BF16)


def img_attend_kernel(
    places_ref, img_ref, slot_ref, weight_ref,
    out0, out1, out2, out3, token_ref, tokens, held, ranked,
):
    for own in range(2):
        tokens[own, 0:256, :] = img_ref[own * 256 : (own + 1) * 256, :]
        for source in range(8):
            start = 256 + source * 32
            tokens[own, start : start + 32, :] = slot_ref[source, own * 32 : (own + 1) * 32, :]
    token_ref[...] = tokens[...]
    for own in range(2):
        held[own * 256 : (own + 1) * 256, :] = attend(tokens[own, 0:256, 0:128], tokens[own])
    for place in range(16):
        start = pl.multiple_of(places_ref[place] * 32, 32)
        ranked[place * 32 : (place + 1) * 32, :] = held[pl.ds(start, 32), :]
    result = jnp.dot(ranked[...], weight_ref[...], preferred_element_type=F32)
    for place, out in enumerate((out0, out1, out2, out3)):
        out[...] = result[place * 128 : (place + 1) * 128].astype(BF16)


def txt_attend_kernel(token_ref, out_ref):
    for own in range(2):
        attended = attend(token_ref[own, 256:512, 0:128], token_ref[own])
        for source in range(8):
            start = source * 32
            out_ref[source, own * 32 : (own + 1) * 32, :] = attended[start : start + 32]


def txt_project_kernel(att_ref, slot_ref, weight_ref, out0, out1, out2, out3):
    hot = one_hot(slot_ref[...], 512).astype(BF16)
    rows = lax.dot_general(
        hot, att_ref[...], (((0,), (0,)), ((), ())), preferred_element_type=F32
    ).astype(BF16)
    part = out0.shape[0]
    result = jnp.dot(rows, weight_ref[...], preferred_element_type=F32)
    for place, out in enumerate((out0, out1, out2, out3)):
        out[...] = result[place * part : (place + 1) * part].astype(BF16)


def feed_kernel(*refs):
    rows_ref = refs[-1]
    count = (len(refs) - 3) // 2
    pieces, outs = refs[0:count], refs[count + 2 : 2 * count + 2]
    win_ref, wout_ref = refs[count], refs[count + 1]
    width = outs[0].shape[1]
    for stream, (start, part) in enumerate(((0, 128), (128, SIDE * POOL))):
        for place, piece in enumerate(pieces):
            rows_ref[place * part : (place + 1) * part, :] = piece[start : start + part, :]
        hidden = lax.dot_general(
            rows_ref[0 : count * part, :],
            win_ref[stream],
            (((1,), (1,)), ((), ())),
            preferred_element_type=F32,
        )
        hidden = jax.nn.gelu(hidden, approximate=True).astype(BF16)
        for columns in (slice(0, 1280), slice(1280, width)):
            result = jnp.dot(hidden, wout_ref[stream, :, columns], preferred_element_type=F32)
            for place, out in enumerate(outs):
                out[start : start + part, columns] = result[
                    place * part : (place + 1) * part
                ].astype(BF16)


def img_final_kernel(mixed_ref, in0, in1, in2, in3, mod_ref, out_ref):
    total = total_of((in0, in1, in2, in3))
    out_ref[...] = (mixed_ref[...].astype(F32) + mod_ref[5:6, :] * total).astype(BF16)


def txt_final_kernel(mixed_ref, in0, in1, in2, in3, mod_ref, slot_ref, placed_ref):
    total = total_of((in0, in1, in2, in3))
    rows = mixed_ref[...].astype(F32) + mod_ref[5] * total
    hot = one_hot(slot_ref[:, 0:POOL], 32).astype(BF16)
    placed_ref[...] = jnp.dot(hot, rows.astype(BF16), preferred_element_type=F32).astype(BF16)


def middle(parts):
    rows, width = parts[0].shape
    return run(
        middle_kernel,
        [like((rows // SIDE, width))] * SIDE,
        parts,
        scratch=[pltpu.VMEM((rows, width), F32)],
    )


def both_middle(img_parts, txt_parts):
    rows, width = txt_parts[0].shape
    return run(
        both_middle_kernel,
        [like((32 + POOL, width))] * SIDE,
        (*img_parts, *txt_parts),
        scratch=[pltpu.VMEM((rows, width), F32)],
    )


def join(kernel, parts):
    width = parts[0].shape[1]
    return run(
        kernel,
        like((SIDE * parts[0].shape[0], width)),
        parts,
        scratch=[pltpu.VMEM((SIDE * POOL, width), F32)],
    )


def feed(parts, weight_in, weight_out, after=()):
    rows, width = parts[0].shape
    return run(
        feed_kernel,
        [like((rows, width))] * len(parts),
        (*parts, weight_in, weight_out),
        scratch=[pltpu.VMEM((len(parts) * 128, width), BF16)],
        flops=rows * len(parts) * width * weight_in.shape[1] * 4,
        limit=14,
        after=after,
    )


def shards(
    image,
    prompt_encoder_rows,
    prompt_row_request,
    request_adapter,
    modulation,
    query_key_gain,
    prompt_embed_weight,
    image_query_key_value,
    prompt_query_key_value,
    image_out_weight,
    prompt_out_weight,
    feed_in_weight,
    feed_out_weight,
    adapter_down,
    adapter_up,
):
    grp = lax.axis_index("grp")
    tp = lax.axis_index("tp")
    chip, core = grp // 2, grp % 2
    z, y = tp // SIDE, tp % SIDE
    width = image.shape[1]

    steps = jnp.arange(16)
    far, near = steps // SIDE, steps % SIDE
    places = jnp.where(
        core == 0,
        ((z + far) % SIDE) * SIDE + (y + near) % SIDE,
        ((z + near) % SIDE) * SIDE + (y + far) % SIDE,
    ).astype(jnp.int32)
    gains = jnp.concatenate([query_key_gain, query_key_gain], -1)

    request = prompt_row_request[:, 0]
    outgoing, slots_own = run(
        pack_kernel,
        [like((16, 32, 256)), like((1, 256), jnp.int32)],
        (prompt_encoder_rows, prompt_row_request.reshape(1, POOL)),
        scratch=[pltpu.VMEM((32, 256), F32), pltpu.VMEM((8, 256), jnp.int32)],
    )
    arrived = lax.all_to_all(outgoing, "tp", 0, 0, tiled=True)
    img_projected, low_part, own_image, own_mod = run(
        img_project_kernel,
        [
            like((512, 384), F32),
            like((16, 32, 192)),
            like((32, width)),
            like((6, width), F32),
        ],
        (
            request_adapter,
            tp.reshape(1).astype(jnp.int32),
            image,
            modulation.transpose(0, 2, 1, 3),
            image_query_key_value.transpose(1, 0, 2),
            adapter_down,
        ),
        smem=2,
        scratch=[
            pltpu.VMEM(image.shape, BF16),
            pltpu.VMEM((3, width, 128), BF16),
            pltpu.VMEM((2, *adapter_down.shape[1:]), BF16),
            pltpu.VMEM((width, 192), F32),
            pltpu.VMEM((256, width), BF16),
            pltpu.SemaphoreType.DMA((4,)),
        ],
        flops=512 * width * 576 * 2,
        limit=56,
        after=(outgoing,),
        hbm=(2, 4, 5),
    )
    prompt_mod = run(
        prompt_mod_kernel, like((2, 8, width), F32), (modulation.transpose(0, 2, 1, 3),),
        after=(outgoing,),
    )
    mod_own = run(
        mod_pair_kernel, like((4, 8, width), F32), (prompt_mod, core_swap(prompt_mod))
    )
    home = request // 4
    row_index = jnp.where(
        home == chip, 0, jnp.where(home == (chip ^ 1), 1, jnp.where(home == 3 - chip, 2, 3))
    )
    row_index = row_index * 4 + (request // 2 % 2 + core) % 2 * 2 + request % 2

    *embed_parts, slots_all = run(
        embed_kernel,
        [like((SIDE * POOL, width + EXTRA))] * SIDE + [like((1, 16 * POOL), jnp.int32)],
        (places, arrived, prompt_embed_weight, low_part),
        smem=1,
        scratch=[pltpu.VMEM((SIDE * POOL, 256), F32), pltpu.VMEM((16, 128), F32)],
        flops=320 * 256 * width * 2,
        after=(mod_own,),
    )
    embed_pieces = exchange(embed_parts, 1)

    embed_sums = exchange(middle(embed_pieces), 0)
    mod_near = run(
        mod_pair_kernel, like((8, 8, width), F32), (mod_own, chip_swap(mod_own, False))
    )
    row_mod = run(
        row_mod_kernel,
        like((6, POOL, width), F32),
        (row_index, mod_near, chip_swap(mod_near, True)),
        smem=1,
    )
    embedded, txt_mod = run(
        embed_norm_kernel,
        [like((POOL, width)), like((POOL, width + EXTRA))],
        (*embed_sums, row_mod),
    )
    txt_mods = spread(join(join_kernel, spread(txt_mod, 0)), 1)

    slot_parts, low = run(
        txt_qkv_kernel,
        [like((512, 512)), like((512, 192), F32)],
        (places, *txt_mods, prompt_query_key_value.transpose(1, 0, 2), gains[1], slots_all),
        smem=1,
        scratch=[pltpu.VMEM((16 * POOL, 384), BF16), pltpu.VMEM((16 * POOL, width), BF16)],
        flops=320 * width * 384 * 2,
        limit=14,
    )
    img_parts = run(
        img_adapt_kernel,
        like((512, 512)),
        (request_adapter, low, img_projected, adapter_up, gains[0]),
        smem=1,
        scratch=[
            pltpu.VMEM((2, 3, 64, 128), BF16),
            pltpu.VMEM((192, 384), BF16),
            pltpu.SemaphoreType.DMA((2,)),
        ],
        flops=512 * 384 * 192 * 2,
        hbm=(3,),
    )
    slot_parts = lax.all_to_all(slot_parts.reshape(8, 64, 512), "grp", 0, 0, tiled=True)

    *img_terms, tokens = run(
        img_attend_kernel,
        [like((128, width))] * SIDE + [like((2, 512, 512))],
        (places, img_parts, slot_parts, image_out_weight),
        smem=1,
        scratch=[
            pltpu.VMEM((2, 512, 512), BF16),
            pltpu.VMEM((512, 128), BF16),
            pltpu.VMEM((512, 128), BF16),
        ],
        flops=1 << 30,
        limit=16,
    )
    img_sums = exchange(img_terms, 1)
    att_parts = run(txt_attend_kernel, like((8, 64, 128)), (tokens,), flops=1 << 29)
    att_parts = lax.all_to_all(att_parts, "grp", 0, 0, tiled=True).reshape(512, 128)
    txt_terms = run(
        txt_project_kernel,
        [like((SIDE * POOL, width))] * SIDE,
        (att_parts, slots_all, prompt_out_weight),
        flops=320 * 128 * width * 2,
        after=(img_sums[1],),
    )
    txt_sums = exchange(txt_terms, 1)

    sums = exchange(both_middle(img_sums, txt_sums), 0)
    mixed_img, mixed_txt, norm_rows = run(
        both_norm_kernel,
        [like((32, width)), like((POOL, width)), like((32 + POOL, width))],
        (own_image, embedded, *sums, own_mod, row_mod),
    )
    rows = spread(join(both_join_kernel, spread(norm_rows, 0)), 1)
    weight_in = feed_in_weight.transpose(0, 2, 1)
    own_term = feed(rows[:1], weight_in, feed_out_weight)
    terms = feed(rows[1:], weight_in, feed_out_weight, after=(own_term[0],))
    pieces = exchange([*own_term, *terms], 1)
    parts = run(
        part_middle_kernel,
        [like((POOL, width))] * SIDE + [like((32, width))] * SIDE,
        pieces,
        scratch=[pltpu.VMEM((SIDE * POOL, width), F32)],
    )

    placed = run(
        txt_final_kernel,
        like((32, width)),
        (mixed_txt, *exchange(parts[:SIDE], 0), row_mod, slots_own),
    )
    image_out = run(
        img_final_kernel, like((32, width)), (mixed_img, *exchange(parts[SIDE:], 0), own_mod)
    )
    placed = lax.all_to_all(placed.reshape(8, 4, width), "grp", 0, 0, tiled=True)
    prompt_out = placed.reshape(32, width)

    return (image_out, prompt_out)


def solution(mesh):
    placed = (
        P("grp", None),
        P(("grp", "tp"), None),
        P(("grp", "tp"), None),
        P("grp"),
        P("grp", None, None, None),
        P(),
        P("tp", None),
        P(None, None, "tp"),
        P(None, None, "tp"),
        P("tp", None),
        P("tp", None),
        P(None, None, "tp"),
        P(None, "tp", None),
        P(None, "tp", None),
        P(None, None, None, "tp"),
    )
    return jax.shard_map(
        shards,
        mesh=mesh,
        in_specs=placed,
        out_specs=(P(("grp", "tp"), None), P(("grp", "tp"), None)),
        check_vma=False,
    )
```

```python
import functools

import jax
import jax.numpy as jnp
from jax import lax
from jax.experimental import pallas as pl
from jax.experimental.pallas import tpu as pltpu
from jax.sharding import PartitionSpec as P

HEAD_DIM = 64
CAP = 2
EPSILON = 1e-06
ADAPTER_SCALE = 0.5
SIDE = 4
POOL = 20
WIDTH = 2432
EXTRA = 512
F32 = jnp.float32
BF16 = jnp.bfloat16


def torus_shift(values, stage, step):
    pairs = []
    for grp in range(8):
        for tp in range(16):
            z, y = divmod(tp, SIDE)
            if (grp + stage) % 2 == 0:
                y = (y + step) % SIDE
            else:
                z = (z + step) % SIDE
            pairs.append((grp * 16 + tp, grp * 16 + z * SIDE + y))
    return lax.ppermute(values, ("grp", "tp"), pairs)


def core_swap(values):
    return lax.ppermute(values, "grp", [(grp, grp ^ 1) for grp in range(8)])


def chip_swap(values, far):
    pairs = []
    for grp in range(8):
        chip = 3 - grp // 2 if far else (grp // 2) ^ 1
        pairs.append((grp, chip * 2 + grp % 2))
    return lax.ppermute(values, "grp", pairs)


def spread(rows, stage):
    return [
        rows,
        torus_shift(rows, stage, -1),
        torus_shift(rows, stage, 2),
        torus_shift(rows, stage, 1),
    ]


def exchange(parts, stage):
    return [
        parts[0],
        torus_shift(parts[3], stage, -1),
        torus_shift(parts[2], stage, 2),
        torus_shift(parts[1], stage, 1),
    ]


def run(kernel, outs, args, smem=0, scratch=(), flops=0, limit=8, after=(), hbm=()):
    count = len(args)
    spaces = [pltpu.SMEM] * smem + [pltpu.VMEM] * (count - smem)
    for index in hbm:
        spaces[index] = pl.ANY
    specs = [pl.BlockSpec(memory_space=space) for space in spaces]
    specs += [pl.BlockSpec(memory_space=pl.ANY)] * len(after)
    single = not isinstance(outs, list)
    shapes = [outs] if single else outs
    moved = sum(a.size * a.dtype.itemsize for a in args)
    moved += sum(s.size * s.dtype.itemsize for s in shapes)

    def body(*refs):
        kernel(*refs[:count], *refs[count + len(after) :])

    result = pl.pallas_call(
        body,
        out_shape=shapes,
        in_specs=specs,
        out_specs=[pl.BlockSpec(memory_space=pltpu.VMEM)] * len(shapes),
        scratch_shapes=list(scratch),
        compiler_params=pltpu.CompilerParams(vmem_limit_bytes=limit << 20),
        cost_estimate=pl.CostEstimate(flops=flops, bytes_accessed=moved, transcendentals=0),
    )(*args, *after)
    return result[0] if single else result


def like(shape, dtype=BF16):
    return jax.ShapeDtypeStruct(shape, dtype)


def normed(values):
    centred = values - jnp.mean(values, -1, keepdims=True)
    return centred * lax.rsqrt(jnp.mean(centred * centred, -1, keepdims=True) + EPSILON)


def low_half(shape):
    return lax.broadcasted_iota(jnp.int32, shape, len(shape) - 1) < HEAD_DIM


def head_norm(values, gains):
    first = low_half(values.shape)
    squares = values * values
    head0 = jnp.sum(jnp.where(first, squares, 0.0), -1, keepdims=True)
    head1 = jnp.sum(jnp.where(first, 0.0, squares), -1, keepdims=True)
    scale = jnp.where(
        first,
        lax.rsqrt(head0 * (1.0 / HEAD_DIM) + EPSILON),
        lax.rsqrt(head1 * (1.0 / HEAD_DIM) + EPSILON),
    )
    return values * scale * gains


def pack_kernel(rows_ref, line_ref, out_ref, slot_ref, held, wide):
    wide[...] = jnp.full(wide.shape, -1, jnp.int32)
    wide[0:1, 0:POOL] = line_ref[...]
    line = wide[0:1, :]
    first = lax.broadcasted_iota(jnp.int32, (POOL, 256), 0)
    second = lax.broadcasted_iota(jnp.int32, (POOL, 256), 1)
    column = jnp.sum(jnp.where(first == second, line, 0), 1, keepdims=True)
    rank = jnp.sum(jnp.where((column == line) & (first < second), 1, 0), 0, keepdims=True)
    slot_ref[...] = line * CAP + rank
    held[...] = jnp.zeros_like(held)
    held[POOL : POOL + 1, :] = (line * CAP + rank).astype(F32)
    for block in range(16):
        held[0:POOL, :] = rows_ref[:, block * 256 : (block + 1) * 256].astype(F32)
        out_ref[block] = held[...].astype(BF16)


def embed_kernel(
    places_ref, arrived_ref, weight_ref, low_ref, out0, out1, out2, out3, slot_ref, held, label
):
    for far, out in enumerate((out0, out1, out2, out3)):
        for near in range(SIDE):
            place = far * SIDE + near
            block = arrived_ref[places_ref[place]].astype(F32)
            held[near * POOL : (near + 1) * POOL, :] = block[0:POOL]
            label[place : place + 1, :] = block[POOL : POOL + 1, 0:128]
        out[:, 0:WIDTH] = jnp.dot(
            held[...].astype(BF16), weight_ref[...], preferred_element_type=F32
        ).astype(BF16)
        out[:, WIDTH:] = jnp.zeros((SIDE * POOL, EXTRA), BF16)
        for near in range(SIDE):
            left = WIDTH + near // 2 * 256
            top = near % 2 * 32
            out[top : top + 32, left : left + 192] = low_ref[places_ref[far * SIDE + near]]
    line = (128, 16 * POOL)
    offset = lax.broadcasted_iota(jnp.int32, line, 1) - lax.broadcasted_iota(jnp.int32, line, 0)
    taken = offset == 0
    for place in range(1, 16):
        taken = taken | (offset == place * POOL)
    taken = taken & (lax.broadcasted_iota(jnp.int32, line, 0) < POOL)
    spot = jnp.dot(
        label[...].astype(BF16),
        jnp.where(taken, 1.0, 0.0).astype(BF16),
        preferred_element_type=F32,
    )
    place = lax.broadcasted_iota(jnp.int32, spot.shape, 0)
    start = place * POOL
    column = lax.broadcasted_iota(jnp.int32, spot.shape, 1)
    inside = (column >= start) & (column < start + POOL)
    target = jnp.sum(jnp.where(inside, spot, 0.0), 0, keepdims=True).astype(jnp.int32)
    block = jnp.sum(jnp.where(inside, place, 0), 0, keepdims=True)
    slot_ref[...] = (
        (target >> 2) * 64 + ((target >> 1) & 1) * 32 + (target & 1) + 2 * block
    )


def middle_kernel(in0, in1, in2, in3, out0, out1, out2, out3, held):
    held[...] = total_of((in0, in1, in2, in3))
    for near, out in enumerate((out0, out1, out2, out3)):
        out[:, 0:WIDTH] = held[near * POOL : (near + 1) * POOL, 0:WIDTH].astype(BF16)
        left = WIDTH + near // 2 * 256
        for half in range(2):
            top = near % 2 * 32 + half * 16
            out[0:16, WIDTH + half * 256 : WIDTH + half * 256 + 256] = held[
                top : top + 16, left : left + 256
            ].astype(BF16)
        out[16:POOL, WIDTH:] = jnp.zeros((POOL - 16, EXTRA), BF16)


def both_middle_kernel(*refs):
    img, txt, outs, held = refs[0:4], refs[4:8], refs[8:12], refs[12]
    held[...] = total_of(txt)
    for near, out in enumerate(outs):
        rows = slice(near * 32, (near + 1) * 32)
        out[0:32, :] = functools.reduce(
            jnp.add, [piece[rows, :].astype(F32) for piece in img]
        ).astype(BF16)
        out[32 : 32 + POOL, :] = held[near * POOL : (near + 1) * POOL, :].astype(BF16)


def part_middle_kernel(
    in0, in1, in2, in3, txt0, txt1, txt2, txt3, img0, img1, img2, img3, held
):
    pieces = (in0, in1, in2, in3)
    held[...] = functools.reduce(jnp.add, [piece[128:, :].astype(F32) for piece in pieces])
    for near, out in enumerate((txt0, txt1, txt2, txt3)):
        out[...] = held[near * POOL : (near + 1) * POOL, :].astype(BF16)
    for near, out in enumerate((img0, img1, img2, img3)):
        rows = slice(near * 32, (near + 1) * 32)
        out[...] = functools.reduce(
            jnp.add, [piece[rows, :].astype(F32) for piece in pieces]
        ).astype(BF16)


def join_kernel(in0, in1, in2, in3, out_ref, held):
    for place, piece in enumerate((in0, in1, in2, in3)):
        held[place * POOL : (place + 1) * POOL, :] = piece[...].astype(F32)
    out_ref[...] = held[...].astype(BF16)


def both_join_kernel(in0, in1, in2, in3, out_ref, held):
    for place, piece in enumerate((in0, in1, in2, in3)):
        out_ref[place * 32 : (place + 1) * 32, :] = piece[0:32, :]
        held[place * POOL : (place + 1) * POOL, :] = piece[32:, :].astype(F32)
    out_ref[128:, :] = held[...].astype(BF16)


def prompt_mod_kernel(mod_ref, out_ref):
    for own in range(2):
        for place in range(6):
            out_ref[own, place : place + 1, :] = mod_ref[own, place, 1:2, :]
        out_ref[own, 6:8, :] = jnp.zeros((2, out_ref.shape[2]), F32)


def mod_pair_kernel(first_ref, second_ref, out_ref):
    count = first_ref.shape[0]
    out_ref[0:count] = first_ref[...]
    out_ref[count : 2 * count] = second_ref[...]


def row_mod_kernel(index_ref, near_ref, far_ref, out_ref):
    for row in range(POOL):
        index = index_ref[row]
        within = lax.rem(index, 8)
        values = jnp.where(index < 8, near_ref[within], far_ref[within])
        for place in range(6):
            out_ref[place, row : row + 1, :] = values[place : place + 1]


def total_of(parts):
    return functools.reduce(jnp.add, [part[...].astype(F32) for part in parts])


def embed_norm_kernel(in0, in1, in2, in3, mod_ref, embedded_ref, out_ref):
    total = total_of((in0, in1, in2, in3))
    embedded = total[:, 0:WIDTH].astype(BF16)
    embedded_ref[...] = embedded
    modded = normed(embedded.astype(F32)) * (1.0 + mod_ref[1]) + mod_ref[0]
    out_ref[:, 0:WIDTH] = modded.astype(BF16)
    out_ref[:, WIDTH:] = total[:, WIDTH:].astype(BF16)


def both_norm_kernel(
    image_ref, embedded_ref, in0, in1, in2, in3, img_mod_ref, txt_mod_ref,
    img_ref, txt_ref, out_ref,
):
    projected = total_of((in0, in1, in2, in3))
    gate, shift, scale = img_mod_ref[2:3, :], img_mod_ref[3:4, :], img_mod_ref[4:5, :]
    mixed = (image_ref[...].astype(F32) + gate * projected[0:32]).astype(BF16)
    img_ref[...] = mixed
    out_ref[0:32, :] = (normed(mixed.astype(F32)) * (1.0 + scale) + shift).astype(BF16)
    mixed = (embedded_ref[...].astype(F32) + txt_mod_ref[2] * projected[32:]).astype(BF16)
    txt_ref[...] = mixed
    hidden = normed(mixed.astype(F32)) * (1.0 + txt_mod_ref[4]) + txt_mod_ref[3]
    out_ref[32 : 32 + POOL, :] = hidden.astype(BF16)


def one_hot(line, count):
    shape = (count, line.shape[1])
    return jnp.where(lax.broadcasted_iota(jnp.int32, shape, 0) == line, 1.0, 0.0)


def with_keep(values, keep):
    first = low_half(values.shape)
    return jnp.where(first, values, keep), jnp.where(first, keep, values)


def project(rows, weight_ref):
    both = jnp.concatenate([weight_ref[0], weight_ref[1]], -1)
    first = jnp.dot(rows, both, preferred_element_type=F32)
    return first, jnp.dot(rows, weight_ref[2], preferred_element_type=F32)


def txt_qkv_kernel(
    places_ref, in0, in1, in2, in3, weight_ref, gain_ref, slot_ref, out_ref, low_ref, held, rows_ref
):
    part = in0.shape[0]
    for place, piece in enumerate((in0, in1, in2, in3)):
        rows_ref[place * part : (place + 1) * part, :] = piece[:, 0:WIDTH]
        wide = piece[:, WIDTH:].astype(F32)
        for near in range(SIDE):
            rows = wide[near * POOL : near * POOL + 16]
            start = pl.multiple_of(places_ref[place * SIDE + near] * 32, 32)
            low_ref[pl.ds(start, 16), :] = rows[:, 0:192]
            low_ref[pl.ds(start + 16, 16), :] = rows[:, 256:448]
    projected, values = project(rows_ref[...], weight_ref)
    held[:, 0:128] = head_norm(projected[:, 0:128], gain_ref[0:1, :]).astype(BF16)
    held[:, 128:256] = head_norm(projected[:, 128:256], gain_ref[1:2, :]).astype(BF16)
    held[:, 256:384] = values.astype(BF16)
    hot = one_hot(slot_ref[...], 512)
    keep = jnp.sum(hot, -1, keepdims=True)
    slots = jnp.dot(hot.astype(BF16), held[...], preferred_element_type=F32)
    val0, val1 = with_keep(slots[:, 256:384], keep)
    out_ref[:, 0:256] = slots[:, 0:256].astype(BF16)
    out_ref[:, 256:384] = val0.astype(BF16)
    out_ref[:, 384:512] = val1.astype(BF16)


def img_project_kernel(
    ids_ref, tp_ref, image_hbm, mod_ref, weight_hbm, down_hbm,
    projected_ref, low_ref, own_ref, own_mod_ref, image, weight, down, wide, modded, sems,
):
    copies = [pltpu.make_async_copy(image_hbm, image, sems.at[0])]
    copies.append(pltpu.make_async_copy(weight_hbm, weight, sems.at[1]))
    for own in range(2):
        copies.append(
            pltpu.make_async_copy(down_hbm.at[ids_ref[own]], down.at[own], sems.at[2 + own])
        )
    for copy in copies:
        copy.start()
    copies[0].wait()
    depth = down.shape[1]
    tp = tp_ref[0]
    own_ref[...] = image[pl.ds(pl.multiple_of(tp * 32, 32), 32), :]
    for place in range(6):
        own_mod_ref[place : place + 1, :] = mod_ref[tp // 8, place, 0:1, :]
    for own in range(2):
        for part in range(2):
            rows = image[own * 256 + part * 128 : own * 256 + (part + 1) * 128, :].astype(F32)
            scaled = normed(rows) * (1.0 + mod_ref[own, 1, 0:1, :]) + mod_ref[own, 0, 0:1, :]
            modded[part * 128 : (part + 1) * 128, :] = scaled.astype(BF16)
        if own == 0:
            copies[1].wait()
        copies[2 + own].wait()
        wide[...] = jnp.zeros_like(wide)
        start = pl.multiple_of(tp * depth, 8)
        wide[pl.ds(start, depth), :] = down[own].astype(F32)
        projected, values = project(modded[...], weight)
        projected_ref[own * 256 : (own + 1) * 256, 0:256] = projected
        projected_ref[own * 256 : (own + 1) * 256, 256:384] = values
        low = jnp.dot(modded[...], wide[...].astype(BF16), preferred_element_type=F32)
        for block in range(8):
            low_ref[own * 8 + block] = low[block * 32 : (block + 1) * 32].astype(BF16)


def img_adapt_kernel(ids_ref, low_ref, projected_ref, up_hbm, gain_ref, out_ref, up, lift, sems):
    copies = []
    for own in range(2):
        copies.append(
            pltpu.make_async_copy(up_hbm.at[ids_ref[own]], up.at[own], sems.at[own])
        )
        copies[own].start()
    for own in range(2):
        copies[own].wait()
        lift[...] = jnp.zeros_like(lift)
        for part in range(3):
            lift[part * 64 : (part + 1) * 64, part * 128 : (part + 1) * 128] = up[own, part]
        rows = slice(own * 256, (own + 1) * 256)
        projected = projected_ref[rows, :] + ADAPTER_SCALE * jnp.dot(
            low_ref[rows, :].astype(BF16), lift[...], preferred_element_type=F32
        )
        out_ref[rows, 0:128] = head_norm(projected[:, 0:128], gain_ref[0:1, :]).astype(BF16)
        out_ref[rows, 128:256] = head_norm(projected[:, 128:256], gain_ref[1:2, :]).astype(BF16)
        val0, val1 = with_keep(projected[:, 256:384], 1.0)
        out_ref[rows, 256:384] = val0.astype(BF16)
        out_ref[rows, 384:512] = val1.astype(BF16)


def attend(queries, tokens):
    scaled = queries.astype(F32) * HEAD_DIM ** (-0.5)
    first = low_half(scaled.shape)
    keys = tokens[:, 128:256]
    results = []
    for head in range(2):
        own = jnp.where(first if head == 0 else ~first, scaled, 0.0).astype(BF16)
        scores = lax.dot_general(
            own, keys, (((1,), (1,)), ((), ())), preferred_element_type=F32
        )
        weights = jnp.exp(scores).astype(BF16)
        summed = jnp.dot(
            weights, tokens[:, 256 + head * 128 : 384 + head * 128], preferred_element_type=F32
        )
        results.append(summed / pltpu.roll(summed, HEAD_DIM, 1))
    return jnp.where(first, results[0], results[1]).astype(BF16)


def img_attend_kernel(
    places_ref, img_ref, slot_ref, weight_ref,
    out0, out1, out2, out3, token_ref, tokens, held, ranked,
):
    for own in range(2):
        tokens[own, 0:256, :] = img_ref[own * 256 : (own + 1) * 256, :]
        for source in range(8):
            start = 256 + source * 32
            tokens[own, start : start + 32, :] = slot_ref[source, own * 32 : (own + 1) * 32, :]
    token_ref[...] = tokens[...]
    for own in range(2):
        held[own * 256 : (own + 1) * 256, :] = attend(tokens[own, 0:256, 0:128], tokens[own])
    for place in range(16):
        start = pl.multiple_of(places_ref[place] * 32, 32)
        ranked[place * 32 : (place + 1) * 32, :] = held[pl.ds(start, 32), :]
    result = jnp.dot(ranked[...], weight_ref[...], preferred_element_type=F32)
    for place, out in enumerate((out0, out1, out2, out3)):
        out[...] = result[place * 128 : (place + 1) * 128].astype(BF16)


def txt_attend_kernel(token_ref, out_ref):
    for own in range(2):
        attended = attend(token_ref[own, 256:512, 0:128], token_ref[own])
        for source in range(8):
            start = source * 32
            out_ref[source, own * 32 : (own + 1) * 32, :] = attended[start : start + 32]


def txt_project_kernel(att_ref, slot_ref, weight_ref, out0, out1, out2, out3):
    hot = one_hot(slot_ref[...], 512).astype(BF16)
    rows = lax.dot_general(
        hot, att_ref[...], (((0,), (0,)), ((), ())), preferred_element_type=F32
    ).astype(BF16)
    part = out0.shape[0]
    result = jnp.dot(rows, weight_ref[...], preferred_element_type=F32)
    for place, out in enumerate((out0, out1, out2, out3)):
        out[...] = result[place * part : (place + 1) * part].astype(BF16)


def feed_kernel(*refs):
    rows_ref = refs[-1]
    count = (len(refs) - 3) // 2
    pieces, outs = refs[0:count], refs[count + 2 : 2 * count + 2]
    win_ref, wout_ref = refs[count], refs[count + 1]
    width = outs[0].shape[1]
    for stream, (start, part) in enumerate(((0, 128), (128, SIDE * POOL))):
        for place, piece in enumerate(pieces):
            rows_ref[place * part : (place + 1) * part, :] = piece[start : start + part, :]
        hidden = lax.dot_general(
            rows_ref[0 : count * part, :],
            win_ref[stream],
            (((1,), (1,)), ((), ())),
            preferred_element_type=F32,
        )
        hidden = jax.nn.gelu(hidden, approximate=True).astype(BF16)
        for columns in (slice(0, 1280), slice(1280, width)):
            result = jnp.dot(hidden, wout_ref[stream, :, columns], preferred_element_type=F32)
            for place, out in enumerate(outs):
                out[start : start + part, columns] = result[
                    place * part : (place + 1) * part
                ].astype(BF16)


def img_final_kernel(mixed_ref, in0, in1, in2, in3, mod_ref, out_ref):
    total = total_of((in0, in1, in2, in3))
    out_ref[...] = (mixed_ref[...].astype(F32) + mod_ref[5:6, :] * total).astype(BF16)


def txt_final_kernel(mixed_ref, in0, in1, in2, in3, mod_ref, slot_ref, placed_ref):
    total = total_of((in0, in1, in2, in3))
    rows = mixed_ref[...].astype(F32) + mod_ref[5] * total
    hot = one_hot(slot_ref[:, 0:POOL], 32).astype(BF16)
    placed = jnp.dot(hot, rows.astype(BF16), preferred_element_type=F32)
    for group in range(8):
        placed_ref[group] = placed[group * 4 : (group + 1) * 4].astype(BF16)


def middle(parts):
    rows, width = parts[0].shape
    return run(
        middle_kernel,
        [like((rows // SIDE, width))] * SIDE,
        parts,
        scratch=[pltpu.VMEM((rows, width), F32)],
    )


def both_middle(img_parts, txt_parts):
    rows, width = txt_parts[0].shape
    return run(
        both_middle_kernel,
        [like((32 + POOL, width))] * SIDE,
        (*img_parts, *txt_parts),
        scratch=[pltpu.VMEM((rows, width), F32)],
    )


def join(kernel, parts):
    width = parts[0].shape[1]
    return run(
        kernel,
        like((SIDE * parts[0].shape[0], width)),
        parts,
        scratch=[pltpu.VMEM((SIDE * POOL, width), F32)],
    )


def feed(parts, weight_in, weight_out, after=()):
    rows, width = parts[0].shape
    return run(
        feed_kernel,
        [like((rows, width))] * len(parts),
        (*parts, weight_in, weight_out),
        scratch=[pltpu.VMEM((len(parts) * 128, width), BF16)],
        flops=rows * len(parts) * width * weight_in.shape[1] * 4,
        limit=14,
        after=after,
    )


def shards(
    image,
    prompt_encoder_rows,
    prompt_row_request,
    request_adapter,
    modulation,
    query_key_gain,
    prompt_embed_weight,
    image_query_key_value,
    prompt_query_key_value,
    image_out_weight,
    prompt_out_weight,
    feed_in_weight,
    feed_out_weight,
    adapter_down,
    adapter_up,
):
    grp = lax.axis_index("grp")
    tp = lax.axis_index("tp")
    chip, core = grp // 2, grp % 2
    z, y = tp // SIDE, tp % SIDE
    width = image.shape[1]

    steps = jnp.arange(16)
    far, near = steps // SIDE, steps % SIDE
    places = jnp.where(
        core == 0,
        ((z + far) % SIDE) * SIDE + (y + near) % SIDE,
        ((z + near) % SIDE) * SIDE + (y + far) % SIDE,
    ).astype(jnp.int32)
    gains = jnp.concatenate([query_key_gain, query_key_gain], -1)

    request = prompt_row_request[:, 0]
    outgoing, slots_own = run(
        pack_kernel,
        [like((16, 32, 256)), like((1, 256), jnp.int32)],
        (prompt_encoder_rows, prompt_row_request.reshape(1, POOL)),
        scratch=[pltpu.VMEM((32, 256), F32), pltpu.VMEM((8, 256), jnp.int32)],
    )
    arrived = lax.all_to_all(outgoing, "tp", 0, 0, tiled=True)
    home = request // 4
    row_index = jnp.where(
        home == chip, 0, jnp.where(home == (chip ^ 1), 1, jnp.where(home == 3 - chip, 2, 3))
    )
    row_index = row_index * 4 + (request // 2 % 2 + core) % 2 * 2 + request % 2

    img_projected, low_part, own_image, own_mod = run(
        img_project_kernel,
        [
            like((512, 384), F32),
            like((16, 32, 192)),
            like((32, width)),
            like((6, width), F32),
        ],
        (
            request_adapter,
            tp.reshape(1).astype(jnp.int32),
            image,
            modulation.transpose(0, 2, 1, 3),
            image_query_key_value.transpose(1, 0, 2),
            adapter_down,
        ),
        smem=2,
        scratch=[
            pltpu.VMEM(image.shape, BF16),
            pltpu.VMEM((3, width, 128), BF16),
            pltpu.VMEM((2, *adapter_down.shape[1:]), BF16),
            pltpu.VMEM((width, 192), F32),
            pltpu.VMEM((256, width), BF16),
            pltpu.SemaphoreType.DMA((4,)),
        ],
        flops=512 * width * 576 * 2,
        limit=56,
        after=(outgoing, row_index),
        hbm=(2, 4, 5),
    )
    prompt_mod = run(
        prompt_mod_kernel, like((2, 8, width), F32), (modulation.transpose(0, 2, 1, 3),),
        after=(outgoing,),
    )
    mod_own = run(
        mod_pair_kernel, like((4, 8, width), F32), (prompt_mod, core_swap(prompt_mod))
    )
    *embed_parts, slots_all = run(
        embed_kernel,
        [like((SIDE * POOL, width + EXTRA))] * SIDE + [like((1, 16 * POOL), jnp.int32)],
        (places, arrived, prompt_embed_weight, low_part),
        smem=1,
        scratch=[pltpu.VMEM((SIDE * POOL, 256), F32), pltpu.VMEM((16, 128), F32)],
        flops=320 * 256 * width * 2,
        after=(mod_own,),
    )
    embed_pieces = exchange(embed_parts, 1)

    embed_sums = exchange(middle(embed_pieces), 0)
    mod_near = run(
        mod_pair_kernel,
        like((8, 8, width), F32),
        (mod_own, chip_swap(mod_own, False)),
        after=(embed_pieces[1],),
    )
    row_mod = run(
        row_mod_kernel,
        like((6, POOL, width), F32),
        (row_index, mod_near, chip_swap(mod_near, True)),
        smem=1,
    )
    embedded, txt_mod = run(
        embed_norm_kernel,
        [like((POOL, width)), like((POOL, width + EXTRA))],
        (*embed_sums, row_mod),
    )
    txt_mods = spread(join(join_kernel, spread(txt_mod, 0)), 1)

    slot_parts, low = run(
        txt_qkv_kernel,
        [like((512, 512)), like((512, 192), F32)],
        (places, *txt_mods, prompt_query_key_value.transpose(1, 0, 2), gains[1], slots_all),
        smem=1,
        scratch=[pltpu.VMEM((16 * POOL, 384), BF16), pltpu.VMEM((16 * POOL, width), BF16)],
        flops=320 * width * 384 * 2,
        limit=14,
    )
    img_parts = run(
        img_adapt_kernel,
        like((512, 512)),
        (request_adapter, low, img_projected, adapter_up, gains[0]),
        smem=1,
        scratch=[
            pltpu.VMEM((2, 3, 64, 128), BF16),
            pltpu.VMEM((192, 384), BF16),
            pltpu.SemaphoreType.DMA((2,)),
        ],
        flops=512 * 384 * 192 * 2,
        hbm=(3,),
    )
    slot_parts = lax.all_to_all(slot_parts.reshape(8, 64, 512), "grp", 0, 0, tiled=True)

    *img_terms, tokens = run(
        img_attend_kernel,
        [like((128, width))] * SIDE + [like((2, 512, 512))],
        (places, img_parts, slot_parts, image_out_weight),
        smem=1,
        scratch=[
            pltpu.VMEM((2, 512, 512), BF16),
            pltpu.VMEM((512, 128), BF16),
            pltpu.VMEM((512, 128), BF16),
        ],
        flops=1 << 30,
        limit=16,
    )
    img_sums = exchange(img_terms, 1)
    att_parts = run(txt_attend_kernel, like((8, 64, 128)), (tokens,), flops=1 << 29)
    att_parts = lax.all_to_all(att_parts, "grp", 0, 0, tiled=True).reshape(512, 128)
    txt_terms = run(
        txt_project_kernel,
        [like((SIDE * POOL, width))] * SIDE,
        (att_parts, slots_all, prompt_out_weight),
        flops=320 * 128 * width * 2,
        after=(img_sums[1],),
    )
    txt_sums = exchange(txt_terms, 1)

    sums = exchange(both_middle(img_sums, txt_sums), 0)
    mixed_img, mixed_txt, norm_rows = run(
        both_norm_kernel,
        [like((32, width)), like((POOL, width)), like((32 + POOL, width))],
        (own_image, embedded, *sums, own_mod, row_mod),
    )
    rows = spread(join(both_join_kernel, spread(norm_rows, 0)), 1)
    weight_in = feed_in_weight.transpose(0, 2, 1)
    own_term = feed(rows[:1], weight_in, feed_out_weight)
    terms = feed(rows[1:], weight_in, feed_out_weight, after=(own_term[0],))
    pieces = exchange([*own_term, *terms], 1)
    parts = run(
        part_middle_kernel,
        [like((POOL, width))] * SIDE + [like((32, width))] * SIDE,
        pieces,
        scratch=[pltpu.VMEM((SIDE * POOL, width), F32)],
    )

    placed = run(
        txt_final_kernel,
        like((8, 4, width)),
        (mixed_txt, *exchange(parts[:SIDE], 0), row_mod, slots_own),
    )
    image_out = run(
        img_final_kernel, like((32, width)), (mixed_img, *exchange(parts[SIDE:], 0), own_mod)
    )
    placed = lax.all_to_all(placed, "grp", 0, 0, tiled=True)
    prompt_out = placed.reshape(32, width)

    return (image_out, prompt_out)


def solution(mesh):
    placed = (
        P("grp", None),
        P(("grp", "tp"), None),
        P(("grp", "tp"), None),
        P("grp"),
        P("grp", None, None, None),
        P(),
        P("tp", None),
        P(None, None, "tp"),
        P(None, None, "tp"),
        P("tp", None),
        P("tp", None),
        P(None, None, "tp"),
        P(None, "tp", None),
        P(None, "tp", None),
        P(None, None, None, "tp"),
    )
    return jax.shard_map(
        shards,
        mesh=mesh,
        in_specs=placed,
        out_specs=(P(("grp", "tp"), None), P(("grp", "tp"), None)),
        check_vma=False,
    )
```

```python
import functools

import jax
import jax.numpy as jnp
from jax import lax
from jax.experimental import pallas as pl
from jax.experimental.pallas import tpu as pltpu
from jax.sharding import PartitionSpec as P

HEAD_DIM = 64
CAP = 2
EPSILON = 1e-06
ADAPTER_SCALE = 0.5
SIDE = 4
POOL = 20
WIDTH = 2432
EXTRA = 512
F32 = jnp.float32
BF16 = jnp.bfloat16


def torus_shift(values, stage, step):
    pairs = []
    for grp in range(8):
        for tp in range(16):
            z, y = divmod(tp, SIDE)
            if (grp + stage) % 2 == 0:
                y = (y + step) % SIDE
            else:
                z = (z + step) % SIDE
            pairs.append((grp * 16 + tp, grp * 16 + z * SIDE + y))
    return lax.ppermute(values, ("grp", "tp"), pairs)


def core_swap(values):
    return lax.ppermute(values, "grp", [(grp, grp ^ 1) for grp in range(8)])


def chip_swap(values, far):
    pairs = []
    for grp in range(8):
        chip = 3 - grp // 2 if far else (grp // 2) ^ 1
        pairs.append((grp, chip * 2 + grp % 2))
    return lax.ppermute(values, "grp", pairs)


def spread(rows, stage):
    return [
        rows,
        torus_shift(rows, stage, -1),
        torus_shift(rows, stage, 2),
        torus_shift(rows, stage, 1),
    ]


def exchange(parts, stage):
    return [
        parts[0],
        torus_shift(parts[3], stage, -1),
        torus_shift(parts[2], stage, 2),
        torus_shift(parts[1], stage, 1),
    ]


def run(kernel, outs, args, smem=0, scratch=(), flops=0, limit=8, after=(), hbm=()):
    count = len(args)
    spaces = [pltpu.SMEM] * smem + [pltpu.VMEM] * (count - smem)
    for index in hbm:
        spaces[index] = pl.ANY
    specs = [pl.BlockSpec(memory_space=space) for space in spaces]
    specs += [pl.BlockSpec(memory_space=pl.ANY)] * len(after)
    single = not isinstance(outs, list)
    shapes = [outs] if single else outs
    moved = sum(a.size * a.dtype.itemsize for a in args)
    moved += sum(s.size * s.dtype.itemsize for s in shapes)

    def body(*refs):
        kernel(*refs[:count], *refs[count + len(after) :])

    result = pl.pallas_call(
        body,
        out_shape=shapes,
        in_specs=specs,
        out_specs=[pl.BlockSpec(memory_space=pltpu.VMEM)] * len(shapes),
        scratch_shapes=list(scratch),
        compiler_params=pltpu.CompilerParams(vmem_limit_bytes=limit << 20),
        cost_estimate=pl.CostEstimate(flops=flops, bytes_accessed=moved, transcendentals=0),
    )(*args, *after)
    return result[0] if single else result


def like(shape, dtype=BF16):
    return jax.ShapeDtypeStruct(shape, dtype)


def normed(values):
    centred = values - jnp.mean(values, -1, keepdims=True)
    return centred * lax.rsqrt(jnp.mean(centred * centred, -1, keepdims=True) + EPSILON)


def low_half(shape):
    return lax.broadcasted_iota(jnp.int32, shape, len(shape) - 1) < HEAD_DIM


def head_norm(values, gains):
    first = low_half(values.shape)
    squares = values * values
    head0 = jnp.sum(jnp.where(first, squares, 0.0), -1, keepdims=True)
    head1 = jnp.sum(jnp.where(first, 0.0, squares), -1, keepdims=True)
    scale = jnp.where(
        first,
        lax.rsqrt(head0 * (1.0 / HEAD_DIM) + EPSILON),
        lax.rsqrt(head1 * (1.0 / HEAD_DIM) + EPSILON),
    )
    return values * scale * gains


def pack_kernel(rows_ref, line_ref, out_ref, slot_ref, held, wide):
    wide[...] = jnp.full(wide.shape, -1, jnp.int32)
    wide[0:1, 0:POOL] = line_ref[...]
    line = wide[0:1, :]
    first = lax.broadcasted_iota(jnp.int32, (POOL, 256), 0)
    second = lax.broadcasted_iota(jnp.int32, (POOL, 256), 1)
    column = jnp.sum(jnp.where(first == second, line, 0), 1, keepdims=True)
    rank = jnp.sum(jnp.where((column == line) & (first < second), 1, 0), 0, keepdims=True)
    slot_ref[...] = line * CAP + rank
    held[...] = jnp.zeros_like(held)
    held[POOL : POOL + 1, :] = (line * CAP + rank).astype(F32)
    for block in range(16):
        held[0:POOL, :] = rows_ref[:, block * 256 : (block + 1) * 256].astype(F32)
        out_ref[block] = held[...].astype(BF16)


def embed_kernel(
    places_ref, arrived_ref, weight_ref, low_ref, out0, out1, out2, out3, slot_ref, held, label
):
    for far, out in enumerate((out0, out1, out2, out3)):
        for near in range(SIDE):
            place = far * SIDE + near
            block = arrived_ref[places_ref[place]].astype(F32)
            held[near * POOL : (near + 1) * POOL, :] = block[0:POOL]
            label[place : place + 1, :] = block[POOL : POOL + 1, 0:128]
        out[:, 0:WIDTH] = jnp.dot(
            held[...].astype(BF16), weight_ref[...], preferred_element_type=F32
        ).astype(BF16)
        out[:, WIDTH:] = jnp.zeros((SIDE * POOL, EXTRA), BF16)
        for near in range(SIDE):
            left = WIDTH + near // 2 * 256
            top = near % 2 * 32
            out[top : top + 32, left : left + 192] = low_ref[places_ref[far * SIDE + near]]
    line = (128, 16 * POOL)
    offset = lax.broadcasted_iota(jnp.int32, line, 1) - lax.broadcasted_iota(jnp.int32, line, 0)
    taken = offset == 0
    for place in range(1, 16):
        taken = taken | (offset == place * POOL)
    taken = taken & (lax.broadcasted_iota(jnp.int32, line, 0) < POOL)
    spot = jnp.dot(
        label[...].astype(BF16),
        jnp.where(taken, 1.0, 0.0).astype(BF16),
        preferred_element_type=F32,
    )
    place = lax.broadcasted_iota(jnp.int32, spot.shape, 0)
    start = place * POOL
    column = lax.broadcasted_iota(jnp.int32, spot.shape, 1)
    inside = (column >= start) & (column < start + POOL)
    target = jnp.sum(jnp.where(inside, spot, 0.0), 0, keepdims=True).astype(jnp.int32)
    block = jnp.sum(jnp.where(inside, place, 0), 0, keepdims=True)
    slot_ref[...] = (
        (target >> 2) * 64 + ((target >> 1) & 1) * 32 + (target & 1) + 2 * block
    )


def middle_kernel(in0, in1, in2, in3, out0, out1, out2, out3, held):
    held[...] = total_of((in0, in1, in2, in3))
    for near, out in enumerate((out0, out1, out2, out3)):
        out[:, 0:WIDTH] = held[near * POOL : (near + 1) * POOL, 0:WIDTH].astype(BF16)
        left = WIDTH + near // 2 * 256
        for half in range(2):
            top = near % 2 * 32 + half * 16
            out[0:16, WIDTH + half * 256 : WIDTH + half * 256 + 256] = held[
                top : top + 16, left : left + 256
            ].astype(BF16)
        out[16:POOL, WIDTH:] = jnp.zeros((POOL - 16, EXTRA), BF16)


def both_middle_kernel(*refs):
    img, txt, outs, held = refs[0:4], refs[4:8], refs[8:12], refs[12]
    held[...] = total_of(txt)
    for near, out in enumerate(outs):
        rows = slice(near * 32, (near + 1) * 32)
        out[0:32, :] = functools.reduce(
            jnp.add, [piece[rows, :].astype(F32) for piece in img]
        ).astype(BF16)
        out[32 : 32 + POOL, :] = held[near * POOL : (near + 1) * POOL, :].astype(BF16)


def part_middle_kernel(
    in0, in1, in2, in3, txt0, txt1, txt2, txt3, img0, img1, img2, img3, held
):
    pieces = (in0, in1, in2, in3)
    held[...] = functools.reduce(jnp.add, [piece[128:, :].astype(F32) for piece in pieces])
    for near, out in enumerate((txt0, txt1, txt2, txt3)):
        out[...] = held[near * POOL : (near + 1) * POOL, :].astype(BF16)
    for near, out in enumerate((img0, img1, img2, img3)):
        rows = slice(near * 32, (near + 1) * 32)
        out[...] = functools.reduce(
            jnp.add, [piece[rows, :].astype(F32) for piece in pieces]
        ).astype(BF16)


def join_kernel(in0, in1, in2, in3, out_ref, held):
    for place, piece in enumerate((in0, in1, in2, in3)):
        held[place * POOL : (place + 1) * POOL, :] = piece[...].astype(F32)
    out_ref[...] = held[...].astype(BF16)


def both_join_kernel(in0, in1, in2, in3, out_ref, held):
    for place, piece in enumerate((in0, in1, in2, in3)):
        out_ref[place * 32 : (place + 1) * 32, :] = piece[0:32, :]
        held[place * POOL : (place + 1) * POOL, :] = piece[32:, :].astype(F32)
    out_ref[128:, :] = held[...].astype(BF16)


def prompt_mod_kernel(mod_ref, out_ref):
    for own in range(2):
        for place in range(6):
            out_ref[own, place : place + 1, :] = mod_ref[own, place, 1:2, :]
        out_ref[own, 6:8, :] = jnp.zeros((2, out_ref.shape[2]), F32)


def mod_pair_kernel(first_ref, second_ref, out_ref):
    count = first_ref.shape[0]
    out_ref[0:count] = first_ref[...]
    out_ref[count : 2 * count] = second_ref[...]


def row_mod_kernel(index_ref, near_ref, far_ref, out_ref):
    for row in range(POOL):
        index = index_ref[row]
        within = lax.rem(index, 8)
        values = jnp.where(index < 8, near_ref[within], far_ref[within])
        for place in range(6):
            out_ref[place, row : row + 1, :] = values[place : place + 1]


def total_of(parts):
    return functools.reduce(jnp.add, [part[...].astype(F32) for part in parts])


def embed_norm_kernel(in0, in1, in2, in3, mod_ref, embedded_ref, out_ref):
    total = total_of((in0, in1, in2, in3))
    embedded = total[:, 0:WIDTH].astype(BF16)
    embedded_ref[...] = embedded
    modded = normed(embedded.astype(F32)) * (1.0 + mod_ref[1]) + mod_ref[0]
    out_ref[:, 0:WIDTH] = modded.astype(BF16)
    out_ref[:, WIDTH:] = total[:, WIDTH:].astype(BF16)


def both_norm_kernel(
    image_ref, embedded_ref, in0, in1, in2, in3, img_mod_ref, txt_mod_ref,
    img_ref, txt_ref, out_ref,
):
    projected = total_of((in0, in1, in2, in3))
    gate, shift, scale = img_mod_ref[2:3, :], img_mod_ref[3:4, :], img_mod_ref[4:5, :]
    mixed = (image_ref[...].astype(F32) + gate * projected[0:32]).astype(BF16)
    img_ref[...] = mixed
    out_ref[0:32, :] = (normed(mixed.astype(F32)) * (1.0 + scale) + shift).astype(BF16)
    mixed = (embedded_ref[...].astype(F32) + txt_mod_ref[2] * projected[32:]).astype(BF16)
    txt_ref[...] = mixed
    hidden = normed(mixed.astype(F32)) * (1.0 + txt_mod_ref[4]) + txt_mod_ref[3]
    out_ref[32 : 32 + POOL, :] = hidden.astype(BF16)


def one_hot(line, count):
    shape = (count, line.shape[1])
    return jnp.where(lax.broadcasted_iota(jnp.int32, shape, 0) == line, 1.0, 0.0)


def with_keep(values, keep):
    first = low_half(values.shape)
    return jnp.where(first, values, keep), jnp.where(first, keep, values)


def project(rows, weight_ref):
    both = jnp.concatenate([weight_ref[0], weight_ref[1]], -1)
    first = jnp.dot(rows, both, preferred_element_type=F32)
    return first, jnp.dot(rows, weight_ref[2], preferred_element_type=F32)


def txt_qkv_kernel(
    places_ref, in0, in1, in2, in3, weight_ref, gain_ref, slot_ref, out_ref, low_ref, held, rows_ref
):
    part = in0.shape[0]
    for place, piece in enumerate((in0, in1, in2, in3)):
        rows_ref[place * part : (place + 1) * part, :] = piece[:, 0:WIDTH]
        wide = piece[:, WIDTH:].astype(F32)
        for near in range(SIDE):
            rows = wide[near * POOL : near * POOL + 16]
            start = pl.multiple_of(places_ref[place * SIDE + near] * 32, 32)
            low_ref[pl.ds(start, 16), :] = rows[:, 0:192]
            low_ref[pl.ds(start + 16, 16), :] = rows[:, 256:448]
    projected, values = project(rows_ref[...], weight_ref)
    held[:, 0:128] = head_norm(projected[:, 0:128], gain_ref[0:1, :]).astype(BF16)
    held[:, 128:256] = head_norm(projected[:, 128:256], gain_ref[1:2, :]).astype(BF16)
    held[:, 256:384] = values.astype(BF16)
    hot = one_hot(slot_ref[...], 512)
    keep = jnp.sum(hot, -1, keepdims=True)
    slots = jnp.dot(hot.astype(BF16), held[...], preferred_element_type=F32)
    val0, val1 = with_keep(slots[:, 256:384], keep)
    out_ref[:, 0:256] = slots[:, 0:256].astype(BF16)
    out_ref[:, 256:384] = val0.astype(BF16)
    out_ref[:, 384:512] = val1.astype(BF16)


def img_project_kernel(
    ids_ref, tp_ref, image_hbm, mod_ref, weight_hbm, down_hbm,
    projected_ref, low_ref, own_ref, own_mod_ref, image, weight, down, wide, modded, sems,
):
    copies = [pltpu.make_async_copy(image_hbm, image, sems.at[0])]
    copies.append(pltpu.make_async_copy(weight_hbm, weight, sems.at[1]))
    for own in range(2):
        copies.append(
            pltpu.make_async_copy(down_hbm.at[ids_ref[own]], down.at[own], sems.at[2 + own])
        )
    for copy in copies:
        copy.start()
    copies[0].wait()
    depth = down.shape[1]
    tp = tp_ref[0]
    own_ref[...] = image[pl.ds(pl.multiple_of(tp * 32, 32), 32), :]
    for place in range(6):
        own_mod_ref[place : place + 1, :] = mod_ref[tp // 8, place, 0:1, :]
    for own in range(2):
        for part in range(2):
            rows = image[own * 256 + part * 128 : own * 256 + (part + 1) * 128, :].astype(F32)
            scaled = normed(rows) * (1.0 + mod_ref[own, 1, 0:1, :]) + mod_ref[own, 0, 0:1, :]
            modded[part * 128 : (part + 1) * 128, :] = scaled.astype(BF16)
        if own == 0:
            copies[1].wait()
        copies[2 + own].wait()
        wide[...] = jnp.zeros_like(wide)
        start = pl.multiple_of(tp * depth, 8)
        wide[pl.ds(start, depth), :] = down[own].astype(F32)
        projected, values = project(modded[...], weight)
        projected_ref[own * 256 : (own + 1) * 256, 0:256] = projected
        projected_ref[own * 256 : (own + 1) * 256, 256:384] = values
        low = jnp.dot(modded[...], wide[...].astype(BF16), preferred_element_type=F32)
        for block in range(8):
            low_ref[own * 8 + block] = low[block * 32 : (block + 1) * 32].astype(BF16)


def img_adapt_kernel(ids_ref, low_ref, projected_ref, up_hbm, gain_ref, out_ref, up, lift, sems):
    copies = []
    for own in range(2):
        copies.append(
            pltpu.make_async_copy(up_hbm.at[ids_ref[own]], up.at[own], sems.at[own])
        )
        copies[own].start()
    for own in range(2):
        copies[own].wait()
        lift[...] = jnp.zeros_like(lift)
        for part in range(3):
            lift[part * 64 : (part + 1) * 64, part * 128 : (part + 1) * 128] = up[own, part]
        rows = slice(own * 256, (own + 1) * 256)
        projected = projected_ref[rows, :] + ADAPTER_SCALE * jnp.dot(
            low_ref[rows, :].astype(BF16), lift[...], preferred_element_type=F32
        )
        out_ref[rows, 0:128] = head_norm(projected[:, 0:128], gain_ref[0:1, :]).astype(BF16)
        out_ref[rows, 128:256] = head_norm(projected[:, 128:256], gain_ref[1:2, :]).astype(BF16)
        val0, val1 = with_keep(projected[:, 256:384], 1.0)
        out_ref[rows, 256:384] = val0.astype(BF16)
        out_ref[rows, 384:512] = val1.astype(BF16)


def attend(queries, tokens):
    scaled = queries.astype(F32) * HEAD_DIM ** (-0.5)
    first = low_half(scaled.shape)
    keys = tokens[:, 128:256]
    results = []
    for head in range(2):
        own = jnp.where(first if head == 0 else ~first, scaled, 0.0).astype(BF16)
        scores = lax.dot_general(
            own, keys, (((1,), (1,)), ((), ())), preferred_element_type=F32
        )
        weights = jnp.exp(scores).astype(BF16)
        summed = jnp.dot(
            weights, tokens[:, 256 + head * 128 : 384 + head * 128], preferred_element_type=F32
        )
        results.append(summed / pltpu.roll(summed, HEAD_DIM, 1))
    return jnp.where(first, results[0], results[1]).astype(BF16)


def img_attend_kernel(
    places_ref, img_ref, slot_ref, weight_ref,
    out0, out1, out2, out3, token_ref, tokens, held, ranked,
):
    for own in range(2):
        tokens[own, 0:256, :] = img_ref[own * 256 : (own + 1) * 256, :]
        for source in range(8):
            start = 256 + source * 32
            tokens[own, start : start + 32, :] = slot_ref[source, own * 32 : (own + 1) * 32, :]
    token_ref[...] = tokens[...]
    for own in range(2):
        held[own * 256 : (own + 1) * 256, :] = attend(tokens[own, 0:256, 0:128], tokens[own])
    for place in range(16):
        start = pl.multiple_of(places_ref[place] * 32, 32)
        ranked[place * 32 : (place + 1) * 32, :] = held[pl.ds(start, 32), :]
    result = jnp.dot(ranked[...], weight_ref[...], preferred_element_type=F32)
    for place, out in enumerate((out0, out1, out2, out3)):
        out[...] = result[place * 128 : (place + 1) * 128].astype(BF16)


def txt_attend_kernel(token_ref, out_ref):
    for own in range(2):
        attended = attend(token_ref[own, 256:512, 0:128], token_ref[own])
        for source in range(8):
            start = source * 32
            out_ref[source, own * 32 : (own + 1) * 32, :] = attended[start : start + 32]


def txt_project_kernel(att_ref, slot_ref, weight_ref, out0, out1, out2, out3):
    hot = one_hot(slot_ref[...], 512).astype(BF16)
    rows = lax.dot_general(
        hot, att_ref[...], (((0,), (0,)), ((), ())), preferred_element_type=F32
    ).astype(BF16)
    part = out0.shape[0]
    result = jnp.dot(rows, weight_ref[...], preferred_element_type=F32)
    for place, out in enumerate((out0, out1, out2, out3)):
        out[...] = result[place * part : (place + 1) * part].astype(BF16)


def feed_kernel(*refs):
    rows_ref = refs[-1]
    count = (len(refs) - 3) // 2
    pieces, outs = refs[0:count], refs[count + 2 : 2 * count + 2]
    win_ref, wout_ref = refs[count], refs[count + 1]
    width = outs[0].shape[1]
    for stream, (start, part) in enumerate(((0, 128), (128, SIDE * POOL))):
        for place, piece in enumerate(pieces):
            rows_ref[place * part : (place + 1) * part, :] = piece[start : start + part, :]
        hidden = lax.dot_general(
            rows_ref[0 : count * part, :],
            win_ref[stream],
            (((1,), (1,)), ((), ())),
            preferred_element_type=F32,
        )
        hidden = jax.nn.gelu(hidden, approximate=True).astype(BF16)
        for columns in (slice(0, 1280), slice(1280, width)):
            result = jnp.dot(hidden, wout_ref[stream, :, columns], preferred_element_type=F32)
            for place, out in enumerate(outs):
                out[start : start + part, columns] = result[
                    place * part : (place + 1) * part
                ].astype(BF16)


def img_final_kernel(mixed_ref, in0, in1, in2, in3, mod_ref, out_ref):
    total = total_of((in0, in1, in2, in3))
    out_ref[...] = (mixed_ref[...].astype(F32) + mod_ref[5:6, :] * total).astype(BF16)


def txt_final_kernel(mixed_ref, in0, in1, in2, in3, mod_ref, slot_ref, placed_ref):
    total = total_of((in0, in1, in2, in3))
    rows = mixed_ref[...].astype(F32) + mod_ref[5] * total
    hot = one_hot(slot_ref[:, 0:POOL], 32).astype(BF16)
    placed = jnp.dot(hot, rows.astype(BF16), preferred_element_type=F32)
    for group in range(8):
        placed_ref[group] = placed[group * 4 : (group + 1) * 4].astype(BF16)


def middle(parts):
    rows, width = parts[0].shape
    return run(
        middle_kernel,
        [like((rows // SIDE, width))] * SIDE,
        parts,
        scratch=[pltpu.VMEM((rows, width), F32)],
    )


def both_middle(img_parts, txt_parts):
    rows, width = txt_parts[0].shape
    return run(
        both_middle_kernel,
        [like((32 + POOL, width))] * SIDE,
        (*img_parts, *txt_parts),
        scratch=[pltpu.VMEM((rows, width), F32)],
    )


def join(kernel, parts):
    width = parts[0].shape[1]
    return run(
        kernel,
        like((SIDE * parts[0].shape[0], width)),
        parts,
        scratch=[pltpu.VMEM((SIDE * POOL, width), F32)],
    )


def feed(parts, weight_in, weight_out, after=()):
    rows, width = parts[0].shape
    return run(
        feed_kernel,
        [like((rows, width))] * len(parts),
        (*parts, weight_in, weight_out),
        scratch=[pltpu.VMEM((len(parts) * 128, width), BF16)],
        flops=rows * len(parts) * width * weight_in.shape[1] * 4,
        limit=14,
        after=after,
    )


def shards(
    image,
    prompt_encoder_rows,
    prompt_row_request,
    request_adapter,
    modulation,
    query_key_gain,
    prompt_embed_weight,
    image_query_key_value,
    prompt_query_key_value,
    image_out_weight,
    prompt_out_weight,
    feed_in_weight,
    feed_out_weight,
    adapter_down,
    adapter_up,
):
    grp = lax.axis_index("grp")
    tp = lax.axis_index("tp")
    chip, core = grp // 2, grp % 2
    z, y = tp // SIDE, tp % SIDE
    width = image.shape[1]

    steps = jnp.arange(16)
    far, near = steps // SIDE, steps % SIDE
    places = jnp.where(
        core == 0,
        ((z + far) % SIDE) * SIDE + (y + near) % SIDE,
        ((z + near) % SIDE) * SIDE + (y + far) % SIDE,
    ).astype(jnp.int32)
    gains = jnp.concatenate([query_key_gain, query_key_gain], -1)

    request = prompt_row_request[:, 0]
    outgoing, slots_own = run(
        pack_kernel,
        [like((16, 32, 256)), like((1, 256), jnp.int32)],
        (prompt_encoder_rows, prompt_row_request.reshape(1, POOL)),
        scratch=[pltpu.VMEM((32, 256), F32), pltpu.VMEM((8, 256), jnp.int32)],
    )
    arrived = lax.all_to_all(outgoing, "tp", 0, 0, tiled=True)
    home = request // 4
    row_index = jnp.where(
        home == chip, 0, jnp.where(home == (chip ^ 1), 1, jnp.where(home == 3 - chip, 2, 3))
    )
    row_index = row_index * 4 + (request // 2 % 2 + core) % 2 * 2 + request % 2

    img_projected, low_part, own_image, own_mod = run(
        img_project_kernel,
        [
            like((512, 384), F32),
            like((16, 32, 192)),
            like((32, width)),
            like((6, width), F32),
        ],
        (
            request_adapter,
            tp.reshape(1).astype(jnp.int32),
            image,
            modulation.transpose(0, 2, 1, 3),
            image_query_key_value.transpose(1, 0, 2),
            adapter_down,
        ),
        smem=2,
        scratch=[
            pltpu.VMEM(image.shape, BF16),
            pltpu.VMEM((3, width, 128), BF16),
            pltpu.VMEM((2, *adapter_down.shape[1:]), BF16),
            pltpu.VMEM((width, 192), F32),
            pltpu.VMEM((256, width), BF16),
            pltpu.SemaphoreType.DMA((4,)),
        ],
        flops=512 * width * 576 * 2,
        limit=56,
        after=(outgoing, row_index),
        hbm=(2, 4, 5),
    )
    prompt_mod = run(
        prompt_mod_kernel, like((2, 8, width), F32), (modulation.transpose(0, 2, 1, 3),),
        after=(outgoing,),
    )
    mod_own = run(
        mod_pair_kernel, like((4, 8, width), F32), (prompt_mod, core_swap(prompt_mod))
    )
    *embed_parts, slots_all = run(
        embed_kernel,
        [like((SIDE * POOL, width + EXTRA))] * SIDE + [like((1, 16 * POOL), jnp.int32)],
        (places, arrived, prompt_embed_weight, low_part),
        smem=1,
        scratch=[pltpu.VMEM((SIDE * POOL, 256), F32), pltpu.VMEM((16, 128), F32)],
        flops=320 * 256 * width * 2,
        after=(mod_own,),
    )
    embed_pieces = exchange(embed_parts, 1)

    embed_sums = exchange(middle(embed_pieces), 0)
    mod_near = run(
        mod_pair_kernel,
        like((8, 8, width), F32),
        (mod_own, chip_swap(mod_own, False)),
    )
    row_mod = run(
        row_mod_kernel,
        like((6, POOL, width), F32),
        (row_index, mod_near, chip_swap(mod_near, True)),
        smem=1,
    )
    embedded, txt_mod = run(
        embed_norm_kernel,
        [like((POOL, width)), like((POOL, width + EXTRA))],
        (*embed_sums, row_mod),
    )
    txt_mods = spread(join(join_kernel, spread(txt_mod, 0)), 1)

    slot_parts, low = run(
        txt_qkv_kernel,
        [like((512, 512)), like((512, 192), F32)],
        (places, *txt_mods, prompt_query_key_value.transpose(1, 0, 2), gains[1], slots_all),
        smem=1,
        scratch=[pltpu.VMEM((16 * POOL, 384), BF16), pltpu.VMEM((16 * POOL, width), BF16)],
        flops=320 * width * 384 * 2,
        limit=14,
    )
    img_parts = run(
        img_adapt_kernel,
        like((512, 512)),
        (request_adapter, low, img_projected, adapter_up, gains[0]),
        smem=1,
        scratch=[
            pltpu.VMEM((2, 3, 64, 128), BF16),
            pltpu.VMEM((192, 384), BF16),
            pltpu.SemaphoreType.DMA((2,)),
        ],
        flops=512 * 384 * 192 * 2,
        hbm=(3,),
    )
    slot_parts = lax.all_to_all(slot_parts.reshape(8, 64, 512), "grp", 0, 0, tiled=True)

    *img_terms, tokens = run(
        img_attend_kernel,
        [like((128, width))] * SIDE + [like((2, 512, 512))],
        (places, img_parts, slot_parts, image_out_weight),
        smem=1,
        scratch=[
            pltpu.VMEM((2, 512, 512), BF16),
            pltpu.VMEM((512, 128), BF16),
            pltpu.VMEM((512, 128), BF16),
        ],
        flops=1 << 30,
        limit=16,
    )
    img_sums = exchange(img_terms, 1)
    att_parts = run(txt_attend_kernel, like((8, 64, 128)), (tokens,), flops=1 << 29)
    att_parts = lax.all_to_all(att_parts, "grp", 0, 0, tiled=True).reshape(512, 128)
    txt_terms = run(
        txt_project_kernel,
        [like((SIDE * POOL, width))] * SIDE,
        (att_parts, slots_all, prompt_out_weight),
        flops=320 * 128 * width * 2,
        after=(img_sums[1],),
    )
    txt_sums = exchange(txt_terms, 1)

    sums = exchange(both_middle(img_sums, txt_sums), 0)
    mixed_img, mixed_txt, norm_rows = run(
        both_norm_kernel,
        [like((32, width)), like((POOL, width)), like((32 + POOL, width))],
        (own_image, embedded, *sums, own_mod, row_mod),
    )
    rows = spread(join(both_join_kernel, spread(norm_rows, 0)), 1)
    weight_in = feed_in_weight.transpose(0, 2, 1)
    own_term = feed(rows[:1], weight_in, feed_out_weight)
    terms = feed(rows[1:], weight_in, feed_out_weight, after=(own_term[0],))
    pieces = exchange([*own_term, *terms], 1)
    parts = run(
        part_middle_kernel,
        [like((POOL, width))] * SIDE + [like((32, width))] * SIDE,
        pieces,
        scratch=[pltpu.VMEM((SIDE * POOL, width), F32)],
    )

    placed = run(
        txt_final_kernel,
        like((8, 4, width)),
        (mixed_txt, *exchange(parts[:SIDE], 0), row_mod, slots_own),
    )
    image_out = run(
        img_final_kernel, like((32, width)), (mixed_img, *exchange(parts[SIDE:], 0), own_mod)
    )
    placed = lax.all_to_all(placed, "grp", 0, 0, tiled=True)
    prompt_out = placed.reshape(32, width)

    return (image_out, prompt_out)


def solution(mesh):
    placed = (
        P("grp", None),
        P(("grp", "tp"), None),
        P(("grp", "tp"), None),
        P("grp"),
        P("grp", None, None, None),
        P(),
        P("tp", None),
        P(None, None, "tp"),
        P(None, None, "tp"),
        P("tp", None),
        P("tp", None),
        P(None, None, "tp"),
        P(None, "tp", None),
        P(None, "tp", None),
        P(None, None, None, "tp"),
    )
    return jax.shard_map(
        shards,
        mesh=mesh,
        in_specs=placed,
        out_specs=(P(("grp", "tp"), None), P(("grp", "tp"), None)),
        check_vma=False,
    )
```

```python
import functools

import jax
import jax.numpy as jnp
from jax import lax
from jax.experimental import pallas as pl
from jax.experimental.pallas import tpu as pltpu
from jax.sharding import PartitionSpec as P

HEAD_DIM = 64
CAP = 2
EPSILON = 1e-06
ADAPTER_SCALE = 0.5
SIDE = 4
POOL = 20
WIDTH = 2432
EXTRA = 512
F32 = jnp.float32
BF16 = jnp.bfloat16


def torus_shift(values, stage, step):
    pairs = []
    for grp in range(8):
        for tp in range(16):
            z, y = divmod(tp, SIDE)
            if (grp + stage) % 2 == 0:
                y = (y + step) % SIDE
            else:
                z = (z + step) % SIDE
            pairs.append((grp * 16 + tp, grp * 16 + z * SIDE + y))
    return lax.ppermute(values, ("grp", "tp"), pairs)


def core_swap(values):
    return lax.ppermute(values, "grp", [(grp, grp ^ 1) for grp in range(8)])


def chip_swap(values, far):
    pairs = []
    for grp in range(8):
        chip = 3 - grp // 2 if far else (grp // 2) ^ 1
        pairs.append((grp, chip * 2 + grp % 2))
    return lax.ppermute(values, "grp", pairs)


def spread(rows, stage):
    return [
        rows,
        torus_shift(rows, stage, -1),
        torus_shift(rows, stage, 2),
        torus_shift(rows, stage, 1),
    ]


def exchange(parts, stage):
    return [
        parts[0],
        torus_shift(parts[3], stage, -1),
        torus_shift(parts[2], stage, 2),
        torus_shift(parts[1], stage, 1),
    ]


def run(kernel, outs, args, smem=0, scratch=(), flops=0, limit=8, after=(), hbm=()):
    count = len(args)
    spaces = [pltpu.SMEM] * smem + [pltpu.VMEM] * (count - smem)
    for index in hbm:
        spaces[index] = pl.ANY
    specs = [pl.BlockSpec(memory_space=space) for space in spaces]
    specs += [pl.BlockSpec(memory_space=pl.ANY)] * len(after)
    single = not isinstance(outs, list)
    shapes = [outs] if single else outs
    moved = sum(a.size * a.dtype.itemsize for a in args)
    moved += sum(s.size * s.dtype.itemsize for s in shapes)

    def body(*refs):
        kernel(*refs[:count], *refs[count + len(after) :])

    result = pl.pallas_call(
        body,
        out_shape=shapes,
        in_specs=specs,
        out_specs=[pl.BlockSpec(memory_space=pltpu.VMEM)] * len(shapes),
        scratch_shapes=list(scratch),
        compiler_params=pltpu.CompilerParams(vmem_limit_bytes=limit << 20),
        cost_estimate=pl.CostEstimate(flops=flops, bytes_accessed=moved, transcendentals=0),
    )(*args, *after)
    return result[0] if single else result


def like(shape, dtype=BF16):
    return jax.ShapeDtypeStruct(shape, dtype)


def normed(values):
    centred = values - jnp.mean(values, -1, keepdims=True)
    return centred * lax.rsqrt(jnp.mean(centred * centred, -1, keepdims=True) + EPSILON)


def low_half(shape):
    return lax.broadcasted_iota(jnp.int32, shape, len(shape) - 1) < HEAD_DIM


def head_norm(values, gains):
    first = low_half(values.shape)
    squares = values * values
    head0 = jnp.sum(jnp.where(first, squares, 0.0), -1, keepdims=True)
    head1 = jnp.sum(jnp.where(first, 0.0, squares), -1, keepdims=True)
    scale = jnp.where(
        first,
        lax.rsqrt(head0 * (1.0 / HEAD_DIM) + EPSILON),
        lax.rsqrt(head1 * (1.0 / HEAD_DIM) + EPSILON),
    )
    return values * scale * gains


def pack_kernel(rows_ref, line_ref, out_ref, slot_ref, held, wide):
    wide[...] = jnp.full(wide.shape, -1, jnp.int32)
    wide[0:1, 0:POOL] = line_ref[...]
    line = wide[0:1, :]
    first = lax.broadcasted_iota(jnp.int32, (POOL, 256), 0)
    second = lax.broadcasted_iota(jnp.int32, (POOL, 256), 1)
    column = jnp.sum(jnp.where(first == second, line, 0), 1, keepdims=True)
    rank = jnp.sum(jnp.where((column == line) & (first < second), 1, 0), 0, keepdims=True)
    slot_ref[...] = line * CAP + rank
    held[...] = jnp.zeros_like(held)
    held[POOL : POOL + 1, :] = (line * CAP + rank).astype(F32)
    for block in range(16):
        held[0:POOL, :] = rows_ref[:, block * 256 : (block + 1) * 256].astype(F32)
        out_ref[block] = held[...].astype(BF16)


def embed_kernel(
    places_ref, arrived_ref, weight_ref, low_ref, out0, out1, out2, out3, slot_ref, held, label
):
    for far, out in enumerate((out0, out1, out2, out3)):
        for near in range(SIDE):
            place = far * SIDE + near
            block = arrived_ref[places_ref[place]].astype(F32)
            held[near * POOL : (near + 1) * POOL, :] = block[0:POOL]
            label[place : place + 1, :] = block[POOL : POOL + 1, 0:128]
        out[:, 0:WIDTH] = jnp.dot(
            held[...].astype(BF16), weight_ref[...], preferred_element_type=F32
        ).astype(BF16)
        out[:, WIDTH:] = jnp.zeros((SIDE * POOL, EXTRA), BF16)
        for near in range(SIDE):
            left = WIDTH + near // 2 * 256
            top = near % 2 * 32
            out[top : top + 32, left : left + 192] = low_ref[places_ref[far * SIDE + near]]
    line = (128, 16 * POOL)
    offset = lax.broadcasted_iota(jnp.int32, line, 1) - lax.broadcasted_iota(jnp.int32, line, 0)
    taken = offset == 0
    for place in range(1, 16):
        taken = taken | (offset == place * POOL)
    taken = taken & (lax.broadcasted_iota(jnp.int32, line, 0) < POOL)
    spot = jnp.dot(
        label[...].astype(BF16),
        jnp.where(taken, 1.0, 0.0).astype(BF16),
        preferred_element_type=F32,
    )
    place = lax.broadcasted_iota(jnp.int32, spot.shape, 0)
    start = place * POOL
    column = lax.broadcasted_iota(jnp.int32, spot.shape, 1)
    inside = (column >= start) & (column < start + POOL)
    target = jnp.sum(jnp.where(inside, spot, 0.0), 0, keepdims=True).astype(jnp.int32)
    block = jnp.sum(jnp.where(inside, place, 0), 0, keepdims=True)
    slot_ref[...] = (
        (target >> 2) * 64 + ((target >> 1) & 1) * 32 + (target & 1) + 2 * block
    )


def middle_kernel(in0, in1, in2, in3, out0, out1, out2, out3, held):
    held[...] = total_of((in0, in1, in2, in3))
    for near, out in enumerate((out0, out1, out2, out3)):
        out[:, 0:WIDTH] = held[near * POOL : (near + 1) * POOL, 0:WIDTH].astype(BF16)
        left = WIDTH + near // 2 * 256
        for half in range(2):
            top = near % 2 * 32 + half * 16
            out[0:16, WIDTH + half * 256 : WIDTH + half * 256 + 256] = held[
                top : top + 16, left : left + 256
            ].astype(BF16)
        out[16:POOL, WIDTH:] = jnp.zeros((POOL - 16, EXTRA), BF16)


def both_middle_kernel(*refs):
    img, txt, outs, held = refs[0:4], refs[4:8], refs[8:12], refs[12]
    held[...] = total_of(txt)
    for near, out in enumerate(outs):
        rows = slice(near * 32, (near + 1) * 32)
        out[0:32, :] = functools.reduce(
            jnp.add, [piece[rows, :].astype(F32) for piece in img]
        ).astype(BF16)
        out[32 : 32 + POOL, :] = held[near * POOL : (near + 1) * POOL, :].astype(BF16)


def part_middle_kernel(
    in0, in1, in2, in3, txt0, txt1, txt2, txt3, img0, img1, img2, img3, held
):
    pieces = (in0, in1, in2, in3)
    held[...] = functools.reduce(jnp.add, [piece[128:, :].astype(F32) for piece in pieces])
    for near, out in enumerate((txt0, txt1, txt2, txt3)):
        out[...] = held[near * POOL : (near + 1) * POOL, :].astype(BF16)
    for near, out in enumerate((img0, img1, img2, img3)):
        rows = slice(near * 32, (near + 1) * 32)
        out[...] = functools.reduce(
            jnp.add, [piece[rows, :].astype(F32) for piece in pieces]
        ).astype(BF16)


def join_kernel(in0, in1, in2, in3, out_ref, held):
    for place, piece in enumerate((in0, in1, in2, in3)):
        held[place * POOL : (place + 1) * POOL, :] = piece[...].astype(F32)
    out_ref[...] = held[...].astype(BF16)


def both_join_kernel(in0, in1, in2, in3, out_ref, held):
    for place, piece in enumerate((in0, in1, in2, in3)):
        out_ref[place * 32 : (place + 1) * 32, :] = piece[0:32, :]
        held[place * POOL : (place + 1) * POOL, :] = piece[32:, :].astype(F32)
    out_ref[128:, :] = held[...].astype(BF16)


def prompt_mod_kernel(mod_ref, out_ref):
    for own in range(2):
        for place in range(6):
            out_ref[own, place : place + 1, :] = mod_ref[own, place, 1:2, :]
        out_ref[own, 6:8, :] = jnp.zeros((2, out_ref.shape[2]), F32)


def mod_pair_kernel(first_ref, second_ref, out_ref):
    count = first_ref.shape[0]
    out_ref[0:count] = first_ref[...]
    out_ref[count : 2 * count] = second_ref[...]


def row_mod_kernel(index_ref, near_ref, far_ref, out_ref):
    for row in range(POOL):
        index = index_ref[row]
        within = lax.rem(index, 8)
        values = jnp.where(index < 8, near_ref[within], far_ref[within])
        for place in range(6):
            out_ref[place, row : row + 1, :] = values[place : place + 1]


def total_of(parts):
    return functools.reduce(jnp.add, [part[...].astype(F32) for part in parts])


def embed_norm_kernel(in0, in1, in2, in3, mod_ref, embedded_ref, out_ref):
    total = total_of((in0, in1, in2, in3))
    embedded = total[:, 0:WIDTH].astype(BF16)
    embedded_ref[...] = embedded
    modded = normed(embedded.astype(F32)) * (1.0 + mod_ref[1]) + mod_ref[0]
    out_ref[:, 0:WIDTH] = modded.astype(BF16)
    out_ref[:, WIDTH:] = total[:, WIDTH:].astype(BF16)


def both_norm_kernel(
    image_ref, embedded_ref, in0, in1, in2, in3, img_mod_ref, txt_mod_ref,
    img_ref, txt_ref, out_ref,
):
    projected = total_of((in0, in1, in2, in3))
    gate, shift, scale = img_mod_ref[2:3, :], img_mod_ref[3:4, :], img_mod_ref[4:5, :]
    mixed = (image_ref[...].astype(F32) + gate * projected[0:32]).astype(BF16)
    img_ref[...] = mixed
    out_ref[0:32, :] = (normed(mixed.astype(F32)) * (1.0 + scale) + shift).astype(BF16)
    mixed = (embedded_ref[...].astype(F32) + txt_mod_ref[2] * projected[32:]).astype(BF16)
    txt_ref[...] = mixed
    hidden = normed(mixed.astype(F32)) * (1.0 + txt_mod_ref[4]) + txt_mod_ref[3]
    out_ref[32 : 32 + POOL, :] = hidden.astype(BF16)


def one_hot(line, count):
    shape = (count, line.shape[1])
    return jnp.where(lax.broadcasted_iota(jnp.int32, shape, 0) == line, 1.0, 0.0)


def with_keep(values, keep):
    first = low_half(values.shape)
    return jnp.where(first, values, keep), jnp.where(first, keep, values)


def project(rows, weight_ref):
    both = jnp.concatenate([weight_ref[0], weight_ref[1]], -1)
    first = jnp.dot(rows, both, preferred_element_type=F32)
    return first, jnp.dot(rows, weight_ref[2], preferred_element_type=F32)


def txt_qkv_kernel(
    places_ref, in0, in1, in2, in3, weight_ref, gain_ref, slot_ref, out_ref, low_ref, held, rows_ref
):
    part = in0.shape[0]
    for place, piece in enumerate((in0, in1, in2, in3)):
        rows_ref[place * part : (place + 1) * part, :] = piece[:, 0:WIDTH]
        wide = piece[:, WIDTH:].astype(F32)
        for near in range(SIDE):
            rows = wide[near * POOL : near * POOL + 16]
            start = pl.multiple_of(places_ref[place * SIDE + near] * 32, 32)
            low_ref[pl.ds(start, 16), :] = rows[:, 0:192]
            low_ref[pl.ds(start + 16, 16), :] = rows[:, 256:448]
    projected, values = project(rows_ref[...], weight_ref)
    held[:, 0:128] = head_norm(projected[:, 0:128], gain_ref[0:1, :]).astype(BF16)
    held[:, 128:256] = head_norm(projected[:, 128:256], gain_ref[1:2, :]).astype(BF16)
    held[:, 256:384] = values.astype(BF16)
    hot = one_hot(slot_ref[...], 512)
    keep = jnp.sum(hot, -1, keepdims=True)
    slots = jnp.dot(hot.astype(BF16), held[...], preferred_element_type=F32)
    val0, val1 = with_keep(slots[:, 256:384], keep)
    out_ref[:, 0:256] = slots[:, 0:256].astype(BF16)
    out_ref[:, 256:384] = val0.astype(BF16)
    out_ref[:, 384:512] = val1.astype(BF16)


def img_project_kernel(
    ids_ref, tp_ref, image_hbm, mod_ref, weight_hbm, down_hbm,
    projected_ref, low_ref, own_ref, own_mod_ref, image, weight, down, wide, modded, sems,
):
    copies = [pltpu.make_async_copy(image_hbm, image, sems.at[0])]
    copies.append(pltpu.make_async_copy(weight_hbm, weight, sems.at[1]))
    for own in range(2):
        copies.append(
            pltpu.make_async_copy(down_hbm.at[ids_ref[own]], down.at[own], sems.at[2 + own])
        )
    for copy in copies:
        copy.start()
    copies[0].wait()
    depth = down.shape[1]
    tp = tp_ref[0]
    own_ref[...] = image[pl.ds(pl.multiple_of(tp * 32, 32), 32), :]
    for place in range(6):
        own_mod_ref[place : place + 1, :] = mod_ref[tp // 8, place, 0:1, :]
    for own in range(2):
        for part in range(2):
            rows = image[own * 256 + part * 128 : own * 256 + (part + 1) * 128, :].astype(F32)
            scaled = normed(rows) * (1.0 + mod_ref[own, 1, 0:1, :]) + mod_ref[own, 0, 0:1, :]
            modded[part * 128 : (part + 1) * 128, :] = scaled.astype(BF16)
        if own == 0:
            copies[1].wait()
        copies[2 + own].wait()
        wide[...] = jnp.zeros_like(wide)
        start = pl.multiple_of(tp * depth, 8)
        wide[pl.ds(start, depth), :] = down[own].astype(F32)
        projected, values = project(modded[...], weight)
        projected_ref[own * 256 : (own + 1) * 256, 0:256] = projected
        projected_ref[own * 256 : (own + 1) * 256, 256:384] = values
        low = jnp.dot(modded[...], wide[...].astype(BF16), preferred_element_type=F32)
        for block in range(8):
            low_ref[own * 8 + block] = low[block * 32 : (block + 1) * 32].astype(BF16)


def img_adapt_kernel(ids_ref, low_ref, projected_ref, up_hbm, gain_ref, out_ref, up, lift, sems):
    copies = []
    for own in range(2):
        copies.append(
            pltpu.make_async_copy(up_hbm.at[ids_ref[own]], up.at[own], sems.at[own])
        )
        copies[own].start()
    for own in range(2):
        copies[own].wait()
        lift[...] = jnp.zeros_like(lift)
        for part in range(3):
            lift[part * 64 : (part + 1) * 64, part * 128 : (part + 1) * 128] = up[own, part]
        rows = slice(own * 256, (own + 1) * 256)
        projected = projected_ref[rows, :] + ADAPTER_SCALE * jnp.dot(
            low_ref[rows, :].astype(BF16), lift[...], preferred_element_type=F32
        )
        out_ref[rows, 0:128] = head_norm(projected[:, 0:128], gain_ref[0:1, :]).astype(BF16)
        out_ref[rows, 128:256] = head_norm(projected[:, 128:256], gain_ref[1:2, :]).astype(BF16)
        val0, val1 = with_keep(projected[:, 256:384], 1.0)
        out_ref[rows, 256:384] = val0.astype(BF16)
        out_ref[rows, 384:512] = val1.astype(BF16)


def attend(queries, tokens):
    scaled = queries.astype(F32) * HEAD_DIM ** (-0.5)
    first = low_half(scaled.shape)
    keys = tokens[:, 128:256]
    results = []
    for head in range(2):
        own = jnp.where(first if head == 0 else ~first, scaled, 0.0).astype(BF16)
        scores = lax.dot_general(
            own, keys, (((1,), (1,)), ((), ())), preferred_element_type=F32
        )
        weights = jnp.exp(scores).astype(BF16)
        summed = jnp.dot(
            weights, tokens[:, 256 + head * 128 : 384 + head * 128], preferred_element_type=F32
        )
        results.append(summed / pltpu.roll(summed, HEAD_DIM, 1))
    return jnp.where(first, results[0], results[1]).astype(BF16)


def img_attend_kernel(
    places_ref, img_ref, slot_ref, weight_ref,
    out0, out1, out2, out3, token_ref, tokens, held, ranked,
):
    for own in range(2):
        tokens[own, 0:256, :] = img_ref[own * 256 : (own + 1) * 256, :]
        for source in range(8):
            start = 256 + source * 32
            tokens[own, start : start + 32, :] = slot_ref[source, own * 32 : (own + 1) * 32, :]
    token_ref[...] = tokens[...]
    for own in range(2):
        held[own * 256 : (own + 1) * 256, :] = attend(tokens[own, 0:256, 0:128], tokens[own])
    for place in range(16):
        start = pl.multiple_of(places_ref[place] * 32, 32)
        ranked[place * 32 : (place + 1) * 32, :] = held[pl.ds(start, 32), :]
    result = jnp.dot(ranked[...], weight_ref[...], preferred_element_type=F32)
    for place, out in enumerate((out0, out1, out2, out3)):
        out[...] = result[place * 128 : (place + 1) * 128].astype(BF16)


def txt_attend_kernel(token_ref, out_ref):
    for own in range(2):
        attended = attend(token_ref[own, 256:512, 0:128], token_ref[own])
        for source in range(8):
            start = source * 32
            out_ref[source, own * 32 : (own + 1) * 32, :] = attended[start : start + 32]


def txt_project_kernel(att_ref, slot_ref, weight_ref, out0, out1, out2, out3):
    hot = one_hot(slot_ref[...], 512).astype(BF16)
    rows = lax.dot_general(
        hot, att_ref[...], (((0,), (0,)), ((), ())), preferred_element_type=F32
    ).astype(BF16)
    part = out0.shape[0]
    result = jnp.dot(rows, weight_ref[...], preferred_element_type=F32)
    for place, out in enumerate((out0, out1, out2, out3)):
        out[...] = result[place * part : (place + 1) * part].astype(BF16)


def feed_kernel(*refs):
    rows_ref = refs[-1]
    count = (len(refs) - 3) // 2
    pieces, outs = refs[0:count], refs[count + 2 : 2 * count + 2]
    win_ref, wout_ref = refs[count], refs[count + 1]
    width = outs[0].shape[1]
    for stream, (start, part) in enumerate(((0, 128), (128, SIDE * POOL))):
        for place, piece in enumerate(pieces):
            rows_ref[place * part : (place + 1) * part, :] = piece[start : start + part, :]
        hidden = lax.dot_general(
            rows_ref[0 : count * part, :],
            win_ref[stream],
            (((1,), (1,)), ((), ())),
            preferred_element_type=F32,
        )
        hidden = jax.nn.gelu(hidden, approximate=True).astype(BF16)
        for columns in (slice(0, 1280), slice(1280, width)):
            result = jnp.dot(hidden, wout_ref[stream, :, columns], preferred_element_type=F32)
            for place, out in enumerate(outs):
                out[start : start + part, columns] = result[
                    place * part : (place + 1) * part
                ].astype(BF16)


def img_final_kernel(mixed_ref, in0, in1, in2, in3, mod_ref, out_ref):
    total = total_of((in0, in1, in2, in3))
    out_ref[...] = (mixed_ref[...].astype(F32) + mod_ref[5:6, :] * total).astype(BF16)


def txt_final_kernel(mixed_ref, in0, in1, in2, in3, mod_ref, slot_ref, placed_ref):
    total = total_of((in0, in1, in2, in3))
    rows = mixed_ref[...].astype(F32) + mod_ref[5] * total
    hot = one_hot(slot_ref[:, 0:POOL], 32).astype(BF16)
    placed = jnp.dot(hot, rows.astype(BF16), preferred_element_type=F32)
    for group in range(8):
        placed_ref[group] = placed[group * 4 : (group + 1) * 4].astype(BF16)


def middle(parts):
    rows, width = parts[0].shape
    return run(
        middle_kernel,
        [like((rows // SIDE, width))] * SIDE,
        parts,
        scratch=[pltpu.VMEM((rows, width), F32)],
    )


def both_middle(img_parts, txt_parts):
    rows, width = txt_parts[0].shape
    return run(
        both_middle_kernel,
        [like((32 + POOL, width))] * SIDE,
        (*img_parts, *txt_parts),
        scratch=[pltpu.VMEM((rows, width), F32)],
    )


def join(kernel, parts):
    width = parts[0].shape[1]
    return run(
        kernel,
        like((SIDE * parts[0].shape[0], width)),
        parts,
        scratch=[pltpu.VMEM((SIDE * POOL, width), F32)],
    )


def feed(parts, weight_in, weight_out, after=()):
    rows, width = parts[0].shape
    return run(
        feed_kernel,
        [like((rows, width))] * len(parts),
        (*parts, weight_in, weight_out),
        scratch=[pltpu.VMEM((len(parts) * 128, width), BF16)],
        flops=rows * len(parts) * width * weight_in.shape[1] * 4,
        limit=14,
        after=after,
    )


def shards(
    image,
    prompt_encoder_rows,
    prompt_row_request,
    request_adapter,
    modulation,
    query_key_gain,
    prompt_embed_weight,
    image_query_key_value,
    prompt_query_key_value,
    image_out_weight,
    prompt_out_weight,
    feed_in_weight,
    feed_out_weight,
    adapter_down,
    adapter_up,
):
    grp = lax.axis_index("grp")
    tp = lax.axis_index("tp")
    chip, core = grp // 2, grp % 2
    z, y = tp // SIDE, tp % SIDE
    width = image.shape[1]

    steps = jnp.arange(16)
    far, near = steps // SIDE, steps % SIDE
    places = jnp.where(
        core == 0,
        ((z + far) % SIDE) * SIDE + (y + near) % SIDE,
        ((z + near) % SIDE) * SIDE + (y + far) % SIDE,
    ).astype(jnp.int32)
    gains = jnp.concatenate([query_key_gain, query_key_gain], -1)

    request = prompt_row_request[:, 0]
    outgoing, slots_own = run(
        pack_kernel,
        [like((16, 32, 256)), like((1, 256), jnp.int32)],
        (prompt_encoder_rows, prompt_row_request.reshape(1, POOL)),
        scratch=[pltpu.VMEM((32, 256), F32), pltpu.VMEM((8, 256), jnp.int32)],
    )
    arrived = lax.all_to_all(outgoing, "tp", 0, 0, tiled=True)
    home = request // 4
    row_index = jnp.where(
        home == chip, 0, jnp.where(home == (chip ^ 1), 1, jnp.where(home == 3 - chip, 2, 3))
    )
    row_index = row_index * 4 + (request // 2 % 2 + core) % 2 * 2 + request % 2

    img_projected, low_part, own_image, own_mod = run(
        img_project_kernel,
        [
            like((512, 384), F32),
            like((16, 32, 192)),
            like((32, width)),
            like((6, width), F32),
        ],
        (
            request_adapter,
            tp.reshape(1).astype(jnp.int32),
            image,
            modulation.transpose(0, 2, 1, 3),
            image_query_key_value.transpose(1, 0, 2),
            adapter_down,
        ),
        smem=2,
        scratch=[
            pltpu.VMEM(image.shape, BF16),
            pltpu.VMEM((3, width, 128), BF16),
            pltpu.VMEM((2, *adapter_down.shape[1:]), BF16),
            pltpu.VMEM((width, 192), F32),
            pltpu.VMEM((256, width), BF16),
            pltpu.SemaphoreType.DMA((4,)),
        ],
        flops=512 * width * 576 * 2,
        limit=56,
        after=(outgoing, row_index),
        hbm=(2, 4, 5),
    )
    prompt_mod = run(
        prompt_mod_kernel, like((2, 8, width), F32), (modulation.transpose(0, 2, 1, 3),),
        after=(outgoing,),
    )
    mod_own = run(
        mod_pair_kernel, like((4, 8, width), F32), (prompt_mod, core_swap(prompt_mod))
    )
    *embed_parts, slots_all = run(
        embed_kernel,
        [like((SIDE * POOL, width + EXTRA))] * SIDE + [like((1, 16 * POOL), jnp.int32)],
        (places, arrived, prompt_embed_weight, low_part),
        smem=1,
        scratch=[pltpu.VMEM((SIDE * POOL, 256), F32), pltpu.VMEM((16, 128), F32)],
        flops=320 * 256 * width * 2,
        after=(mod_own,),
    )
    embed_pieces = exchange(embed_parts, 1)

    embed_sums = exchange(middle(embed_pieces), 0)
    mod_near = run(
        mod_pair_kernel,
        like((8, 8, width), F32),
        (mod_own, chip_swap(mod_own, False)),
        after=(embed_parts[0],),
    )
    row_mod = run(
        row_mod_kernel,
        like((6, POOL, width), F32),
        (row_index, mod_near, chip_swap(mod_near, True)),
        smem=1,
    )
    embedded, txt_mod = run(
        embed_norm_kernel,
        [like((POOL, width)), like((POOL, width + EXTRA))],
        (*embed_sums, row_mod),
    )
    txt_mods = spread(join(join_kernel, spread(txt_mod, 0)), 1)

    slot_parts, low = run(
        txt_qkv_kernel,
        [like((512, 512)), like((512, 192), F32)],
        (places, *txt_mods, prompt_query_key_value.transpose(1, 0, 2), gains[1], slots_all),
        smem=1,
        scratch=[pltpu.VMEM((16 * POOL, 384), BF16), pltpu.VMEM((16 * POOL, width), BF16)],
        flops=320 * width * 384 * 2,
        limit=14,
    )
    img_parts = run(
        img_adapt_kernel,
        like((512, 512)),
        (request_adapter, low, img_projected, adapter_up, gains[0]),
        smem=1,
        scratch=[
            pltpu.VMEM((2, 3, 64, 128), BF16),
            pltpu.VMEM((192, 384), BF16),
            pltpu.SemaphoreType.DMA((2,)),
        ],
        flops=512 * 384 * 192 * 2,
        hbm=(3,),
    )
    slot_parts = lax.all_to_all(slot_parts.reshape(8, 64, 512), "grp", 0, 0, tiled=True)

    *img_terms, tokens = run(
        img_attend_kernel,
        [like((128, width))] * SIDE + [like((2, 512, 512))],
        (places, img_parts, slot_parts, image_out_weight),
        smem=1,
        scratch=[
            pltpu.VMEM((2, 512, 512), BF16),
            pltpu.VMEM((512, 128), BF16),
            pltpu.VMEM((512, 128), BF16),
        ],
        flops=1 << 30,
        limit=16,
    )
    img_sums = exchange(img_terms, 1)
    att_parts = run(txt_attend_kernel, like((8, 64, 128)), (tokens,), flops=1 << 29)
    att_parts = lax.all_to_all(att_parts, "grp", 0, 0, tiled=True).reshape(512, 128)
    txt_terms = run(
        txt_project_kernel,
        [like((SIDE * POOL, width))] * SIDE,
        (att_parts, slots_all, prompt_out_weight),
        flops=320 * 128 * width * 2,
        after=(img_sums[1],),
    )
    txt_sums = exchange(txt_terms, 1)

    sums = exchange(both_middle(img_sums, txt_sums), 0)
    mixed_img, mixed_txt, norm_rows = run(
        both_norm_kernel,
        [like((32, width)), like((POOL, width)), like((32 + POOL, width))],
        (own_image, embedded, *sums, own_mod, row_mod),
    )
    rows = spread(join(both_join_kernel, spread(norm_rows, 0)), 1)
    weight_in = feed_in_weight.transpose(0, 2, 1)
    own_term = feed(rows[:1], weight_in, feed_out_weight)
    terms = feed(rows[1:], weight_in, feed_out_weight, after=(own_term[0],))
    pieces = exchange([*own_term, *terms], 1)
    parts = run(
        part_middle_kernel,
        [like((POOL, width))] * SIDE + [like((32, width))] * SIDE,
        pieces,
        scratch=[pltpu.VMEM((SIDE * POOL, width), F32)],
    )

    placed = run(
        txt_final_kernel,
        like((8, 4, width)),
        (mixed_txt, *exchange(parts[:SIDE], 0), row_mod, slots_own),
    )
    image_out = run(
        img_final_kernel, like((32, width)), (mixed_img, *exchange(parts[SIDE:], 0), own_mod)
    )
    placed = lax.all_to_all(placed, "grp", 0, 0, tiled=True)
    prompt_out = placed.reshape(32, width)

    return (image_out, prompt_out)


def solution(mesh):
    placed = (
        P("grp", None),
        P(("grp", "tp"), None),
        P(("grp", "tp"), None),
        P("grp"),
        P("grp", None, None, None),
        P(),
        P("tp", None),
        P(None, None, "tp"),
        P(None, None, "tp"),
        P("tp", None),
        P("tp", None),
        P(None, None, "tp"),
        P(None, "tp", None),
        P(None, "tp", None),
        P(None, None, None, "tp"),
    )
    return jax.shard_map(
        shards,
        mesh=mesh,
        in_specs=placed,
        out_specs=(P(("grp", "tp"), None), P(("grp", "tp"), None)),
        check_vma=False,
    )
```
